32 devices in a mesh: atoms: 16 (over z, y, x), rep: 2 (over core).
Axes of the slice: x: 2, y: 2, z: 4, core: 2. Of those that a mesh axis runs over, the one named last changes fastest.
Arguments:
- scalars_in: float32 [16384, 128], P(('atoms', 'rep')), may hold values from -6 to 6
- vectors_in: float32 [3, 16384, 128], P(None, ('atoms', 'rep')), may hold values from -6 to 6
- positions: float32 [3, 16384], P(None, ('atoms', 'rep')), may hold values from 0 to 3
- cotan_scalar: float32 [16384, 128], P(('atoms', 'rep')), may hold values from -6 to 6
- cotan_vector: float32 [3, 16384, 128], P(None, ('atoms', 'rep')), may hold values from -6 to 6
- target_energy: float32 [16384], P(('atoms', 'rep'))
- forces: float32 [3, 16384], P(None, ('atoms', 'rep'))
- elements: int32 [16384], P(('atoms', 'rep')), may hold values from 0 to 99
- crystal: int32 [16384], P(('atoms', 'rep')), may hold values from 0 to 511, never falling along the last dimension, each value on 1 to 64 neighbouring positions
- lattice: float32 [512, 9], replicated, may hold values from -0.5 to 4.5, as said below
- edge_src: int32 [262144], P(('atoms', 'rep')), may hold values from 0 to 1023, as said below
- edge_dst: int32 [262144], P(('atoms', 'rep')), may hold values from 0 to 511, as said below
- edge_shift: int32 [3, 262144], P(None, ('atoms', 'rep')), may hold values from -1 to 1
- edge_count: int32 [32], P(('atoms', 'rep')), may hold values from 4096 to 8192, as said below
- send_rows: int32 [32, 8, 64], P(('atoms', 'rep')), may hold values from 0 to 511, as said below
- params: float32 [189440], P(('atoms', 'rep'))
- first_moment: float32 [189440], P(('atoms', 'rep')), may hold values from -40 to 40
- second_moment: float32 [189440], P(('atoms', 'rep')), may hold values from 41.3696 to 165.4784
Outputs:
- scalars_out: float32 [16384, 128], P(('atoms', 'rep'))
- vectors_out: float32 [3, 16384, 128], P(None, ('atoms', 'rep'))
- grad_scalars: float32 [16384, 128], P(('atoms', 'rep'))
- grad_vectors: float32 [3, 16384, 128], P(None, ('atoms', 'rep'))
- grad_positions: float32 [3, 16384], P(None, ('atoms', 'rep'))
- element_mean: float32 [100], replicated
- force_scale: float32 [], replicated
- grad_params: float32 [189440], P(('atoms', 'rep'))
- moment_one: float32 [189440], P(('atoms', 'rep'))
- moment_two: float32 [189440], P(('atoms', 'rep'))
- params_new: float32 [189440], P(('atoms', 'rep'))
- params_low: bfloat16 [189440], P(('atoms', 'rep'))
- weight_norms: float32 [7], replicated
- update_norms: float32 [7], replicated
The draws below stay inside these ranges and needn't reach their ends.
Inputs may be any that keep to these rules, and one draw needn't show every extreme that they name: Rows of one list send_rows[p, j] are distinct. `edge_src`: A value of 512 or more names a received slot whose sending device exists. `edge_dst`: within the slots of one device the values never fall. `edge_count`: some device uses all its 8192 slots. `lattice`: the diagonal lies between 3 and 4.5, the other entries between -0.5 and 0.5.
All inputs are finite; a program needn't handle non-finite values.
Results may differ from the reference program's by a relative error of at most 0.001.
Values sent between devices are 32-bit elements; how exact they have to be, the bound alone decides.
A program may use at most 128 MiB of HBM per device.

```python
import math
import jax
import jax.numpy as jnp
import numpy as np
from jax import lax

F = 128
R = 20
ATOM_DEV = 512
HOPS = 4
ELEMS = 100
STEP = 10
GROUPS = 7
RANKS = 32
ATOMS = 16384
EDGE_DEV = 8192
CAP = 64
CRYSTALS = 512
PARAMS = 189440


def graph_tables(key):
    keys = jax.random.split(key, 10)
    row_keys = jax.random.split(keys[0], RANKS * 2 * HOPS)
    send_table = jax.vmap(lambda one_key: jax.random.permutation(one_key, ATOM_DEV)[:CAP])(row_keys)
    send_table = send_table.reshape(RANKS, 2 * HOPS, CAP).astype(jnp.int32)
    counts = jax.random.randint(keys[1], (RANKS,), EDGE_DEV // 2, EDGE_DEV + 1)
    fullest = jax.random.randint(keys[2], (), 0, RANKS)
    counts = jnp.where(jnp.arange(RANKS) == fullest, EDGE_DEV, counts).astype(jnp.int32)
    raw_dst = jnp.sort(jax.random.randint(keys[3], (RANKS, EDGE_DEV), 0, ATOM_DEV), axis=1)
    stretched = jnp.minimum(raw_dst * EDGE_DEV // counts[:, None], ATOM_DEV - 1)
    slot_ids = jnp.arange(EDGE_DEV)[None, :]
    destination = jnp.where(slot_ids < counts[:, None], stretched, ATOM_DEV - 1).astype(jnp.int32)
    remote_flag = jax.random.randint(keys[4], (RANKS, EDGE_DEV), 0, 2)
    hop_block = jax.random.randint(keys[5], (RANKS, EDGE_DEV), 0, 2 * HOPS)
    slot_place = jax.random.randint(keys[6], (RANKS, EDGE_DEV), 0, CAP)
    local_src = jax.random.randint(keys[7], (RANKS, EDGE_DEV), 0, ATOM_DEV)
    device_ids = jnp.arange(RANKS)[:, None]
    hop_offset = jnp.where(hop_block < HOPS, hop_block + 1, HOPS - 1 - hop_block)
    sender_ids = device_ids - hop_offset
    usable = (remote_flag == 1) & (sender_ids >= 0) & (sender_ids < RANKS)
    source = jnp.where(usable, ATOM_DEV + hop_block * CAP + slot_place, local_src).astype(jnp.int32)
    move_draw = jax.random.randint(keys[8], (3, RANKS * EDGE_DEV), 0, 4)
    step_draw = jax.random.randint(keys[9], (3, RANKS * EDGE_DEV), -1, 2)
    shift_table = jnp.where(move_draw == 0, step_draw, 0).astype(jnp.int32)
    return (send_table, counts, destination.reshape(-1), source.reshape(-1), shift_table)


def draw_send_rows(key, part):
    tables = graph_tables(key)
    return tables[0]


def draw_edge_count(key, part):
    tables = graph_tables(key)
    return tables[1]


def draw_edge_dst(key, part):
    tables = graph_tables(key)
    return tables[2]


def draw_edge_src(key, part):
    tables = graph_tables(key)
    return tables[3]


def draw_edge_shift(key, part):
    tables = graph_tables(key)
    return tables[4]


def draw_lattice(key, part):
    key = jax.random.fold_in(key, 21)
    column = jnp.arange(9)[None, :]
    spread = jax.random.uniform(key, (CRYSTALS, 9), jnp.float32, 0.0, 1.0)
    return jnp.where(column % 4 == 0, 3.0 + 1.5 * spread, spread - 0.5).astype(jnp.float32)


def rising_values(key, rise):
    first, second = jax.random.split(key)
    index = jnp.arange(ATOMS).astype(jnp.float32)
    factor = 1.0 + (rise - 1.0) * index / (ATOMS - 1)
    atom_scale = jnp.exp(jax.random.uniform(first, (ATOMS,), jnp.float32, 0.0, 2.302585))
    return (factor * atom_scale, second)


def draw_target_energy(key, part):
    key = jax.random.fold_in(key, 31)
    scale, other = rising_values(key, 3.0)
    value = jax.random.normal(other, (ATOMS,), jnp.float32)
    return (value * scale).astype(jnp.float32)


def draw_forces(key, part):
    key = jax.random.fold_in(key, 41)
    scale, other = rising_values(key, 3.0)
    value = jax.random.normal(other, (3, ATOMS), jnp.float32)
    return (value * scale[None, :]).astype(jnp.float32)


def draw_params(key, part):
    key = jax.random.fold_in(key, 51)
    index = jnp.arange(PARAMS)
    bounds = [F * F, 4 * F * F, 4 * F * F + 3 * R * F, 6 * F * F + 3 * R * F, 8 * F * F + 3 * R * F, 11 * F * F + 3 * R * F, PARAMS - F]
    scales = [F ** (-0.5), F ** (-0.5), 2.0 * R ** (-0.5), F ** (-0.5), (2 * F) ** (-0.5), F ** (-0.5), 0.3, F ** (-0.5)]
    scale = jnp.full((PARAMS,), scales[0], jnp.float32)
    for bound, level in zip(bounds, scales[1:]):
        scale = jnp.where(index >= bound, level, scale)
    value = jax.random.normal(key, (PARAMS,), jnp.float32)
    return (value * scale).astype(jnp.float32)


def plant(array, own_key, smallest, top_value):
    longest = array.shape.index(max(array.shape))
    spots = []
    for shift in (0, 1):
        where = [jax.random.randint(jax.random.fold_in(own_key, axis), (), 0, length) for axis, length in enumerate(array.shape)]
        where[longest] = (where[longest] + shift) % array.shape[longest]
        spots.append(tuple(where))
    return array.at[spots[0]].set(smallest).at[spots[1]].set(top_value)


def block_levels(stream_key, shape, cuts, smallest, high):
    level = 1.0
    for axis_at, parts in cuts:
        heights = jax.random.uniform(jax.random.fold_in(jax.random.fold_in(stream_key, 6), axis_at), (parts,), jnp.float32, smallest / len(cuts), high / len(cuts))
        level = level * jnp.repeat(jnp.exp(heights), shape[axis_at] // parts).reshape((-1,) + (1,) * (len(shape) - 1 - axis_at))
    return level


def cumulative_ranks(count, slope):
    portions = [(1 << 20) // math.isqrt(standing ** slope) + 1 for standing in range(1, count + 1)]
    scale = 1 + sum(portions) // (1 << 30)
    return np.cumsum(np.array([max(1, weight // scale) for weight in portions]))


def ranked(rng, dims, number_of, lean):
    grid = cumulative_ranks(number_of, lean)
    lot = jax.random.randint(jax.random.fold_in(rng, 1), dims, 0, int(grid[number_of - 1]))
    standing = jnp.searchsorted(jnp.asarray(grid, jnp.int32), lot, side="right")
    return jax.random.permutation(jax.random.fold_in(rng, 2), number_of)[standing].astype(jnp.int32)


def length_profile(count, total, limit, skew):
    weights = [(1 << 20) // math.isqrt(rank ** skew) + 1 for rank in range(2, count + 1)]
    spare, given = total - limit - (count - 1), [1] * (count - 1)
    while spare > 0:
        free = [i for i in range(count - 1) if given[i] < limit]
        mass, budget = sum([weights[i] for i in free]), spare
        for i in free:
            more = min(limit - given[i], max(1, budget * weights[i] // mass), spare)
            given[i] = given[i] + more
            spare = spare - more
    return np.array([limit] + given)


def uneven_parts(own_key, number_of, total, reach, slope):
    if number_of == 2:
        one = jax.random.randint(own_key, (), max(1, total - reach), min(reach, total - 1) + 1)
        return jnp.stack([one, total - one])
    sizes = jnp.asarray(length_profile(number_of, total, reach, slope), jnp.int32)
    pairs = (number_of - 1) // 2
    source_of, taker = sizes[1:1 + 2 * pairs:2], sizes[2:2 + 2 * pairs:2]
    slack = jnp.minimum(source_of - 1, reach - taker)
    moved = jax.random.randint(jax.random.fold_in(own_key, 1), (pairs,), 0, 1 << 20) % (slack + 1)
    sizes = sizes.at[1:1 + 2 * pairs:2].set(source_of - moved).at[2:2 + 2 * pairs:2].set(taker + moved)
    return sizes[jax.random.permutation(jax.random.fold_in(own_key, 2), number_of)]


def normal_values(own_key, dims, deviation, most, shards=(), held_as=jnp.bfloat16):
    values = deviation * jax.random.normal(own_key, dims, jnp.float32)
    if shards:
        values = values * block_levels(own_key, dims, shards, -0.22, 0.18)
    return jnp.clip(values, -most, most).astype(held_as)


def setup_inputs(seed: int = 0) -> dict:
    key_list = jax.random.split(jax.random.key(seed), 19)
    scalars_in = normal_values(key_list[0], (ATOMS, F), 1.0, 6.0, ((0, 32),), jnp.float32)
    vectors_in = normal_values(key_list[1], (3, ATOMS, F), 0.7, 6.0, ((1, 32),), jnp.float32)
    positions = jnp.clip(3.0 * jax.random.uniform(key_list[2], (3, ATOMS), jnp.float32) ** block_levels(key_list[2], (3, ATOMS), ((1, 32),), -0.2, 0.2), 0.0, 3.0)
    cotan_scalar = normal_values(key_list[3], (ATOMS, F), 1.0, 6.0, ((0, 32),), jnp.float32)
    cotan_vector = normal_values(key_list[4], (3, ATOMS, F), 1.0, 6.0, ((1, 32),), jnp.float32)
    target_energy = draw_target_energy(jax.random.fold_in(key_list[18], 71), 0)
    forces = draw_forces(jax.random.fold_in(key_list[18], 71), 0)
    elements = plant(ranked(key_list[7], (ATOMS,), ELEMS, 2), jax.random.fold_in(key_list[7], 3), 0, ELEMS - 1).astype(jnp.int32)
    crystal = jnp.searchsorted(jnp.cumsum(uneven_parts(key_list[8], CRYSTALS, ATOMS, 64, 1)), jnp.arange(ATOMS), side="right").astype(jnp.int32)
    lattice = draw_lattice(jax.random.fold_in(key_list[18], 71), 0)
    edge_src = draw_edge_src(jax.random.fold_in(key_list[18], 71), 0)
    edge_dst = draw_edge_dst(jax.random.fold_in(key_list[18], 71), 0)
    edge_shift = draw_edge_shift(jax.random.fold_in(key_list[18], 71), 0)
    edge_count = draw_edge_count(jax.random.fold_in(key_list[18], 71), 0)
    send_rows = draw_send_rows(jax.random.fold_in(key_list[18], 71), 0)
    params = draw_params(jax.random.fold_in(key_list[18], 71), 0)
    first_moment = normal_values(key_list[16], (PARAMS,), (0.0555 * ATOMS ** 0.5), 40.0, ((0, 32),), jnp.float32)
    second_moment = jnp.clip(jnp.exp(math.log(165.4784) - 1.3862944 * jax.random.uniform(key_list[17], (PARAMS,), jnp.float32) ** block_levels(key_list[17], (PARAMS,), ((0, 32),), -0.2, 0.2)), 41.3696, 165.4784)
    return dict(scalars_in=scalars_in, vectors_in=vectors_in, positions=positions, cotan_scalar=cotan_scalar, cotan_vector=cotan_vector, target_energy=target_energy, forces=forces, elements=elements, crystal=crystal, lattice=lattice, edge_src=edge_src, edge_dst=edge_dst, edge_shift=edge_shift, edge_count=edge_count, send_rows=send_rows, params=params, first_moment=first_moment, second_moment=second_moment)


CUTOFF = 5.0
BETA_ONE = 0.9
BETA_TWO = 0.99
RATE = 0.3
DECAY = 0.01
EPSILON = 1e-06
PRECISION_MAX = lax.Precision.HIGHEST

@jax.custom_vjp
def low(v):
    return lax.optimization_barrier(v.astype(jnp.bfloat16)).astype(jnp.float32)

@jax.custom_vjp
def low_back(v):
    return v

def low_keep(v):
    return (low(v), None)

def low_pass(kept, grad):
    return (grad,)

def back_keep(v):
    return (v, None)

def back_low(kept, grad):
    return (low(grad),)
low.defvjp(low_keep, low_pass)
low_back.defvjp(back_keep, back_low)

def product(left, right):
    return jnp.dot(left, right, precision=PRECISION_MAX, preferred_element_type=jnp.float32)

def layout():
    shapes = [(F, F), (F, 3 * F), (R, 3 * F), (F, 2 * F), (2 * F, F), (F, 3 * F)]
    lengths = [F, 3 * F, 3 * F, F, 3 * F, F]
    return (shapes, lengths)

def unpack(all_params):
    shapes, lengths = layout()
    result = []
    start = 0
    for shape in shapes:
        count = shape[0] * shape[1]
        result.append(all_params[start:start + count].reshape(shape))
        start += count
    for length in lengths:
        result.append(all_params[start:start + length])
        start += length
    return result

def group_ids(index):
    shapes, lengths = layout()
    labels = jnp.zeros(index.shape, jnp.int32)
    start = 0
    for shape in shapes:
        start += shape[0] * shape[1]
        labels = labels + (index >= start).astype(jnp.int32)
    return labels

def features(scalars, w_one, b_one, w_two, b_two):
    return product(jax.nn.silu(product(scalars, w_one) + b_one), w_two) + b_two

def periodic(shifts, cells):
    columns = []
    for comp in range(3):
        columns.append(shifts[..., 0, :] * cells[..., comp] + shifts[..., 1, :] * cells[..., 3 + comp] + shifts[..., 2, :] * cells[..., 6 + comp])
    return jnp.stack(columns, axis=-2)

def messages(x_src, v_src, relative, used, w_filter, b_filter):
    distance = jnp.sqrt(jnp.maximum(lax.optimization_barrier(jnp.sum(relative * relative, axis=0)), 0.25))
    heading = relative / distance[None, :]
    orders = jnp.arange(1, R + 1).astype(jnp.float32)
    radial = jnp.sin(orders[None, :] * (jnp.pi / CUTOFF) * distance[:, None]) / distance[:, None]
    envelope = jnp.where(distance < CUTOFF, 0.5 * (jnp.cos(jnp.pi * distance / CUTOFF) + 1.0), 0.0) * used
    filter_rows = (product(radial, w_filter) + b_filter) * envelope[:, None]
    product_rows = x_src * filter_rows
    scalar = product_rows[:, :F]
    vector = product_rows[:, F:2 * F][None] * heading[:, :, None] + product_rows[:, 2 * F:][None] * v_src
    return (scalar, vector)

def edge_sums(table_x, table_v, table_p, w_filter, b_filter, item, atoms_count):
    src_rows, dst_pos_rows, dst_local, offsets, used = item
    relative = table_p[:, src_rows] + offsets - table_p[:, dst_pos_rows]
    scalar, vector = messages(table_x[src_rows], table_v[:, src_rows], relative, used, w_filter, b_filter)
    sum_scalar = jax.ops.segment_sum(scalar, dst_local, num_segments=atoms_count, indices_are_sorted=True)
    sum_vector = jax.ops.segment_sum(jnp.transpose(vector, (1, 0, 2)), dst_local, num_segments=atoms_count, indices_are_sorted=True)
    return (sum_scalar, jnp.transpose(sum_vector, (1, 0, 2)))

def update(s_one, v_one, w_mixing, u_one, c_one, u_two, c_two):
    atoms_count = s_one.shape[0]
    mixing = product(v_one.reshape(3 * atoms_count, F), w_mixing).reshape(3, atoms_count, 2 * F)
    v_linear = mixing[..., :F]
    w_linear = mixing[..., F:]
    magnitude = jnp.sqrt(lax.optimization_barrier(jnp.sum(v_linear * v_linear, axis=0)) + 1.0)
    hidden = jax.nn.silu(product(jnp.concatenate([s_one, magnitude], axis=1), u_one) + c_one)
    gating = product(hidden, u_two) + c_two
    inner_prod = lax.optimization_barrier(jnp.sum(v_linear * w_linear, axis=0))
    s_two = s_one + gating[:, 2 * F:] + gating[:, F:2 * F] * inner_prod
    v_two = v_one + gating[:, :F][None] * w_linear
    return (s_two, v_two)

def reference(scalars_in, vectors_in, positions, cotan_scalar, cotan_vector, target_energy, forces, elements, crystal, lattice, edge_src, edge_dst, edge_shift, edge_count, send_rows, params, first_moment, second_moment):
    device_ids = jnp.arange(RANKS, dtype=jnp.int32)[:, None]
    local_src = edge_src.reshape(RANKS, EDGE_DEV)
    local_dst = edge_dst.reshape(RANKS, EDGE_DEV)
    slot_index = jnp.maximum(local_src - ATOM_DEV, 0)
    hop_block = slot_index // CAP
    slot_place = slot_index % CAP
    hop_offset = jnp.where(hop_block < HOPS, hop_block + 1, HOPS - 1 - hop_block)
    sender_ids = jnp.clip(device_ids - hop_offset, 0, RANKS - 1)
    remote_src = sender_ids * ATOM_DEV + send_rows[sender_ids, hop_block, slot_place]
    global_src = jnp.where(local_src < ATOM_DEV, device_ids * ATOM_DEV + local_src, remote_src).astype(jnp.int32)
    global_dst = (device_ids * ATOM_DEV + local_dst).astype(jnp.int32)
    valid = (jnp.arange(EDGE_DEV, dtype=jnp.int32)[None, :] < edge_count[:, None]).astype(jnp.float32)
    cells = lattice[crystal[global_dst]]
    shift_rows = jnp.transpose(edge_shift.reshape(3, RANKS, EDGE_DEV), (1, 0, 2)).astype(jnp.float32)
    offsets = periodic(shift_rows, cells)
    onehot = (elements[:, None] == jnp.arange(ELEMS, dtype=jnp.int32)[None, :]).astype(jnp.float32)
    elem_total = product(target_energy[None, :], onehot)[0]
    elem_count = lax.optimization_barrier(jnp.sum(onehot, axis=0))
    element_mean = elem_total / jnp.maximum(elem_count, 1.0)
    force_scale = jnp.sqrt(jnp.mean(forces * forces) + 1e-06)
    goal = (target_energy - element_mean[elements]) / force_scale

    def loss_of(scalars, vectors, places, all_params):
        w_one, w_two, w_filter, w_mixing, u_one, u_two, b_one, b_two, b_filter, c_one, c_two, w_read = unpack(all_params)
        table_x = features(scalars, w_one, b_one, w_two, b_two)

        def per_device(item):
            return edge_sums(table_x, vectors, places, w_filter, b_filter, item, ATOM_DEV)
        delta_s, delta_v = lax.map(jax.checkpoint(per_device), (global_src, global_dst, local_dst, offsets, valid))
        s_one = scalars + delta_s.reshape(ATOMS, F)
        v_one = vectors + jnp.transpose(delta_v, (1, 0, 2, 3)).reshape(3, ATOMS, F)
        s_two, v_two = update(s_one, v_one, w_mixing, u_one, c_one, u_two, c_two)
        energy = product(s_two, w_read[:, None])[:, 0]
        objective = jnp.sum(cotan_scalar * s_two) + jnp.sum(cotan_vector * v_two) + 0.5 * jnp.sum((energy - goal) ** 2)
        return (objective, (s_two, v_two))
    objective, pull, outputs = jax.vjp(loss_of, scalars_in, vectors_in, positions, params, has_aux=True)
    grad_scalars, grad_vectors, grad_positions, grad_params = pull(jnp.ones((), jnp.float32))
    moment_one = BETA_ONE * first_moment + (1.0 - BETA_ONE) * grad_params
    moment_two = BETA_TWO * second_moment + (1.0 - BETA_TWO) * grad_params * grad_params
    direction = moment_one / (1.0 - BETA_ONE ** STEP) / (jnp.sqrt(moment_two / (1.0 - BETA_TWO ** STEP)) + EPSILON) + DECAY * params
    labels = group_ids(jnp.arange(PARAMS, dtype=jnp.int32))
    weight_norms = jnp.sqrt(jax.ops.segment_sum(params * params, labels, num_segments=GROUPS))
    update_norms = jnp.sqrt(jax.ops.segment_sum(direction * direction, labels, num_segments=GROUPS))
    trust_ratio = weight_norms / update_norms
    params_new = params - RATE * trust_ratio[labels] * direction
    return (outputs[0], outputs[1], grad_scalars, grad_vectors, grad_positions, element_mean, force_scale, grad_params, moment_one, moment_two, params_new, params_new.astype(jnp.bfloat16), weight_norms, update_norms)
```

```python
import functools

import jax
import jax.numpy as jnp
from jax import lax
from jax.experimental import pallas as pl
from jax.experimental.pallas import tpu as pltpu
from jax.sharding import PartitionSpec as P

F = 128
R = 20
HOPS = 4
ELEMS = 100
STEP = 10
GROUPS = 7

CUTOFF = 5.0
BETA_ONE = 0.9
BETA_TWO = 0.99
RATE = 0.3
DECAY = 0.01
EPSILON = 1e-06
PRECISION_MAX = lax.Precision.HIGHEST

BLOCK = 256
WINDOW = 128
SUB = 32
ROWS = 256
F32 = jnp.float32
BF16 = jnp.bfloat16

AT_W1, AT_W2, AT_WF, AT_WM, AT_U1, AT_U2 = 0, 128, 512, 572, 828, 1084
AT_B1, AT_B2, AT_BF, AT_C1, AT_C2, AT_READ, PARAM_ROWS = 1468, 1469, 1472, 1475, 1476, 1479, 1480


def product(left, right):
    return jnp.dot(left, right, precision=PRECISION_MAX, preferred_element_type=F32)


def mm(left, right, contract=(1, 0)):
    return lax.dot_general(
        left, right, (((contract[0],), (contract[1],)), ((), ())), preferred_element_type=F32
    )


def split(value):
    high = value.astype(BF16)
    return high, (value - high.astype(F32)).astype(BF16)


def dot3(left, right, contract=(1, 0)):
    return (
        mm(left[0], right[0], contract)
        + mm(left[1], right[0], contract)
        + mm(left[0], right[1], contract)
    )


def sigmoid(value):
    return 1.0 / (1.0 + jnp.exp(-value))


def column(ref, start, parts, j, count=F):
    if parts == 1:
        return ref[start : start + count, :]
    return ref[pl.ds(start + j, count, stride=parts), :]


def add_column(ref, start, parts, j, value, count=F):
    if parts == 1:
        ref[start : start + count, :] += value
    else:
        ref[pl.ds(start + j, count, stride=parts), :] += value


def rows_of(start, count, unit):
    return pl.ds(pl.multiple_of(start, unit), count)


def layer_kernel(
    src_s,
    dst_s,
    count_s,
    crystal_s,
    dst_v,
    shift_v,
    lat,
    par,
    s_own,
    v_own,
    p_own,
    s_halo,
    v_halo,
    p_halo,
    cot_s,
    cot_v,
    goal,
    s_two,
    v_two,
    gs_own,
    gv_own,
    gs_halo,
    gv_halo,
    gp,
    gpar,
    tab,
    rows,
    acc,
    cells,
    dtab,
    lrow,
    drow,
    misc,
    sums,
    gd,
    gbuf,
    fbuf,
    mbuf,
    ltbuf,
    tbuf,
    wcat,
    wq,
    gwf,
    gpd,
):
    atoms = s_own.shape[0]
    halo = s_halo.shape[0]
    edges = shift_v.shape[1]
    blocks = edges // BLOCK

    wcat[...] = jnp.zeros_like(wcat)
    wq[...] = jnp.zeros_like(wq)
    gwf[...] = jnp.zeros_like(gwf)
    gpd[...] = jnp.zeros_like(gpd)
    gpar[...] = jnp.zeros_like(gpar)
    sums[...] = jnp.zeros_like(sums)
    for j in range(3):
        wide = jnp.concatenate(
            [
                column(par, AT_WF, 3, j, R),
                par[AT_BF + j : AT_BF + j + 1, :],
                jnp.zeros((3, F), F32),
            ],
            axis=0,
        )
        high = wide.astype(BF16).astype(F32)
        low = wide - high
        pieces = jnp.concatenate([high, high, low, jnp.zeros((56, F), F32)], axis=0)
        wcat[:, j * F : (j + 1) * F] = pieces.astype(BF16)
        pieces = jnp.concatenate([high, low, jnp.zeros((80, F), F32)], axis=0)
        wq[j * F : (j + 1) * F, :] = jnp.transpose(pieces).astype(BF16)

    @pl.loop(0, atoms // 8)
    def _(step):
        for j in range(8):
            a = step * 8 + j
            cells[pl.ds(a, 1), 0:9] = lat[pl.ds(crystal_s[a], 1), :]

    across = jnp.transpose(cells[...])
    blank = jnp.zeros((5, atoms), F32)
    part = jnp.concatenate(
        [p_own[...], blank, across[0:3], blank, across[3:6], blank, across[6:9], blank], axis=0
    )
    high = part.astype(BF16).astype(F32)
    middle = (part - high).astype(BF16).astype(F32)
    low = part - high - middle
    dtab[...] = jnp.concatenate([high, middle, low], axis=0).astype(BF16)

    for s_ref, v_ref, p_ref, base, count in (
        (s_own, v_own, p_own, 0, atoms),
        (s_halo, v_halo, p_halo, atoms, halo),
    ):
        place = jnp.concatenate([p_ref[...], jnp.zeros((F - 3, count), F32)], axis=0)
        tab[pl.ds(base * 8 + 6, count, stride=8), :] = jnp.transpose(place)
        tab[pl.ds(base * 8 + 7, count, stride=8), :] = jnp.zeros((count, F), F32)
        for c in range(3):
            tab[pl.ds(base * 8 + 3 + c, count, stride=8), :] = v_ref[c]

        @pl.loop(0, count // ROWS)
        def _(step):
            first = step * ROWS
            s_pair = split(s_ref[rows_of(first, ROWS, ROWS), :])
            act = dot3(s_pair, split(column(par, AT_W1, 1, 0))) + par[AT_B1 : AT_B1 + 1, :]
            hidden = split(act * sigmoid(act))
            for j in range(3):
                x = dot3(hidden, split(column(par, AT_W2, 3, j))) + par[AT_B2 + j : AT_B2 + j + 1, :]
                tab[pl.ds((base + first) * 8 + j, ROWS, stride=8), :] = x

    @pl.loop(0, edges // 32)
    def _(step):
        for j in range(32):
            e = step * 32 + j
            rows[rows_of(e * 8, 8, 8), :] = tab[rows_of(src_s[e] * 8, 8, 8), :]

    lanes = lax.broadcasted_iota(jnp.int32, (1, BLOCK), 1)
    slots = lax.broadcasted_iota(jnp.int32, (WINDOW, BLOCK), 0)
    eight = lax.broadcasted_iota(jnp.int32, (8, 1), 0)
    order = lax.broadcasted_iota(jnp.int32, (24, 1), 0)
    wide_lane = lax.broadcasted_iota(jnp.int32, (1, F), 1)

    def destinations(i):
        return jnp.concatenate(
            [dst_v[pl.ds(i * (BLOCK // F) + k, 1), :] for k in range(BLOCK // F)], axis=1
        )

    def window_range(i):
        return dst_s[i * BLOCK] // WINDOW, dst_s[i * BLOCK + BLOCK - 1] // WINDOW

    def hot(dst, w):
        return jnp.where(dst - w * WINDOW == slots, 1.0, 0.0).astype(BF16)

    def over_windows(first, last, body, start):
        return lax.fori_loop(first + 1, last + 1, body, body(first, start))

    def lane_pieces(pieces, extra):
        full = jnp.concatenate(
            [pieces, pieces[0:24], extra, jnp.zeros((F - 80, BLOCK), F32)], axis=0
        )
        return jnp.transpose(full)

    def comp(i, k, sub):
        return pl.ds(i * (BLOCK * 8) + sub * (SUB * 8) + k, SUB, stride=8)

    @pl.loop(0, blocks)
    def _(i):
        here = rows_of(i * BLOCK, BLOCK, BLOCK)
        first, last = window_range(i)
        dst = destinations(i)
        place = jnp.transpose(rows[pl.ds(i * (BLOCK * 8) + 6, BLOCK, stride=8), :])[0:8]
        ends = over_windows(
            first,
            last,
            lambda w, got: got + mm(dtab[:, rows_of(w * WINDOW, WINDOW, WINDOW)], hot(dst, w)),
            jnp.zeros((96, BLOCK), F32),
        )
        ends = ends[0:32] + ends[32:64] + ends[64:96]
        shift = shift_v[:, here].astype(F32)
        rel = (
            place
            + (shift[0:1] * ends[8:16] + shift[1:2] * ends[16:24] + shift[2:3] * ends[24:32])
            - ends[0:8]
        )
        square = jnp.sum(rel * rel, axis=0, keepdims=True)
        dist = jnp.sqrt(jnp.maximum(square, 0.25))
        inv = 1.0 / dist
        unit = rel * inv
        free = jnp.where(square > 0.25, 1.0, 0.0)
        angle = dist * (jnp.pi / CUTOFF)
        phase = (eight + 1).astype(F32) * angle
        sin_a, cos_a = jnp.sin(phase), jnp.cos(phase)
        sin_8, cos_8 = sin_a[7:8], cos_a[7:8]
        sin_b = sin_a * cos_8 + cos_a * sin_8
        cos_b = cos_a * cos_8 - sin_a * sin_8
        sin_c = sin_b * cos_8 + cos_b * sin_8
        cos_c = cos_b * cos_8 - sin_b * sin_8
        sines = jnp.concatenate([sin_a, sin_b, sin_c], axis=0)
        cosines = jnp.concatenate([cos_a, cos_b, cos_c], axis=0)
        radial = sines * inv
        slope = ((order + 1).astype(F32) * (jnp.pi / CUTOFF) * cosines - radial) * inv
        radial = jnp.where(order < R, radial, jnp.where(order == R, 1.0, 0.0))
        slope = jnp.where(order < R, slope, 0.0)
        inside = (dist < CUTOFF) & (i * BLOCK + lanes < count_s[0])
        envelope = jnp.where(inside, 0.5 * (cos_a[0:1] + 1.0), 0.0)
        fall = jnp.where(inside, (-0.5 * jnp.pi / CUTOFF) * sin_a[0:1], 0.0)
        scaled = envelope * radial
        high = scaled.astype(BF16).astype(F32)
        pieces = jnp.concatenate([high, scaled - high], axis=0)
        extra = jnp.where(
            eight < 3,
            unit,
            jnp.where(
                eight == 3,
                dst.astype(F32),
                jnp.where(eight == 4, inv, jnp.where(eight == 5, free, 0.0)),
            ),
        )
        lrow[:, here] = pieces.astype(BF16)
        drow[:, here] = fall * radial + envelope * slope
        misc[:, here] = extra
        ltbuf[...] = lane_pieces(pieces, extra)
        fbuf[...] = mm(ltbuf[...].astype(BF16), wcat[...])
        for sub in range(BLOCK // SUB):
            at = slice(sub * SUB, (sub + 1) * SUB)
            m1, m2, m3 = [
                rows[comp(i, j, sub), :] * fbuf[at, j * F : (j + 1) * F] for j in range(3)
            ]
            out = [m1]
            for c in range(3):
                out.append(m2 * ltbuf[at, 72 + c : 73 + c] + m3 * rows[comp(i, 3 + c, sub), :])
            for k in range(4):
                high, low = split(out[k])
                mbuf[at, k * F : (k + 1) * F] = high
                mbuf[at, (4 + k) * F : (5 + k) * F] = low

        def collect(w, ignored):
            pick = hot(dst, w)
            sums[rows_of(w * WINDOW, WINDOW, WINDOW), :] += mm(pick, mbuf[:, : 4 * F]) + mm(
                pick, mbuf[:, 4 * F :]
            )
            return ignored

        over_windows(first, last, collect, 0)

    @pl.loop(0, atoms // ROWS)
    def _(step):
        at = rows_of(step * ROWS, ROWS, ROWS)
        s_one = s_own[at, :] + sums[at, 0:F]
        v_one = [v_own[c, at, :] + sums[at, (c + 1) * F : (c + 2) * F] for c in range(3)]
        wm = [split(column(par, AT_WM, 2, j)) for j in range(2)]
        u1 = [split(par[AT_U1 + j * F : AT_U1 + (j + 1) * F, :]) for j in range(2)]
        u2 = [split(column(par, AT_U2, 3, j)) for j in range(3)]
        v_pair = [split(v) for v in v_one]
        v_lin = [dot3(v, wm[0]) for v in v_pair]
        w_lin = [dot3(v, wm[1]) for v in v_pair]
        size = jnp.sqrt(v_lin[0] * v_lin[0] + v_lin[1] * v_lin[1] + v_lin[2] * v_lin[2] + 1.0)
        s_pair, size_pair = split(s_one), split(size)
        act = dot3(s_pair, u1[0]) + dot3(size_pair, u1[1]) + par[AT_C1 : AT_C1 + 1, :]
        gate = sigmoid(act)
        hidden = split(act * gate)
        a1, a2, a3 = [dot3(hidden, u2[j]) + par[AT_C2 + j : AT_C2 + j + 1, :] for j in range(3)]
        inner = v_lin[0] * w_lin[0] + v_lin[1] * w_lin[1] + v_lin[2] * w_lin[2]
        s_out = s_one + a3 + a2 * inner
        s_two[at, :] = s_out
        read = par[AT_READ : AT_READ + 1, :]
        out_pair = split(s_out)
        energy = dot3(split(jnp.broadcast_to(read, (8, F))), out_pair, (1, 1))
        error = energy - goal[:, at]
        error_col = jnp.transpose(error)[:, 0:1]
        gpar[AT_READ : AT_READ + 1, :] += dot3(split(error), out_pair)[0:1]
        gs = cot_s[at, :] + error_col * read
        gv = []
        for c in range(3):
            v_two[c, at, :] = v_one[c] + a1 * w_lin[c]
            gv.append(cot_v[c, at, :])
        ga = [gv[0] * w_lin[0] + gv[1] * w_lin[1] + gv[2] * w_lin[2], gs * inner, gs]
        g_inner = gs * a2
        ga_pair = [split(g) for g in ga]
        for j in range(3):
            add_column(gpar, AT_U2, 3, j, dot3(hidden, ga_pair[j], (0, 0)))
            gpar[AT_C2 + j : AT_C2 + j + 1, :] += jnp.sum(ga[j], axis=0, keepdims=True)
        g_hidden = (
            dot3(ga_pair[0], u2[0], (1, 1))
            + dot3(ga_pair[1], u2[1], (1, 1))
            + dot3(ga_pair[2], u2[2], (1, 1))
        )
        g_act = g_hidden * (gate * (1.0 + act * (1.0 - gate)))
        g_act_pair = split(g_act)
        add_column(gpar, AT_U1, 1, 0, dot3(s_pair, g_act_pair, (0, 0)))
        add_column(gpar, AT_U1 + F, 1, 0, dot3(size_pair, g_act_pair, (0, 0)))
        gpar[AT_C1 : AT_C1 + 1, :] += jnp.sum(g_act, axis=0, keepdims=True)
        g_s_one = gs + dot3(g_act_pair, u1[0], (1, 1))
        g_size = dot3(g_act_pair, u1[1], (1, 1)) / size
        gs_own[at, :] = g_s_one
        down = [g_s_one]
        for c in range(3):
            g_w = split(a1 * gv[c] + g_inner * v_lin[c])
            g_v = split(g_inner * w_lin[c] + g_size * v_lin[c])
            add_column(gpar, AT_WM, 2, 0, dot3(v_pair[c], g_v, (0, 0)))
            add_column(gpar, AT_WM, 2, 1, dot3(v_pair[c], g_w, (0, 0)))
            g_v_one = gv[c] + dot3(g_v, wm[0], (1, 1)) + dot3(g_w, wm[1], (1, 1))
            gv_own[c, at, :] = g_v_one
            down.append(g_v_one)
        for k in range(4):
            high, low = split(down[k])
            for part in range(ROWS // WINDOW):
                to = (step * (ROWS // WINDOW) + part) * (2 * WINDOW)
                of = slice(part * WINDOW, (part + 1) * WINDOW)
                gd[rows_of(to, WINDOW, WINDOW), k * F : (k + 1) * F] = high[of]
                gd[rows_of(to + WINDOW, WINDOW, WINDOW), k * F : (k + 1) * F] = low[of]

    twice = (lax.broadcasted_iota(jnp.int32, (1, 2 * WINDOW), 1) % WINDOW).astype(F32)

    @pl.loop(0, blocks)
    def _(i):
        here = rows_of(i * BLOCK, BLOCK, BLOCK)
        first, last = window_range(i)
        dst = destinations(i)
        extra = misc[:, here]
        ltbuf[...] = lane_pieces(lrow[:, here].astype(F32), extra)
        fbuf[...] = mm(ltbuf[...].astype(BF16), wcat[...])
        dst_col = ltbuf[:, 75:76]

        def fetch(w):
            near = dst_col - (w * WINDOW).astype(F32)
            return mm(
                jnp.where(near == twice, 1.0, 0.0).astype(BF16),
                gd[rows_of(w * 2 * WINDOW, 2 * WINDOW, 2 * WINDOW), :],
            )

        gbuf[...] = fetch(first)

        @pl.loop(first + 1, last + 1)
        def _(w):
            gbuf[...] += fetch(w)

        for sub in range(BLOCK // SUB):
            at = slice(sub * SUB, (sub + 1) * SUB)
            g_s = gbuf[at, 0:F]
            g_v = [gbuf[at, (c + 1) * F : (c + 2) * F] for c in range(3)]
            x = [rows[comp(i, j, sub), :] for j in range(3)]
            v = [rows[comp(i, 3 + c, sub), :] for c in range(3)]
            f = [fbuf[at, j * F : (j + 1) * F] for j in range(3)]
            u = [ltbuf[at, 72 + c : 73 + c] for c in range(3)]
            g_m = [
                g_s,
                g_v[0] * u[0] + g_v[1] * u[1] + g_v[2] * u[2],
                g_v[0] * v[0] + g_v[1] * v[1] + g_v[2] * v[2],
            ]
            m2 = x[1] * f[1]
            m3 = x[2] * f[2]
            turn = jnp.zeros((SUB, F), F32)
            for c in range(3):
                total = jnp.sum(g_v[c] * m2, axis=1, keepdims=True)
                turn = jnp.where(wide_lane == 48 + c, total, turn)
                rows[comp(i, 3 + c, sub), :] = g_v[c] * m3
            tbuf[at, :] = turn
            for j in range(3):
                high, low = split(g_m[j] * x[j])
                mbuf[at, j * F : (j + 1) * F] = high
                mbuf[at, (3 + j) * F : (4 + j) * F] = low
                rows[comp(i, j, sub), :] = g_m[j] * f[j]
        h_high, h_low = mbuf[:, : 3 * F], mbuf[:, 3 * F : 6 * F]
        back = jnp.transpose(mm(h_high, wq[...]) + mm(h_low, wq[...]) + tbuf[...])
        pieces = lrow[:, here]
        gwf[...] += mm(pieces, h_high) + mm(pieces, h_low)
        g_row = back[0:24] + back[24:48]
        g_unit = back[48:56]
        unit = jnp.where(eight < 3, extra, 0.0)
        inv, free = extra[4:5], extra[5:6]
        g_dist = jnp.sum(g_row * drow[:, here], axis=0, keepdims=True)
        along = jnp.sum(g_unit * unit, axis=0, keepdims=True)
        g_rel = g_unit * inv + (g_dist - along * inv) * free * unit
        rows[pl.ds(i * (BLOCK * 8) + 6, BLOCK, stride=8), :] = jnp.transpose(
            jnp.concatenate([g_rel, jnp.zeros((F - 8, BLOCK), F32)], axis=0)
        )
        high = g_rel.astype(BF16).astype(F32)
        middle = (g_rel - high).astype(BF16).astype(F32)
        g_pieces = jnp.concatenate([high, middle, g_rel - high - middle, jnp.zeros_like(g_rel)], axis=0)
        g_pieces = g_pieces.astype(BF16)

        def collect(w, ignored):
            got = mm(g_pieces, hot(dst, w), (1, 1))
            gpd[:, rows_of(w * WINDOW, WINDOW, WINDOW)] += got[0:8] + got[8:16] + got[16:24]
            return ignored

        over_windows(first, last, collect, 0)

    for j in range(3):
        total = gwf[0:24, j * F : (j + 1) * F] + gwf[24:48, j * F : (j + 1) * F]
        add_column(gpar, AT_WF, 3, j, total[0:R], R)
        gpar[AT_BF + j : AT_BF + j + 1, :] = total[R : R + 1]

    tab[...] = jnp.zeros_like(tab)
    acc[...] = jnp.zeros_like(acc)
    half = edges // 2

    @pl.loop(0, half // 8)
    def _(step):
        for j in range(8):
            for start, total in ((0, tab), (half, acc)):
                e = start + step * 8 + j
                to = rows_of(src_s[e] * 8, 8, 8)
                total[to, :] += rows[rows_of(e * 8, 8, 8), :]

    for s_ref, gs_ref, gv_ref, base, count in (
        (s_own, gs_own, gv_own, 0, atoms),
        (s_halo, gs_halo, gv_halo, atoms, halo),
    ):
        own = base == 0
        for k in range(0, count, ROWS):
            at = pl.ds((base + k) * 8 + 6, ROWS, stride=8)
            place = jnp.transpose(tab[at, :] + acc[at, :])[0:8]
            if own:
                place = place - gpd[:, k : k + ROWS]
            gp[:, base + k : base + k + ROWS] = place

        @pl.loop(0, count // ROWS)
        def _(step):
            first = step * ROWS
            to = rows_of(first, ROWS, ROWS)

            def gathered(k):
                at = pl.ds((base + first) * 8 + k, ROWS, stride=8)
                return tab[at, :] + acc[at, :]

            for c in range(3):
                if own:
                    gv_ref[c, to, :] += gathered(3 + c)
                else:
                    gv_ref[c, to, :] = gathered(3 + c)
            w1 = split(column(par, AT_W1, 1, 0))
            s_pair = split(s_ref[to, :])
            act = dot3(s_pair, w1) + par[AT_B1 : AT_B1 + 1, :]
            gate = sigmoid(act)
            hidden = split(act * gate)
            g_hidden = jnp.zeros((ROWS, F), F32)
            for j in range(3):
                g_x = gathered(j)
                g_pair = split(g_x)
                add_column(gpar, AT_W2, 3, j, dot3(hidden, g_pair, (0, 0)))
                gpar[AT_B2 + j : AT_B2 + j + 1, :] += jnp.sum(g_x, axis=0, keepdims=True)
                g_hidden = g_hidden + dot3(g_pair, split(column(par, AT_W2, 3, j)), (1, 1))
            g_act = g_hidden * (gate * (1.0 + act * (1.0 - gate)))
            g_act_pair = split(g_act)
            add_column(gpar, AT_W1, 1, 0, dot3(s_pair, g_act_pair, (0, 0)))
            gpar[AT_B1 : AT_B1 + 1, :] += jnp.sum(g_act, axis=0, keepdims=True)
            g_s = dot3(g_act_pair, w1, (1, 1))
            if own:
                gs_ref[to, :] += g_s
            else:
                gs_ref[to, :] = g_s


def layer(atoms, halo, edges, smem, vmem):
    shape = jax.ShapeDtypeStruct
    total = atoms + halo
    in_vmem = pl.BlockSpec(memory_space=pltpu.VMEM)
    in_smem = pl.BlockSpec(memory_space=pltpu.SMEM)
    outs = (
        shape((atoms, F), F32),
        shape((3, atoms, F), F32),
        shape((atoms, F), F32),
        shape((3, atoms, F), F32),
        shape((halo, F), F32),
        shape((3, halo, F), F32),
        shape((8, total), F32),
        shape((PARAM_ROWS, F), F32),
    )
    scratch = [
        pltpu.VMEM((total * 8, F), F32),
        pltpu.VMEM((edges * 8, F), F32),
        pltpu.VMEM((total * 8, F), F32),
        pltpu.VMEM((atoms, F), F32),
        pltpu.VMEM((96, atoms), BF16),
        pltpu.VMEM((48, edges), BF16),
        pltpu.VMEM((24, edges), F32),
        pltpu.VMEM((8, edges), F32),
        pltpu.VMEM((atoms, 4 * F), F32),
        pltpu.VMEM((2 * atoms, 4 * F), BF16),
        pltpu.VMEM((BLOCK, 4 * F), F32),
        pltpu.VMEM((BLOCK, 3 * F), F32),
        pltpu.VMEM((BLOCK, 8 * F), BF16),
        pltpu.VMEM((BLOCK, F), F32),
        pltpu.VMEM((BLOCK, F), F32),
        pltpu.VMEM((F, 3 * F), BF16),
        pltpu.VMEM((3 * F, F), BF16),
        pltpu.VMEM((48, 3 * F), F32),
        pltpu.VMEM((8, atoms), F32),
    ]
    return pl.pallas_call(
        layer_kernel,
        out_shape=outs,
        in_specs=[in_smem] * smem + [in_vmem] * vmem,
        out_specs=(in_vmem,) * len(outs),
        scratch_shapes=scratch,
        compiler_params=pltpu.CompilerParams(vmem_limit_bytes=62 * 1024 * 1024),
        name="layer",
    )


def layout():
    shapes = [(F, F), (F, 3 * F), (R, 3 * F), (F, 2 * F), (2 * F, F), (F, 3 * F)]
    lengths = [F, 3 * F, 3 * F, F, 3 * F, F]
    return (shapes, lengths)


def group_ids(index):
    shapes, lengths = layout()
    labels = jnp.zeros(index.shape, jnp.int32)
    start = 0
    for shape in shapes:
        start += shape[0] * shape[1]
        labels = labels + (index >= start).astype(jnp.int32)
    return labels


def passed_along(shard, axis, by):
    devices = lax.axis_size(axis)
    pairs = [(i, i + by) for i in range(devices) if 0 <= i + by < devices]
    return lax.ppermute(shard, axis, pairs)


def body(
    scalars_in,
    vectors_in,
    positions,
    cotan_scalar,
    cotan_vector,
    target_energy,
    forces,
    elements,
    crystal,
    lattice,
    edge_src,
    edge_dst,
    edge_shift,
    edge_count,
    send_rows,
    params,
    first_moment,
    second_moment,
):
    both = ("atoms", "rep")
    atoms_dev = scalars_in.shape[0]
    edges_dev = edge_src.shape[0]
    capacity = send_rows.shape[2]
    hop_offsets = [k + 1 for k in range(HOPS)] + [-(k + 1) for k in range(HOPS)]
    all_params = lax.all_gather(params, both, axis=0, tiled=True)
    onehot = (elements[:, None] == jnp.arange(ELEMS, dtype=jnp.int32)[None, :]).astype(F32)
    elem_total = product(target_energy[None, :], onehot)[0]
    elem_count = jnp.sum(onehot, axis=0)
    force_square = jnp.sum(forces * forces)
    elem_total, elem_count, force_square = lax.psum((elem_total, elem_count, force_square), both)
    element_mean = elem_total / jnp.maximum(elem_count, 1.0)
    total_atoms = atoms_dev * lax.axis_size(both)
    force_scale = jnp.sqrt(force_square / (3.0 * total_atoms) + 1e-06)
    goal = (target_energy - product(onehot, element_mean[:, None])[:, 0]) / force_scale

    picker = (
        send_rows[0].reshape(-1)[:, None] == jnp.arange(atoms_dev, dtype=jnp.int32)[None, :]
    ).astype(F32)
    joined = jnp.concatenate(
        [scalars_in, vectors_in[0], vectors_in[1], vectors_in[2], jnp.transpose(positions)], axis=1
    )
    picked = product(picker, joined).reshape(2 * HOPS, capacity, 4 * F + 3)
    received = jnp.concatenate(
        [passed_along(picked[k], both, hop_offsets[k]) for k in range(2 * HOPS)], axis=0
    )
    halo_rows = 2 * HOPS * capacity
    s_halo = received[:, :F]
    v_halo = jnp.stack([received[:, (c + 1) * F : (c + 2) * F] for c in range(3)])
    p_halo = jnp.transpose(received[:, 4 * F :])

    run = layer(atoms_dev, halo_rows, edges_dev, 4, 13)
    s_two, v_two, gs_own, gv_own, gs_halo, gv_halo, gp, gpar = run(
        edge_src,
        edge_dst,
        edge_count,
        crystal,
        edge_dst.reshape(-1, F),
        edge_shift,
        lattice,
        all_params.reshape(PARAM_ROWS, F),
        scalars_in,
        vectors_in,
        positions,
        s_halo,
        v_halo,
        p_halo,
        cotan_scalar,
        cotan_vector,
        goal[None, :],
    )
    back = jnp.concatenate(
        [gs_halo, gv_halo[0], gv_halo[1], gv_halo[2], jnp.transpose(gp[:3, atoms_dev:])], axis=1
    ).reshape(2 * HOPS, capacity, 4 * F + 3)
    returned = jnp.concatenate(
        [passed_along(back[k], both, -hop_offsets[k]) for k in range(2 * HOPS)], axis=0
    )
    added = product(jnp.transpose(picker), returned)
    grad_scalars = gs_own + added[:, :F]
    grad_vectors = gv_own + jnp.stack([added[:, (c + 1) * F : (c + 2) * F] for c in range(3)])
    grad_positions = gp[:3, :atoms_dev] + jnp.transpose(added[:, 4 * F :])

    grad_shard = lax.psum_scatter(gpar.reshape(-1), both, scatter_dimension=0, tiled=True)
    shard_len = params.shape[0]
    moment_one = BETA_ONE * first_moment + (1.0 - BETA_ONE) * grad_shard
    moment_two = BETA_TWO * second_moment + (1.0 - BETA_TWO) * grad_shard * grad_shard
    direction = (
        moment_one
        / (1.0 - BETA_ONE**STEP)
        / (jnp.sqrt(moment_two / (1.0 - BETA_TWO**STEP)) + EPSILON)
        + DECAY * params
    )
    first_index = lax.axis_index(both) * shard_len
    labels = group_ids(first_index + jnp.arange(shard_len, dtype=jnp.int32))
    member = (labels[None, :] == jnp.arange(GROUPS, dtype=jnp.int32)[:, None]).astype(F32)
    weight_square = product(member, (params * params)[:, None])[:, 0]
    update_square = product(member, (direction * direction)[:, None])[:, 0]
    weight_square, update_square = lax.psum((weight_square, update_square), both)
    weight_norms = jnp.sqrt(weight_square)
    update_norms = jnp.sqrt(update_square)
    trust_ratio = weight_norms / update_norms
    params_new = params - RATE * product(trust_ratio[None, :], member)[0] * direction
    return (
        s_two,
        v_two,
        grad_scalars,
        grad_vectors,
        grad_positions,
        element_mean,
        force_scale,
        grad_shard,
        moment_one,
        moment_two,
        params_new,
        params_new.astype(BF16),
        weight_norms,
        update_norms,
    )


def solution(mesh):
    joint = ("atoms", "rep")
    in_specs = (
        P(joint, None),
        P(None, joint, None),
        P(None, joint),
        P(joint, None),
        P(None, joint, None),
        P(joint),
        P(None, joint),
        P(joint),
        P(joint),
        P(),
        P(joint),
        P(joint),
        P(None, joint),
        P(joint),
        P(joint, None, None),
        P(joint),
        P(joint),
        P(joint),
    )
    out_specs = (
        P(joint, None),
        P(None, joint, None),
        P(joint, None),
        P(None, joint, None),
        P(None, joint),
        P(),
        P(),
        P(joint),
        P(joint),
        P(joint),
        P(joint),
        P(joint),
        P(),
        P(),
    )
    return jax.shard_map(body, mesh=mesh, in_specs=in_specs, out_specs=out_specs, check_vma=False)
```

```python
import functools

import jax
import jax.numpy as jnp
from jax import lax
from jax.experimental import pallas as pl
from jax.experimental.pallas import tpu as pltpu
from jax.sharding import PartitionSpec as P

F = 128
R = 20
HOPS = 4
ELEMS = 100
STEP = 10
GROUPS = 7

CUTOFF = 5.0
BETA_ONE = 0.9
BETA_TWO = 0.99
RATE = 0.3
DECAY = 0.01
EPSILON = 1e-06

BLOCK = 256
WINDOW = 128
SUB = 32
ROWS = 256
F32 = jnp.float32
BF16 = jnp.bfloat16

AT_W1, AT_W2, AT_WF, AT_WM, AT_U1, AT_U2 = 0, 128, 512, 572, 828, 1084
AT_B1, AT_B2, AT_BF, AT_C1, AT_C2, AT_READ, PARAM_ROWS = 1468, 1469, 1472, 1475, 1476, 1479, 1480
PARAM_PAD = PARAM_ROWS + 8
GROUP_ENDS = (128, 512, 572, 828, 1084, 1468)
MESH = pl.DeviceIdType.MESH


def mm(left, right, contract=(1, 0)):
    return lax.dot_general(
        left, right, (((contract[0],), (contract[1],)), ((), ())), preferred_element_type=F32
    )


def split(value):
    high = value.astype(BF16)
    return high, (value - high.astype(F32)).astype(BF16)


def dot3(left, right, contract=(1, 0)):
    return (
        mm(left[0], right[0], contract)
        + mm(left[1], right[0], contract)
        + mm(left[0], right[1], contract)
    )


def sigmoid(value):
    return 1.0 / (1.0 + jnp.exp(-value))


def column(ref, start, parts, j, count=F):
    if parts == 1:
        return ref[start : start + count, :]
    return ref[pl.ds(start + j, count, stride=parts), :]


def add_column(ref, start, parts, j, value, count=F):
    if parts == 1:
        ref[start : start + count, :] += value
    else:
        ref[pl.ds(start + j, count, stride=parts), :] += value


def rows_of(start, count, unit):
    return pl.ds(pl.multiple_of(start, unit), count)


def layer_kernel(
    src_s,
    dst_s,
    count_s,
    crystal_s,
    dst_v,
    shift_v,
    lat,
    par,
    s_own,
    v_own,
    p_own,
    halo_rows,
    p_halo,
    cot_s,
    cot_v,
    goal,
    s_two,
    v_two,
    gs_own,
    gv_own,
    g_halo,
    gp_own,
    gp_halo,
    gpar,
    tab,
    rows,
    acc,
    cells,
    dtab,
    lrow,
    drow,
    misc,
    sums,
    gd,
    gbuf,
    fbuf,
    mbuf,
    ltbuf,
    tbuf,
    wcat,
    wq,
    gwf,
    gpd,
):
    atoms = s_own.shape[0]
    halo = halo_rows.shape[1]
    s_halo, v_halo = halo_rows.at[0], halo_rows.at[1:4]
    gs_halo, gv_halo = g_halo.at[0], g_halo.at[1:4]
    edges = shift_v.shape[1]
    blocks = edges // BLOCK

    wcat[...] = jnp.zeros_like(wcat)
    wq[...] = jnp.zeros_like(wq)
    gwf[...] = jnp.zeros_like(gwf)
    gpd[...] = jnp.zeros_like(gpd)
    gpar[...] = jnp.zeros_like(gpar)
    sums[...] = jnp.zeros_like(sums)
    for j in range(3):
        wide = jnp.concatenate(
            [
                column(par, AT_WF, 3, j, R),
                par[AT_BF + j : AT_BF + j + 1, :],
                jnp.zeros((3, F), F32),
            ],
            axis=0,
        )
        high = wide.astype(BF16).astype(F32)
        low = wide - high
        pieces = jnp.concatenate([high, high, low, jnp.zeros((56, F), F32)], axis=0)
        wcat[:, j * F : (j + 1) * F] = pieces.astype(BF16)
        pieces = jnp.concatenate([high, low, jnp.zeros((80, F), F32)], axis=0)
        wq[j * F : (j + 1) * F, :] = jnp.transpose(pieces).astype(BF16)

    @pl.loop(0, atoms // 8)
    def _(step):
        for j in range(8):
            a = step * 8 + j
            cells[pl.ds(a, 1), 0:9] = lat[pl.ds(crystal_s[a], 1), :]

    across = jnp.transpose(cells[...])
    blank = jnp.zeros((5, atoms), F32)
    part = jnp.concatenate(
        [p_own[...], blank, across[0:3], blank, across[3:6], blank, across[6:9], blank], axis=0
    )
    high = part.astype(BF16).astype(F32)
    middle = (part - high).astype(BF16).astype(F32)
    low = part - high - middle
    dtab[...] = jnp.concatenate([high, middle, low], axis=0).astype(BF16)

    for s_ref, v_ref, p_ref, base, count in (
        (s_own, v_own, p_own, 0, atoms),
        (s_halo, v_halo, p_halo, atoms, halo),
    ):
        place = jnp.concatenate([p_ref[0:3, :], jnp.zeros((F - 3, count), F32)], axis=0)
        tab[pl.ds(base * 8 + 6, count, stride=8), :] = jnp.transpose(place)
        tab[pl.ds(base * 8 + 7, count, stride=8), :] = jnp.zeros((count, F), F32)
        for c in range(3):
            tab[pl.ds(base * 8 + 3 + c, count, stride=8), :] = v_ref[c]

        @pl.loop(0, count // ROWS)
        def _(step):
            first = step * ROWS
            s_pair = split(s_ref[rows_of(first, ROWS, ROWS), :])
            act = dot3(s_pair, split(column(par, AT_W1, 1, 0))) + par[AT_B1 : AT_B1 + 1, :]
            hidden = split(act * sigmoid(act))
            for j in range(3):
                x = dot3(hidden, split(column(par, AT_W2, 3, j))) + par[AT_B2 + j : AT_B2 + j + 1, :]
                tab[pl.ds((base + first) * 8 + j, ROWS, stride=8), :] = x

    @pl.loop(0, edges // 32)
    def _(step):
        for j in range(32):
            e = step * 32 + j
            rows[rows_of(e * 8, 8, 8), :] = tab[rows_of(src_s[e] * 8, 8, 8), :]

    lanes = lax.broadcasted_iota(jnp.int32, (1, BLOCK), 1)
    slots = lax.broadcasted_iota(jnp.int32, (WINDOW, BLOCK), 0)
    eight = lax.broadcasted_iota(jnp.int32, (8, 1), 0)
    order = lax.broadcasted_iota(jnp.int32, (24, 1), 0)
    wide_lane = lax.broadcasted_iota(jnp.int32, (1, F), 1)

    def destinations(i):
        return jnp.concatenate(
            [dst_v[pl.ds(i * (BLOCK // F) + k, 1), :] for k in range(BLOCK // F)], axis=1
        )

    def window_range(i):
        return dst_s[i * BLOCK] // WINDOW, dst_s[i * BLOCK + BLOCK - 1] // WINDOW

    def hot(dst, w):
        return jnp.where(dst - w * WINDOW == slots, 1.0, 0.0).astype(BF16)

    def over_windows(first, last, body, start):
        return lax.fori_loop(first + 1, last + 1, body, body(first, start))

    def lane_pieces(pieces, extra):
        full = jnp.concatenate(
            [pieces, pieces[0:24], extra, jnp.zeros((F - 80, BLOCK), F32)], axis=0
        )
        return jnp.transpose(full)

    def comp(i, k, sub):
        return pl.ds(i * (BLOCK * 8) + sub * (SUB * 8) + k, SUB, stride=8)

    @pl.loop(0, blocks)
    def _(i):
        here = rows_of(i * BLOCK, BLOCK, BLOCK)
        first, last = window_range(i)
        dst = destinations(i)
        place = jnp.transpose(rows[pl.ds(i * (BLOCK * 8) + 6, BLOCK, stride=8), :])[0:8]
        ends = over_windows(
            first,
            last,
            lambda w, got: got + mm(dtab[:, rows_of(w * WINDOW, WINDOW, WINDOW)], hot(dst, w)),
            jnp.zeros((96, BLOCK), F32),
        )
        ends = ends[0:32] + ends[32:64] + ends[64:96]
        shift = shift_v[:, here].astype(F32)
        rel = (
            place
            + (shift[0:1] * ends[8:16] + shift[1:2] * ends[16:24] + shift[2:3] * ends[24:32])
            - ends[0:8]
        )
        square = jnp.sum(rel * rel, axis=0, keepdims=True)
        dist = jnp.sqrt(jnp.maximum(square, 0.25))
        inv = 1.0 / dist
        unit = rel * inv
        free = jnp.where(square > 0.25, 1.0, 0.0)
        angle = dist * (jnp.pi / CUTOFF)
        phase = (eight + 1).astype(F32) * angle
        sin_a, cos_a = jnp.sin(phase), jnp.cos(phase)
        sin_8, cos_8 = sin_a[7:8], cos_a[7:8]
        sin_b = sin_a * cos_8 + cos_a * sin_8
        cos_b = cos_a * cos_8 - sin_a * sin_8
        sin_c = sin_b * cos_8 + cos_b * sin_8
        cos_c = cos_b * cos_8 - sin_b * sin_8
        sines = jnp.concatenate([sin_a, sin_b, sin_c], axis=0)
        cosines = jnp.concatenate([cos_a, cos_b, cos_c], axis=0)
        radial = sines * inv
        slope = ((order + 1).astype(F32) * (jnp.pi / CUTOFF) * cosines - radial) * inv
        radial = jnp.where(order < R, radial, jnp.where(order == R, 1.0, 0.0))
        slope = jnp.where(order < R, slope, 0.0)
        inside = (dist < CUTOFF) & (i * BLOCK + lanes < count_s[0])
        envelope = jnp.where(inside, 0.5 * (cos_a[0:1] + 1.0), 0.0)
        fall = jnp.where(inside, (-0.5 * jnp.pi / CUTOFF) * sin_a[0:1], 0.0)
        scaled = envelope * radial
        high = scaled.astype(BF16).astype(F32)
        pieces = jnp.concatenate([high, scaled - high], axis=0)
        extra = jnp.where(
            eight < 3,
            unit,
            jnp.where(
                eight == 3,
                dst.astype(F32),
                jnp.where(eight == 4, inv, jnp.where(eight == 5, free, 0.0)),
            ),
        )
        lrow[:, here] = pieces.astype(BF16)
        drow[:, here] = fall * radial + envelope * slope
        misc[:, here] = extra
        ltbuf[...] = lane_pieces(pieces, extra)
        fbuf[...] = mm(ltbuf[...].astype(BF16), wcat[...])
        for sub in range(BLOCK // SUB):
            at = slice(sub * SUB, (sub + 1) * SUB)
            m1, m2, m3 = [
                rows[comp(i, j, sub), :] * fbuf[at, j * F : (j + 1) * F] for j in range(3)
            ]
            out = [m1]
            for c in range(3):
                out.append(m2 * ltbuf[at, 72 + c : 73 + c] + m3 * rows[comp(i, 3 + c, sub), :])
            for k in range(4):
                high, low = split(out[k])
                mbuf[at, k * F : (k + 1) * F] = high
                mbuf[at, (4 + k) * F : (5 + k) * F] = low

        def collect(w, ignored):
            pick = hot(dst, w)
            sums[rows_of(w * WINDOW, WINDOW, WINDOW), :] += mm(pick, mbuf[:, : 4 * F]) + mm(
                pick, mbuf[:, 4 * F :]
            )
            return ignored

        over_windows(first, last, collect, 0)

    @pl.loop(0, atoms // ROWS)
    def _(step):
        at = rows_of(step * ROWS, ROWS, ROWS)
        s_one = s_own[at, :] + sums[at, 0:F]
        v_one = [v_own[c, at, :] + sums[at, (c + 1) * F : (c + 2) * F] for c in range(3)]
        wm = [split(column(par, AT_WM, 2, j)) for j in range(2)]
        u1 = [split(par[AT_U1 + j * F : AT_U1 + (j + 1) * F, :]) for j in range(2)]
        u2 = [split(column(par, AT_U2, 3, j)) for j in range(3)]
        v_pair = [split(v) for v in v_one]
        v_lin = [dot3(v, wm[0]) for v in v_pair]
        w_lin = [dot3(v, wm[1]) for v in v_pair]
        size = jnp.sqrt(v_lin[0] * v_lin[0] + v_lin[1] * v_lin[1] + v_lin[2] * v_lin[2] + 1.0)
        s_pair, size_pair = split(s_one), split(size)
        act = dot3(s_pair, u1[0]) + dot3(size_pair, u1[1]) + par[AT_C1 : AT_C1 + 1, :]
        gate = sigmoid(act)
        hidden = split(act * gate)
        a1, a2, a3 = [dot3(hidden, u2[j]) + par[AT_C2 + j : AT_C2 + j + 1, :] for j in range(3)]
        inner = v_lin[0] * w_lin[0] + v_lin[1] * w_lin[1] + v_lin[2] * w_lin[2]
        s_out = s_one + a3 + a2 * inner
        s_two[at, :] = s_out
        read = par[AT_READ : AT_READ + 1, :]
        out_pair = split(s_out)
        energy = dot3(split(jnp.broadcast_to(read, (8, F))), out_pair, (1, 1))
        error = energy - goal[:, at]
        error_col = jnp.transpose(error)[:, 0:1]
        gpar[AT_READ : AT_READ + 1, :] += dot3(split(error), out_pair)[0:1]
        gs = cot_s[at, :] + error_col * read
        gv = []
        for c in range(3):
            v_two[c, at, :] = v_one[c] + a1 * w_lin[c]
            gv.append(cot_v[c, at, :])
        ga = [gv[0] * w_lin[0] + gv[1] * w_lin[1] + gv[2] * w_lin[2], gs * inner, gs]
        g_inner = gs * a2
        ga_pair = [split(g) for g in ga]
        for j in range(3):
            add_column(gpar, AT_U2, 3, j, dot3(hidden, ga_pair[j], (0, 0)))
            gpar[AT_C2 + j : AT_C2 + j + 1, :] += jnp.sum(ga[j], axis=0, keepdims=True)
        g_hidden = (
            dot3(ga_pair[0], u2[0], (1, 1))
            + dot3(ga_pair[1], u2[1], (1, 1))
            + dot3(ga_pair[2], u2[2], (1, 1))
        )
        g_act = g_hidden * (gate * (1.0 + act * (1.0 - gate)))
        g_act_pair = split(g_act)
        add_column(gpar, AT_U1, 1, 0, dot3(s_pair, g_act_pair, (0, 0)))
        add_column(gpar, AT_U1 + F, 1, 0, dot3(size_pair, g_act_pair, (0, 0)))
        gpar[AT_C1 : AT_C1 + 1, :] += jnp.sum(g_act, axis=0, keepdims=True)
        g_s_one = gs + dot3(g_act_pair, u1[0], (1, 1))
        g_size = dot3(g_act_pair, u1[1], (1, 1)) / size
        gs_own[at, :] = g_s_one
        down = [g_s_one]
        for c in range(3):
            g_w = split(a1 * gv[c] + g_inner * v_lin[c])
            g_v = split(g_inner * w_lin[c] + g_size * v_lin[c])
            add_column(gpar, AT_WM, 2, 0, dot3(v_pair[c], g_v, (0, 0)))
            add_column(gpar, AT_WM, 2, 1, dot3(v_pair[c], g_w, (0, 0)))
            g_v_one = gv[c] + dot3(g_v, wm[0], (1, 1)) + dot3(g_w, wm[1], (1, 1))
            gv_own[c, at, :] = g_v_one
            down.append(g_v_one)
        for k in range(4):
            high, low = split(down[k])
            for part in range(ROWS // WINDOW):
                to = (step * (ROWS // WINDOW) + part) * (2 * WINDOW)
                of = slice(part * WINDOW, (part + 1) * WINDOW)
                gd[rows_of(to, WINDOW, WINDOW), k * F : (k + 1) * F] = high[of]
                gd[rows_of(to + WINDOW, WINDOW, WINDOW), k * F : (k + 1) * F] = low[of]

    twice = (lax.broadcasted_iota(jnp.int32, (1, 2 * WINDOW), 1) % WINDOW).astype(F32)

    @pl.loop(0, blocks)
    def _(i):
        here = rows_of(i * BLOCK, BLOCK, BLOCK)
        first, last = window_range(i)
        dst = destinations(i)
        extra = misc[:, here]
        ltbuf[...] = lane_pieces(lrow[:, here].astype(F32), extra)
        fbuf[...] = mm(ltbuf[...].astype(BF16), wcat[...])
        dst_col = ltbuf[:, 75:76]

        def fetch(w):
            near = dst_col - (w * WINDOW).astype(F32)
            return mm(
                jnp.where(near == twice, 1.0, 0.0).astype(BF16),
                gd[rows_of(w * 2 * WINDOW, 2 * WINDOW, 2 * WINDOW), :],
            )

        gbuf[...] = fetch(first)

        @pl.loop(first + 1, last + 1)
        def _(w):
            gbuf[...] += fetch(w)

        for sub in range(BLOCK // SUB):
            at = slice(sub * SUB, (sub + 1) * SUB)
            g_s = gbuf[at, 0:F]
            g_v = [gbuf[at, (c + 1) * F : (c + 2) * F] for c in range(3)]
            x = [rows[comp(i, j, sub), :] for j in range(3)]
            v = [rows[comp(i, 3 + c, sub), :] for c in range(3)]
            f = [fbuf[at, j * F : (j + 1) * F] for j in range(3)]
            u = [ltbuf[at, 72 + c : 73 + c] for c in range(3)]
            g_m = [
                g_s,
                g_v[0] * u[0] + g_v[1] * u[1] + g_v[2] * u[2],
                g_v[0] * v[0] + g_v[1] * v[1] + g_v[2] * v[2],
            ]
            m2 = x[1] * f[1]
            m3 = x[2] * f[2]
            turn = jnp.zeros((SUB, F), F32)
            for c in range(3):
                total = jnp.sum(g_v[c] * m2, axis=1, keepdims=True)
                turn = jnp.where(wide_lane == 48 + c, total, turn)
                rows[comp(i, 3 + c, sub), :] = g_v[c] * m3
            tbuf[at, :] = turn
            for j in range(3):
                high, low = split(g_m[j] * x[j])
                mbuf[at, j * F : (j + 1) * F] = high
                mbuf[at, (3 + j) * F : (4 + j) * F] = low
                rows[comp(i, j, sub), :] = g_m[j] * f[j]
        h_high, h_low = mbuf[:, : 3 * F], mbuf[:, 3 * F : 6 * F]
        back = jnp.transpose(mm(h_high, wq[...]) + mm(h_low, wq[...]) + tbuf[...])
        pieces = lrow[:, here]
        gwf[...] += mm(pieces, h_high) + mm(pieces, h_low)
        g_row = back[0:24] + back[24:48]
        g_unit = back[48:56]
        unit = jnp.where(eight < 3, extra, 0.0)
        inv, free = extra[4:5], extra[5:6]
        g_dist = jnp.sum(g_row * drow[:, here], axis=0, keepdims=True)
        along = jnp.sum(g_unit * unit, axis=0, keepdims=True)
        g_rel = g_unit * inv + (g_dist - along * inv) * free * unit
        rows[pl.ds(i * (BLOCK * 8) + 6, BLOCK, stride=8), :] = jnp.transpose(
            jnp.concatenate([g_rel, jnp.zeros((F - 8, BLOCK), F32)], axis=0)
        )
        high = g_rel.astype(BF16).astype(F32)
        middle = (g_rel - high).astype(BF16).astype(F32)
        g_pieces = jnp.concatenate([high, middle, g_rel - high - middle, jnp.zeros_like(g_rel)], axis=0)
        g_pieces = g_pieces.astype(BF16)

        def collect(w, ignored):
            got = mm(g_pieces, hot(dst, w), (1, 1))
            gpd[:, rows_of(w * WINDOW, WINDOW, WINDOW)] += got[0:8] + got[8:16] + got[16:24]
            return ignored

        over_windows(first, last, collect, 0)

    for j in range(3):
        total = gwf[0:24, j * F : (j + 1) * F] + gwf[24:48, j * F : (j + 1) * F]
        add_column(gpar, AT_WF, 3, j, total[0:R], R)
        gpar[AT_BF + j : AT_BF + j + 1, :] = total[R : R + 1]

    tab[...] = jnp.zeros_like(tab)
    acc[...] = jnp.zeros_like(acc)
    half = edges // 2

    @pl.loop(0, half // 8)
    def _(step):
        for j in range(8):
            for start, total in ((0, tab), (half, acc)):
                e = start + step * 8 + j
                to = rows_of(src_s[e] * 8, 8, 8)
                total[to, :] += rows[rows_of(e * 8, 8, 8), :]

    for s_ref, gs_ref, gv_ref, gp_ref, base, count in (
        (s_own, gs_own, gv_own, gp_own, 0, atoms),
        (s_halo, gs_halo, gv_halo, gp_halo, atoms, halo),
    ):
        own = base == 0
        for k in range(0, count, ROWS):
            at = pl.ds((base + k) * 8 + 6, ROWS, stride=8)
            place = jnp.transpose(tab[at, :] + acc[at, :])[0:8]
            if own:
                place = place - gpd[:, k : k + ROWS]
            gp_ref[:, k : k + ROWS] = place

        @pl.loop(0, count // ROWS)
        def _(step):
            first = step * ROWS
            to = rows_of(first, ROWS, ROWS)

            def gathered(k):
                at = pl.ds((base + first) * 8 + k, ROWS, stride=8)
                return tab[at, :] + acc[at, :]

            for c in range(3):
                if own:
                    gv_ref[c, to, :] += gathered(3 + c)
                else:
                    gv_ref[c, to, :] = gathered(3 + c)
            w1 = split(column(par, AT_W1, 1, 0))
            s_pair = split(s_ref[to, :])
            act = dot3(s_pair, w1) + par[AT_B1 : AT_B1 + 1, :]
            gate = sigmoid(act)
            hidden = split(act * gate)
            g_hidden = jnp.zeros((ROWS, F), F32)
            for j in range(3):
                g_x = gathered(j)
                g_pair = split(g_x)
                add_column(gpar, AT_W2, 3, j, dot3(hidden, g_pair, (0, 0)))
                gpar[AT_B2 + j : AT_B2 + j + 1, :] += jnp.sum(g_x, axis=0, keepdims=True)
                g_hidden = g_hidden + dot3(g_pair, split(column(par, AT_W2, 3, j)), (1, 1))
            g_act = g_hidden * (gate * (1.0 + act * (1.0 - gate)))
            g_act_pair = split(g_act)
            add_column(gpar, AT_W1, 1, 0, dot3(s_pair, g_act_pair, (0, 0)))
            gpar[AT_B1 : AT_B1 + 1, :] += jnp.sum(g_act, axis=0, keepdims=True)
            g_s = dot3(g_act_pair, w1, (1, 1))
            if own:
                gs_ref[to, :] += g_s
            else:
                gs_ref[to, :] = g_s


def layer(atoms, halo, edges, smem, vmem):
    shape = jax.ShapeDtypeStruct
    total = atoms + halo
    in_vmem = pl.BlockSpec(memory_space=pltpu.VMEM)
    in_smem = pl.BlockSpec(memory_space=pltpu.SMEM)
    outs = (
        shape((atoms, F), F32),
        shape((3, atoms, F), F32),
        shape((atoms, F), F32),
        shape((3, atoms, F), F32),
        shape((4, halo, F), F32),
        shape((8, atoms), F32),
        shape((8, halo), F32),
        shape((PARAM_PAD, F), F32),
    )
    scratch = [
        pltpu.VMEM((total * 8, F), F32),
        pltpu.VMEM((edges * 8, F), F32),
        pltpu.VMEM((total * 8, F), F32),
        pltpu.VMEM((atoms, F), F32),
        pltpu.VMEM((96, atoms), BF16),
        pltpu.VMEM((48, edges), BF16),
        pltpu.VMEM((24, edges), F32),
        pltpu.VMEM((8, edges), F32),
        pltpu.VMEM((atoms, 4 * F), F32),
        pltpu.VMEM((2 * atoms, 4 * F), BF16),
        pltpu.VMEM((BLOCK, 4 * F), F32),
        pltpu.VMEM((BLOCK, 3 * F), F32),
        pltpu.VMEM((BLOCK, 8 * F), BF16),
        pltpu.VMEM((BLOCK, F), F32),
        pltpu.VMEM((BLOCK, F), F32),
        pltpu.VMEM((F, 3 * F), BF16),
        pltpu.VMEM((3 * F, F), BF16),
        pltpu.VMEM((48, 3 * F), F32),
        pltpu.VMEM((8, atoms), F32),
    ]
    return pl.pallas_call(
        layer_kernel,
        out_shape=outs,
        in_specs=[in_smem] * smem + [in_vmem] * vmem,
        out_specs=(in_vmem,) * len(outs),
        scratch_shapes=scratch,
        compiler_params=pltpu.CompilerParams(vmem_limit_bytes=62 * 1024 * 1024),
        name="layer",
    )


def hop_offset(j):
    return j + 1 if j < HOPS else HOPS - 1 - j


class Place:
    def __init__(self):
        self.chips = lax.axis_size("atoms")
        self.cores = lax.axis_size("rep")
        self.count = self.chips * self.cores
        self.groups = self.chips // 4
        chip = lax.axis_index("atoms")
        self.core = lax.axis_index("rep")
        self.joint = chip * self.cores + self.core
        self.group = chip // 4
        self.quarter = chip % 4
        self.mate = 1 - self.core

    def other_groups(self):
        return [lax.rem(self.group + k, self.groups) for k in range(1, self.groups)]

    def other_quarters(self):
        return [lax.rem(self.quarter + k, 4) for k in range(1, 4)]

    def in_group(self, group):
        return (group * 4 + self.quarter, self.core)

    def in_quarter(self, quarter):
        return (self.group * 4 + quarter, self.core)

    def beside(self):
        return (self.group * 4 + self.quarter, self.mate)

    def hop(self, by):
        other = self.joint + by
        exists = (other >= 0) & (other < self.count)
        other = jnp.clip(other, 0, self.count - 1)
        return exists, (other // self.cores, other % self.cores)

    def greet(self):
        barrier = pltpu.get_barrier_semaphore()
        fixed = [self.in_group(g) for g in self.other_groups()]
        fixed += [self.in_quarter(q) for q in self.other_quarters()]
        fixed.append(self.beside())
        for device in fixed:
            pl.semaphore_signal(barrier, inc=1, device_id=device, device_id_type=MESH)
        hops = [self.hop(hop_offset(j)) for j in range(2 * HOPS)]
        expected = jnp.int32(len(fixed))
        for exists, device in hops:
            expected = expected + jnp.where(exists, 1, 0)

            @pl.when(exists)
            def _():
                pl.semaphore_signal(barrier, inc=1, device_id=device, device_id_type=MESH)

        pl.semaphore_wait(barrier, expected)


def send(src, dst, send_sem, recv_sem, device):
    return pltpu.make_async_remote_copy(
        src_ref=src,
        dst_ref=dst,
        send_sem=send_sem,
        recv_sem=recv_sem,
        device_id=device,
        device_id_type=MESH,
    )


def start_all(copies):
    for copy in copies:
        copy.start()
    return copies


def wait_sent(copies):
    for copy in copies:
        copy.wait_send()


def window_rows(length):
    return -(-((length + F - 1) // F + 1) // 8) * 8


class SmallSum:
    def __init__(self, place, slots_a, slots_b, slots_c, sends, recvs):
        self.place = place
        self.slots = (slots_a, slots_b, slots_c)
        self.sends, self.recvs = sends, recvs
        self.sent = []

    def start(self, phase, value):
        p = self.place
        slots = self.slots[phase]
        mine = (p.group, p.quarter, p.core)[phase]
        slots[mine] = value
        base = (0, p.groups, p.groups + 4)[phase]
        devices = (
            [p.in_group(g) for g in p.other_groups()],
            [p.in_quarter(q) for q in p.other_quarters()],
            [p.beside()],
        )[phase]
        for k, device in enumerate(devices):
            self.sent.append(
                send(
                    slots.at[mine],
                    slots.at[mine],
                    self.sends.at[base + k],
                    self.recvs.at[base + mine],
                    device,
                )
            )
            self.sent[-1].start()

    def finish(self, phase):
        p = self.place
        slots = self.slots[phase]
        base = (0, p.groups, p.groups + 4)[phase]
        others = (p.other_groups(), p.other_quarters(), [p.mate])[phase]
        for o in others:
            send(
                slots.at[o], slots.at[o], self.sends.at[base], self.recvs.at[base + o], p.beside()
            ).wait_recv()
        total = slots[0]
        for k in range(1, slots.shape[0]):
            total = total + slots[k]
        return total

    def done(self):
        wait_sent(self.sent)


def small_scratch(groups, rows):
    count = groups + 4 + 2
    return [
        pltpu.VMEM((groups, rows, F), F32),
        pltpu.VMEM((4, rows, F), F32),
        pltpu.VMEM((2, rows, F), F32),
        pltpu.SemaphoreType.DMA((count,)),
        pltpu.SemaphoreType.DMA((count,)),
    ]


def lay_flat(ref, count):
    return jnp.concatenate([ref[k : k + 1, :] for k in range(count)], axis=1)


def gather_kernel(
    send_s,
    par_in,
    s_own,
    v_own,
    p_own,
    energy,
    elements,
    forces,
    par,
    halo_rows,
    p_halo,
    goal,
    stats,
    slots,
    pack,
    places,
    p_out,
    p_in,
    zeros,
    ag_send,
    ag_recv,
    row_send,
    row_recv,
    place_send,
    place_recv,
    zero_sem,
    *small,
    length,
):
    here = Place()
    atoms = s_own.shape[0]
    cap = halo_rows.shape[1] // (2 * HOPS)
    wide = slots.shape[3]
    here.greet()
    sums = SmallSum(here, *small)

    offset = lax.rem(here.joint * length, F)
    lane = lax.broadcasted_iota(jnp.int32, (1, F), 1)
    turned = pltpu.roll(par_in[...], offset, 1)
    above = jnp.concatenate([jnp.zeros((1, F), F32), turned[: wide - 1]], axis=0)
    mine = slots.at[here.group, here.quarter, here.core]
    mine[...] = jnp.where(lane < offset, above, turned)
    first = start_all(
        [
            send(mine, mine, ag_send.at[k], ag_recv.at[here.group], here.in_group(g))
            for k, g in enumerate(here.other_groups())
        ]
    )

    count = atoms // F
    energy_row, element_row = lay_flat(energy, count), lay_flat(elements, count)
    hot = jnp.where(
        element_row == lax.broadcasted_iota(jnp.int32, (F, atoms), 0), 1.0, 0.0
    ).astype(BF16)
    high = energy_row.astype(BF16).astype(F32)
    middle = (energy_row - high).astype(BF16).astype(F32)
    eight = lax.broadcasted_iota(jnp.int32, (8, 1), 0)
    left = jnp.where(
        eight == 0,
        high,
        jnp.where(
            eight == 1, middle, jnp.where(eight == 2, energy_row - high - middle, jnp.where(eight == 3, 1.0, 0.0))
        ),
    )
    found = mm(left.astype(BF16), hot, (1, 1))
    squares = jnp.sum(forces[...] * forces[...], axis=0, keepdims=True)
    square = squares[:, 0:F]
    for k in range(1, count):
        square = square + squares[:, k * F : (k + 1) * F]
    tile = jnp.where(
        eight == 0,
        found[0:1] + found[1:2] + found[2:3],
        jnp.where(eight == 1, found[3:4], jnp.where(eight == 2, square, 0.0)),
    )
    sums.start(0, tile)

    places[...] = jnp.transpose(
        jnp.concatenate([p_own[...], jnp.zeros((F - 3, atoms), F32)], axis=0)
    )
    zeros[...] = jnp.zeros_like(zeros)
    hops = range(2 * HOPS)
    row_copies, place_copies = [], []
    for j in hops:
        exists, device = here.hop(hop_offset(j))
        block = pl.ds(j * cap, cap)

        @pl.loop(0, cap // 8)
        def _(step):
            for k in range(8):
                r = j * cap + step * 8 + k
                t = send_s[r]
                pack[0, pl.ds(r, 1), :] = s_own[pl.ds(t, 1), :]
                for c in range(3):
                    pack[1 + c, pl.ds(r, 1), :] = v_own[c, pl.ds(t, 1), :]
                p_out[pl.ds(r, 1), :] = places[pl.ds(t, 1), :]

        copy = send(
            pack.at[:, block], halo_rows.at[:, block], row_send.at[j], row_recv.at[j], device
        )
        row_copies.append((exists, copy))

        @pl.when(exists)
        def _():
            copy.start()

    for j in range(0, 2 * HOPS, 2):
        pair = slice(j * cap, (j + 2) * cap)
        p_in[2 * HOPS + j // 2] = jnp.transpose(p_out[pair, :])[0:8]
        for k in (j, j + 1):
            exists, device = here.hop(hop_offset(k))
            copy = send(
                p_in.at[2 * HOPS + j // 2], p_in.at[k], place_send.at[k], place_recv.at[k], device
            )
            place_copies.append((exists, copy))

            @pl.when(exists)
            def _():
                copy.start()

    for j in hops:
        known, device = here.hop(-hop_offset(j))

        @pl.when(jnp.logical_not(known))
        def _():
            p_in[j] = jnp.zeros((8, F), F32)
            fill = pltpu.make_async_copy(
                zeros, halo_rows.at[:, pl.ds(j * cap, cap)], zero_sem.at[j]
            )
            fill.start()
            fill.wait()

    for g in here.other_groups():
        spot = slots.at[g, here.quarter, here.core]
        send(spot, spot, ag_send.at[0], ag_recv.at[g], here.beside()).wait_recv()
    base = here.groups
    line = slots.at[:, here.quarter, here.core]
    second = start_all(
        [
            send(line, line, ag_send.at[base + k], ag_recv.at[base + here.quarter], here.in_quarter(q))
            for k, q in enumerate(here.other_quarters())
        ]
    )
    third = [
        send(
            line, line, ag_send.at[base + 4], ag_recv.at[base + 4 + here.quarter], here.beside()
        )
    ]
    third[0].start()
    sums.start(1, sums.finish(0))
    for k, q in enumerate(here.other_quarters()):
        line = slots.at[:, q, here.core]
        send(line, line, ag_send.at[0], ag_recv.at[base + q], here.beside()).wait_recv()
        copy = send(
            line, line, ag_send.at[base + 5 + k], ag_recv.at[base + 4 + q], here.beside()
        )
        copy.start()
        third.append(copy)
    sums.start(2, sums.finish(1))
    for q in range(4):
        line = slots.at[:, q, here.mate]
        send(line, line, ag_send.at[0], ag_recv.at[base + 4 + q], here.beside()).wait_recv()

    par[...] = jnp.zeros_like(par)
    for p in range(here.count):
        row = p * length // F
        chip, core = p // here.cores, p % here.cores
        take = min(wide, PARAM_PAD - row)
        par[row : row + take, :] += slots[chip // 4, chip % 4, core, 0:take, :]

    total = sums.finish(2)
    mean = total[0:1] / jnp.maximum(total[1:2], 1.0)
    whole = jnp.sum(total[2:3], axis=1, keepdims=True)
    scale = jnp.sqrt(whole / (3.0 * atoms * here.count) + 1e-06)
    high = mean.astype(BF16).astype(F32)
    middle = (mean - high).astype(BF16).astype(F32)
    left = jnp.where(
        eight == 0,
        high,
        jnp.where(eight == 1, middle, jnp.where(eight == 2, mean - high - middle, 0.0)),
    )
    found = mm(left.astype(BF16), hot)
    goal[...] = (energy_row - (found[0:1] + found[1:2] + found[2:3])) / scale
    stats[...] = jnp.where(eight == 0, mean, jnp.where(eight == 1, scale, 0.0))

    for j in hops:
        known, device = here.hop(-hop_offset(j))

        @pl.when(known)
        def _():
            block = pl.ds(j * cap, cap)
            send(
                pack.at[:, block], halo_rows.at[:, block], row_send.at[j], row_recv.at[j], device
            ).wait_recv()
            send(p_in.at[j], p_in.at[j], place_send.at[j], place_recv.at[j], device).wait_recv()

    low_half = lane < cap
    for j in range(0, 2 * HOPS, 2):
        p_halo[:, j * cap : (j + 2) * cap] = jnp.where(low_half, p_in[j], p_in[j + 1])
    for exists, copy in row_copies + place_copies:

        @pl.when(exists)
        def _():
            copy.wait_send()

    wait_sent(first + second + third)
    sums.done()


def gather_all(atoms, cap, groups, length):
    shape = jax.ShapeDtypeStruct
    halo = 2 * HOPS * cap
    wide = window_rows(length)
    in_vmem = pl.BlockSpec(memory_space=pltpu.VMEM)
    in_smem = pl.BlockSpec(memory_space=pltpu.SMEM)
    return pl.pallas_call(
        functools.partial(gather_kernel, length=length),
        out_shape=(
            shape((PARAM_PAD, F), F32),
            shape((4, halo, F), F32),
            shape((8, halo), F32),
            shape((1, atoms), F32),
            shape((8, F), F32),
        ),
        in_specs=[in_smem] + [in_vmem] * 7,
        out_specs=(in_vmem, pl.BlockSpec(memory_space=pl.ANY), in_vmem, in_vmem, in_vmem),
        scratch_shapes=[
            pltpu.VMEM((groups, 4, 2, wide, F), F32),
            pltpu.VMEM((4, halo, F), F32),
            pltpu.VMEM((atoms, F), F32),
            pltpu.VMEM((halo, F), F32),
            pltpu.VMEM((3 * HOPS, 8, F), F32),
            pltpu.VMEM((4, cap, F), F32),
            pltpu.SemaphoreType.DMA((groups + 8,)),
            pltpu.SemaphoreType.DMA((groups + 8,)),
            pltpu.SemaphoreType.DMA((2 * HOPS,)),
            pltpu.SemaphoreType.DMA((2 * HOPS,)),
            pltpu.SemaphoreType.DMA((2 * HOPS,)),
            pltpu.SemaphoreType.DMA((2 * HOPS,)),
            pltpu.SemaphoreType.DMA((2 * HOPS,)),
        ]
        + small_scratch(groups, 8),
        compiler_params=pltpu.CompilerParams(
            collective_id=0, has_side_effects=True, vmem_limit_bytes=40 * 1024 * 1024
        ),
        name="gather_inputs",
    )


def reduce_kernel(
    gpar,
    g_halo,
    gp_halo,
    gs_own,
    gv_own,
    gp_own,
    pick,
    par,
    one,
    two,
    grad_s,
    grad_v,
    grad_p,
    grad,
    one_new,
    two_new,
    par_new,
    norms,
    slots,
    pair_in,
    line_in,
    spot_in,
    back,
    p_back,
    turn,
    rs_send,
    rs_recv,
    row_send,
    row_recv,
    place_send,
    place_recv,
    *small,
    length,
):
    here = Place()
    atoms = gs_own.shape[0]
    cap = back.shape[1] // (2 * HOPS)
    wide = slots.shape[3]
    here.greet()
    sums = SmallSum(here, *small)

    for p in range(here.count):
        row = p * length // F
        chip, core = p // here.cores, p % here.cores
        take = min(wide, PARAM_PAD - row)
        slots[chip // 4, chip % 4, core, 0:take, :] = gpar[row : row + take, :]
    order = here.other_quarters() + [here.quarter]
    base = here.groups
    third = start_all(
        [
            send(
                slots.at[:, q, here.mate],
                pair_in.at[:, q],
                rs_send.at[base + 4 + k],
                rs_recv.at[base + 4 + q],
                here.beside(),
            )
            for k, q in enumerate(order)
        ]
    )

    hops = range(2 * HOPS)
    copies = []
    for j in hops:
        exists, device = here.hop(-hop_offset(j))
        block = pl.ds(j * cap, cap)
        tile = pl.ds((j // 2) * F, F)
        rows_copy = send(
            g_halo.at[:, block], back.at[:, block], row_send.at[j], row_recv.at[j], device
        )
        place_copy = send(
            gp_halo.at[:, tile], p_back.at[j], place_send.at[j], place_recv.at[j], device
        )
        copies += [(exists, rows_copy), (exists, place_copy)]

        @pl.when(exists)
        def _():
            rows_copy.start()
            place_copy.start()

        known, device = here.hop(hop_offset(j))

        @pl.when(jnp.logical_not(known))
        def _():
            back[:, block, :] = jnp.zeros((4, cap, F), F32)
            p_back[j] = jnp.zeros((8, F), F32)

    second = []
    for k, q in enumerate(order):
        line = pair_in.at[:, q]
        send(line, line, rs_send.at[0], rs_recv.at[base + 4 + q], here.beside()).wait_recv()
        slots[:, q, here.core] += pair_in[:, q]
        if k < 3:
            copy = send(
                slots.at[:, q, here.core],
                line_in.at[here.quarter],
                rs_send.at[base + k],
                rs_recv.at[base + here.quarter],
                here.in_quarter(q),
            )
            copy.start()
            second.append(copy)
    for q in here.other_quarters():
        line = line_in.at[q]
        send(line, line, rs_send.at[0], rs_recv.at[base + q], here.beside()).wait_recv()
        slots[:, here.quarter, here.core] += line_in[q]
    first = start_all(
        [
            send(
                slots.at[g, here.quarter, here.core],
                spot_in.at[here.group],
                rs_send.at[k],
                rs_recv.at[here.group],
                here.in_group(g),
            )
            for k, g in enumerate(here.other_groups())
        ]
    )
    total = slots[here.group, here.quarter, here.core]
    for g in here.other_groups():
        spot = spot_in.at[g]
        send(spot, spot, rs_send.at[0], rs_recv.at[g], here.beside()).wait_recv()
        total = total + spot_in[g]

    offset = lax.rem(here.joint * length, F)
    lane = lax.broadcasted_iota(jnp.int32, (1, F), 1)
    turn[0:wide, :] = pltpu.roll(total, lax.rem(F - offset, F), 1)
    turn[wide : wide + 8, :] = jnp.zeros((8, F), F32)
    place = lax.broadcasted_iota(jnp.int32, (wide, F), 0) * F + lane
    inside = place < length
    g = jnp.where(lane + offset < F, turn[0:wide, :], turn[1 : wide + 1, :])
    g = jnp.where(inside, g, 0.0)
    grad[...] = g
    m_one = BETA_ONE * one[...] + (1.0 - BETA_ONE) * g
    m_two = BETA_TWO * two[...] + (1.0 - BETA_TWO) * g * g
    one_new[...] = m_one
    two_new[...] = m_two
    direction = (
        m_one
        / (1.0 - BETA_ONE**STEP)
        / (jnp.sqrt(m_two / (1.0 - BETA_TWO**STEP)) + EPSILON)
        + DECAY * par[...]
    )
    spot = place + here.joint * length
    label = jnp.zeros((wide, F), jnp.int32)
    for end in GROUP_ENDS:
        label = label + jnp.where(spot >= end * F, 1, 0)
    label = jnp.where(inside, label, GROUPS)
    lines = []
    for value in (par[...], direction):
        square = value * value
        lines += [
            jnp.sum(jnp.where(label == k, square, 0.0), axis=0, keepdims=True)
            for k in range(GROUPS)
        ]
        lines.append(jnp.zeros((1, F), F32))
    sums.start(0, jnp.concatenate(lines, axis=0))

    hot = jnp.where(
        pick[...] == lax.broadcasted_iota(jnp.int32, (atoms, 2 * HOPS * cap), 0), 1.0, 0.0
    ).astype(BF16)
    for j in hops:
        known, device = here.hop(hop_offset(j))

        @pl.when(known)
        def _():
            block = pl.ds(j * cap, cap)
            tile = p_back.at[j]
            send(
                back.at[:, block], back.at[:, block], row_send.at[j], row_recv.at[j], device
            ).wait_recv()
            send(tile, tile, place_send.at[j], place_recv.at[j], device).wait_recv()

    sums.start(1, sums.finish(0))
    for k in range(2):
        high, low = split(back[k])
        extra = mm(hot, high) + mm(hot, low)
        if k == 0:
            grad_s[...] = gs_own[...] + extra
        else:
            grad_v[k - 1] = gv_own[k - 1] + extra
    sums.start(2, sums.finish(1))
    for k in range(2, 4):
        high, low = split(back[k])
        grad_v[k - 1] = gv_own[k - 1] + (mm(hot, high) + mm(hot, low))
    low_half = lane < cap
    place = jnp.concatenate(
        [jnp.where(low_half, p_back[j], p_back[j + 1]) for j in range(0, 2 * HOPS, 2)], axis=1
    )
    high = place.astype(BF16).astype(F32)
    middle = (place - high).astype(BF16).astype(F32)
    pieces = jnp.concatenate([high, middle, place - high - middle, jnp.zeros_like(place)], axis=0)
    got = mm(pieces.astype(BF16), hot, (1, 1))
    grad_p[...] = gp_own[...] + (got[0:8] + got[8:16] + got[16:24])

    whole = jnp.sqrt(jnp.sum(sums.finish(2), axis=1, keepdims=True))
    ratio = whole[0:8] / whole[8:16]
    norms[...] = jnp.broadcast_to(whole, (16, F))
    trust = jnp.zeros((wide, F), F32)
    for k in range(GROUPS):
        trust = jnp.where(label == k, ratio[k : k + 1], trust)
    par_new[...] = par[...] - RATE * trust * direction

    for exists, copy in copies:

        @pl.when(exists)
        def _():
            copy.wait_send()

    wait_sent(first + second + third)
    sums.done()


def reduce_all(atoms, cap, groups, length):
    shape = jax.ShapeDtypeStruct
    halo = 2 * HOPS * cap
    wide = window_rows(length)
    in_vmem = pl.BlockSpec(memory_space=pltpu.VMEM)
    outs = (
        [shape((atoms, F), F32), shape((3, atoms, F), F32), shape((8, atoms), F32)]
        + [shape((wide, F), F32)] * 4
        + [shape((16, F), F32)]
    )
    return pl.pallas_call(
        functools.partial(reduce_kernel, length=length),
        out_shape=tuple(outs),
        in_specs=[in_vmem] * 10,
        out_specs=(in_vmem,) * len(outs),
        scratch_shapes=[
            pltpu.VMEM((groups, 4, 2, wide, F), F32),
            pltpu.VMEM((groups, 4, wide, F), F32),
            pltpu.VMEM((4, groups, wide, F), F32),
            pltpu.VMEM((groups, wide, F), F32),
            pltpu.VMEM((4, halo, F), F32),
            pltpu.VMEM((2 * HOPS, 8, F), F32),
            pltpu.VMEM((wide + 8, F), F32),
            pltpu.SemaphoreType.DMA((groups + 8,)),
            pltpu.SemaphoreType.DMA((groups + 8,)),
            pltpu.SemaphoreType.DMA((2 * HOPS,)),
            pltpu.SemaphoreType.DMA((2 * HOPS,)),
            pltpu.SemaphoreType.DMA((2 * HOPS,)),
            pltpu.SemaphoreType.DMA((2 * HOPS,)),
        ]
        + small_scratch(groups, 16),
        compiler_params=pltpu.CompilerParams(
            collective_id=1, has_side_effects=True, vmem_limit_bytes=40 * 1024 * 1024
        ),
        name="reduce_outputs",
    )


def body(
    scalars_in,
    vectors_in,
    positions,
    cotan_scalar,
    cotan_vector,
    target_energy,
    forces,
    elements,
    crystal,
    lattice,
    edge_src,
    edge_dst,
    edge_shift,
    edge_count,
    send_rows,
    params,
    first_moment,
    second_moment,
):
    atoms = scalars_in.shape[0]
    edges = edge_src.shape[0]
    cap = send_rows.shape[2]
    halo = 2 * HOPS * cap
    groups = lax.axis_size("atoms") // 4
    length = params.shape[0]
    wide = window_rows(length)

    def padded(value):
        return jnp.pad(value, (0, wide * F - length)).reshape(wide, F)

    par_share = padded(params)
    pick = send_rows.reshape(1, halo)
    par, halo_rows, p_halo, goal, stats = gather_all(atoms, cap, groups, length)(
        pick.reshape(-1),
        par_share,
        scalars_in,
        vectors_in,
        positions,
        target_energy.reshape(-1, F),
        elements.reshape(-1, F),
        forces,
    )
    s_two, v_two, gs_own, gv_own, g_halo, gp_own, gp_halo, gpar = layer(atoms, halo, edges, 4, 12)(
        edge_src,
        edge_dst,
        edge_count,
        crystal,
        edge_dst.reshape(-1, F),
        edge_shift,
        lattice,
        par,
        scalars_in,
        vectors_in,
        positions,
        halo_rows,
        p_halo,
        cotan_scalar,
        cotan_vector,
        goal,
    )
    grad_s, grad_v, grad_p, grad, one_new, two_new, par_new, norms = reduce_all(
        atoms, cap, groups, length
    )(
        gpar,
        g_halo,
        gp_halo,
        gs_own,
        gv_own,
        gp_own,
        pick,
        par_share,
        padded(first_moment),
        padded(second_moment),
    )

    def share(value):
        return value.reshape(-1)[:length]

    params_new = share(par_new)
    return (
        s_two,
        v_two,
        grad_s,
        grad_v,
        grad_p[:3],
        stats[0, :ELEMS],
        stats[1, 0],
        share(grad),
        share(one_new),
        share(two_new),
        params_new,
        params_new.astype(BF16),
        norms[:GROUPS, 0],
        norms[8 : 8 + GROUPS, 0],
    )


def solution(mesh):
    joint = ("atoms", "rep")
    in_specs = (
        P(joint, None),
        P(None, joint, None),
        P(None, joint),
        P(joint, None),
        P(None, joint, None),
        P(joint),
        P(None, joint),
        P(joint),
        P(joint),
        P(),
        P(joint),
        P(joint),
        P(None, joint),
        P(joint),
        P(joint, None, None),
        P(joint),
        P(joint),
        P(joint),
    )
    out_specs = (
        P(joint, None),
        P(None, joint, None),
        P(joint, None),
        P(None, joint, None),
        P(None, joint),
        P(),
        P(),
        P(joint),
        P(joint),
        P(joint),
        P(joint),
        P(joint),
        P(),
        P(),
    )
    return jax.shard_map(body, mesh=mesh, in_specs=in_specs, out_specs=out_specs, check_vma=False)
```

```python
import functools

import jax
import jax.numpy as jnp
from jax import lax
from jax.experimental import pallas as pl
from jax.experimental.pallas import tpu as pltpu
from jax.sharding import PartitionSpec as P

F = 128
R = 20
HOPS = 4
ELEMS = 100
STEP = 10
GROUPS = 7

CUTOFF = 5.0
BETA_ONE = 0.9
BETA_TWO = 0.99
RATE = 0.3
DECAY = 0.01
EPSILON = 1e-06

BLOCK = 256
WINDOW = 128
PAIR = 2
LANE_ROWS = 80
SUB = 32
ROWS = 256
F32 = jnp.float32
BF16 = jnp.bfloat16

AT_W1, AT_W2, AT_WF, AT_WM, AT_U1, AT_U2 = 0, 128, 512, 572, 828, 1084
AT_B1, AT_B2, AT_BF, AT_C1, AT_C2, AT_READ, PARAM_ROWS = 1468, 1469, 1472, 1475, 1476, 1479, 1480
PARAM_PAD = PARAM_ROWS + 8
GROUP_ENDS = (128, 512, 572, 828, 1084, 1468)
MESH = pl.DeviceIdType.MESH


def mm(left, right, contract=(1, 0)):
    return lax.dot_general(
        left, right, (((contract[0],), (contract[1],)), ((), ())), preferred_element_type=F32
    )


def split(value):
    high = value.astype(BF16)
    return high, (value - high.astype(F32)).astype(BF16)


def dot3(left, right, contract=(1, 0)):
    return (
        mm(left[0], right[0], contract)
        + mm(left[1], right[0], contract)
        + mm(left[0], right[1], contract)
    )


def sigmoid(value):
    return 1.0 / (1.0 + jnp.exp(-value))


def column(ref, start, parts, j, count=F):
    if parts == 1:
        return ref[start : start + count, :]
    return ref[pl.ds(start + j, count, stride=parts), :]


def add_column(ref, start, parts, j, value, count=F):
    if parts == 1:
        ref[start : start + count, :] += value
    else:
        ref[pl.ds(start + j, count, stride=parts), :] += value


def rows_of(start, count, unit):
    return pl.ds(pl.multiple_of(start, unit), count)


def lay_flat(ref, count):
    return jnp.concatenate([ref[k : k + 1, :] for k in range(count)], axis=1)


def weave(*parts):
    parts = list(parts)
    while parts:
        for part in list(parts):
            try:
                next(part)
            except StopIteration:
                parts.remove(part)


def layer_kernel(
    dst_s,
    count_s,
    src_s,
    crystal,
    dst_v,
    shift_v,
    lat,
    par,
    s_own,
    v_own,
    p_own,
    halo_rows,
    p_halo,
    cot_s,
    cot_v,
    goal,
    s_two,
    v_two,
    gs_own,
    gv_own,
    g_halo,
    gp_own,
    gp_halo,
    gpar,
    tab,
    rows,
    acc,
    stage,
    dtab,
    lane_buf,
    slope_buf,
    inv_buf,
    free_buf,
    turn_buf,
    sums,
    gd,
    gbuf,
    fbuf,
    mbuf,
    ltbuf,
    tbuf,
    wcat,
    wq,
    gwf,
    gpd,
):
    atoms = s_own.shape[0]
    halo = halo_rows.shape[1]
    blocks_128 = shift_v.shape[1] // F
    ends_buf = stage.at[0 : blocks_128 * 16]
    shift_buf = stage.at[blocks_128 * 16 : blocks_128 * 24]
    place_buf = stage.at[blocks_128 * 24 : blocks_128 * 32]
    s_halo, v_halo = halo_rows.at[0], halo_rows.at[1:4]
    gs_halo, gv_halo = g_halo.at[0], g_halo.at[1:4]
    edges = shift_v.shape[1]
    blocks = edges // BLOCK

    wcat[...] = jnp.zeros_like(wcat)
    wq[...] = jnp.zeros_like(wq)
    gwf[...] = jnp.zeros_like(gwf)
    gpd[...] = jnp.zeros_like(gpd)
    gpar[...] = jnp.zeros_like(gpar)
    sums[...] = jnp.zeros_like(sums)
    for j in range(3):
        wide = jnp.concatenate(
            [
                column(par, AT_WF, 3, j, R),
                par[AT_BF + j : AT_BF + j + 1, :],
                jnp.zeros((3, F), F32),
            ],
            axis=0,
        )
        high = wide.astype(BF16).astype(F32)
        low = wide - high
        pieces = jnp.concatenate([high, high, low, jnp.zeros((56, F), F32)], axis=0)
        wcat[:, j * F : (j + 1) * F] = pieces.astype(BF16)
        pieces = jnp.concatenate([high, low, jnp.zeros((80, F), F32)], axis=0)
        wq[j * F : (j + 1) * F, :] = jnp.transpose(pieces).astype(BF16)

    names = lay_flat(crystal, atoms // F)
    spots = lax.broadcasted_iota(jnp.int32, (F, atoms), 0)
    for k in range(atoms // F):
        acc[16 * k : 16 * k + 16, :] = jnp.zeros((16, F), F32)

    @pl.loop(0, lat.shape[1] // F)
    def _(step):
        table = lat[:, rows_of(step * F, F, F)]
        high = table.astype(BF16).astype(F32)
        middle = (table - high).astype(BF16).astype(F32)
        gap = jnp.zeros((7, F), F32)
        pieces = jnp.concatenate([high, gap, middle, gap, table - high - middle, gap], axis=0)
        got = mm(pieces.astype(BF16), jnp.where(names - step * F == spots, 1.0, 0.0).astype(BF16))
        got = got[0:16] + got[16:32] + got[32:48]
        for k in range(atoms // F):
            acc[16 * k : 16 * k + 16, :] += got[:, k * F : (k + 1) * F]

    across = jnp.concatenate([acc[16 * k : 16 * k + 16, :] for k in range(atoms // F)], axis=1)
    part = jnp.concatenate([p_own[...], across[0:9], jnp.zeros((4, atoms), F32)], axis=0)
    high = part.astype(BF16).astype(F32)
    middle = (part - high).astype(BF16).astype(F32)
    low = part - high - middle
    dtab[...] = jnp.concatenate([high, middle, low], axis=0).astype(BF16)

    for s_ref, v_ref, p_ref, base, count in (
        (s_own, v_own, p_own, 0, atoms),
        (s_halo, v_halo, p_halo, atoms, halo),
    ):
        place = jnp.concatenate([p_ref[0:3, :], jnp.zeros((F - 3, count), F32)], axis=0)
        tab[pl.ds(base * 8 + 6, count, stride=8), :] = jnp.transpose(place)
        tab[pl.ds(base * 8 + 7, count, stride=8), :] = jnp.zeros((count, F), F32)
        for c in range(3):
            tab[pl.ds(base * 8 + 3 + c, count, stride=8), :] = v_ref[c]

        @pl.loop(0, count // ROWS)
        def _(step):
            first = step * ROWS
            s_pair = split(s_ref[rows_of(first, ROWS, ROWS), :])
            act = dot3(s_pair, split(column(par, AT_W1, 1, 0))) + par[AT_B1 : AT_B1 + 1, :]
            hidden = split(act * sigmoid(act))
            for j in range(3):
                x = dot3(hidden, split(column(par, AT_W2, 3, j))) + par[AT_B2 + j : AT_B2 + j + 1, :]
                tab[pl.ds((base + first) * 8 + j, ROWS, stride=8), :] = x

    slots = lax.broadcasted_iota(jnp.int32, (WINDOW, BLOCK), 0)
    eight = lax.broadcasted_iota(jnp.int32, (8, 1), 0)
    wide_lane = lax.broadcasted_iota(jnp.int32, (1, F), 1)
    chunks = edges // F
    per = BLOCK // F

    def destinations(i):
        return jnp.concatenate([dst_v[pl.ds(i * per + k, 1), :] for k in range(per)], axis=1)

    def window_range(i):
        return dst_s[i * BLOCK] // WINDOW, dst_s[i * BLOCK + BLOCK - 1] // WINDOW

    def hot(dst, w):
        return jnp.where(dst - w * WINDOW == slots, 1.0, 0.0).astype(BF16)

    def window(w):
        return rows_of(w * WINDOW, WINDOW, WINDOW)

    def lane_chunk(i, k):
        return rows_of((i * per + k) * LANE_ROWS, LANE_ROWS, LANE_ROWS)

    def source(i, j):
        return pl.ds(pl.multiple_of(src_s[i * BLOCK + j], 8), 8)

    def ends_in(i, w):
        got = mm(dtab[:, window(w)], hot(destinations(i), w))
        return got[0:16] + got[16:32] + got[32:48]

    def gather(i):
        for j in range(BLOCK):
            spot = pl.multiple_of(i * (BLOCK * 8), BLOCK * 8) + j * 8
            rows[pl.ds(pl.multiple_of(spot, 8), 8), :] = tab[source(i, j), :]
            if j % 16 == 15:
                yield

    def ends(i):
        got = ends_in(i, window_range(i)[0])
        yield
        for k in range(per):
            chunk = i * per + k
            shift_buf[pl.ds(pl.multiple_of(chunk * 8, 8), 3), :] = shift_v[
                :, rows_of(chunk * F, F, F)
            ].astype(F32)
            ends_buf[rows_of(chunk * 16, 16, 16), :] = got[:, k * F : (k + 1) * F]
            yield

    def places_of(i):
        for k in range(per):
            chunk = i * per + k
            place = rows[pl.ds(chunk * (F * 8) + 6, F, stride=8), :]
            yield
            place_buf[rows_of(chunk * 8, 8, 8), :] = jnp.transpose(place)[0:8]
            yield

    @pl.loop(0, blocks // PAIR)
    def _(step):
        for t in range(PAIR):
            i = step * PAIR + t
            weave(ends(i), places_of(jnp.maximum(i - 1, 0)), gather(i))
            first, last = window_range(i)

            @pl.loop(first + 1, last + 1)
            def _(w):
                more = ends_in(i, w)
                for k in range(per):
                    ends_buf[rows_of((i * per + k) * 16, 16, 16), :] += more[:, k * F : (k + 1) * F]

    weave(places_of(blocks - 1))

    def dense(ref, row, step):
        return ref[pl.ds(row, chunks, stride=step), :]

    def put_row(row, value):
        lane_buf[pl.ds(row, chunks, stride=LANE_ROWS), :] = value

    shift = [dense(shift_buf, k, 8) for k in range(3)]
    rel = [
        dense(place_buf, c, 8)
        + (
            shift[0] * dense(ends_buf, 3 + c, 16)
            + shift[1] * dense(ends_buf, 6 + c, 16)
            + shift[2] * dense(ends_buf, 9 + c, 16)
        )
        - dense(ends_buf, c, 16)
        for c in range(3)
    ]
    square = rel[0] * rel[0] + rel[1] * rel[1] + rel[2] * rel[2]
    dist = jnp.sqrt(jnp.maximum(square, 0.25))
    inv = 1.0 / dist
    inv_buf[...] = inv
    free_buf[...] = jnp.where(square > 0.25, 1.0, 0.0)
    for c in range(3):
        put_row(72 + c, rel[c] * inv)
    put_row(75, dst_v[...].astype(F32))
    nothing = jnp.zeros((chunks, F), F32)
    for row in (21, 22, 23, 45, 46, 47, 69, 70, 71, 76, 77, 78, 79):
        put_row(row, nothing)
    for row in (21, 22, 23):
        slope_buf[pl.ds(row, chunks, stride=24), :] = nothing
    angle = dist * (jnp.pi / CUTOFF)
    sin_one, cos_one = jnp.sin(angle), jnp.cos(angle)
    place = lax.broadcasted_iota(jnp.int32, (chunks, F), 0) * F + lax.broadcasted_iota(
        jnp.int32, (chunks, F), 1
    )
    inside = (dist < CUTOFF) & (place < count_s[0])
    envelope = jnp.where(inside, 0.5 * (cos_one + 1.0), 0.0)
    fall = jnp.where(inside, (-0.5 * jnp.pi / CUTOFF) * sin_one, 0.0)
    sin_n, cos_n = sin_one, cos_one
    for n in range(R + 1):
        if n < R:
            radial = sin_n * inv
            slope = (((n + 1) * jnp.pi / CUTOFF) * cos_n - radial) * inv
            scaled = envelope * radial
            change = fall * radial + envelope * slope
            sin_n, cos_n = sin_n * cos_one + cos_n * sin_one, cos_n * cos_one - sin_n * sin_one
        else:
            scaled, change = envelope, fall
        high = scaled.astype(BF16).astype(F32)
        put_row(n, high)
        put_row(24 + n, scaled - high)
        put_row(48 + n, high)
        slope_buf[pl.ds(n, chunks, stride=24), :] = change

    def comp(i, k, sub):
        return pl.ds(i * (BLOCK * 8) + sub * (SUB * 8) + k, SUB, stride=8)

    def filters(i, t):
        for k in range(per):
            full = jnp.concatenate(
                [lane_buf[lane_chunk(i, k), :], jnp.zeros((F - LANE_ROWS, F), F32)], axis=0
            )
            ltbuf[t, k * F : (k + 1) * F, :] = jnp.transpose(full)
            yield
        fbuf[t] = mm(ltbuf[t].astype(BF16), wcat[...])
        yield

    def messages(i, t):
        for sub in range(BLOCK // SUB):
            at = slice(sub * SUB, (sub + 1) * SUB)
            m1, m2, m3 = [
                rows[comp(i, j, sub), :] * fbuf[t, at, j * F : (j + 1) * F] for j in range(3)
            ]
            out = [m1]
            for c in range(3):
                out.append(m2 * ltbuf[t, at, 72 + c : 73 + c] + m3 * rows[comp(i, 3 + c, sub), :])
            for k in range(4):
                high, low = split(out[k])
                mbuf[t, at, k * F : (k + 1) * F] = high
                mbuf[t, at, (4 + k) * F : (5 + k) * F] = low
            yield

    def collect(i, t, w):
        pick = hot(destinations(i), w)
        for k in range(2):
            of = slice(k * 2 * F, (k + 1) * 2 * F)
            more = slice((k + 2) * 2 * F, (k + 3) * 2 * F)
            sums[window(w), of] += mm(pick, mbuf[t, :, of]) + mm(pick, mbuf[t, :, more])
            yield

    def collect_more(i, t):
        first, last = window_range(i)

        @pl.loop(first + 1, last + 1)
        def _(w):
            weave(collect(i, t, w))

    mbuf[...] = jnp.zeros_like(mbuf)
    weave(filters(0, 0))

    @pl.loop(0, blocks // PAIR)
    def _(step):
        for t in range(PAIR):
            i = step * PAIR + t
            before = jnp.maximum(i - 1, 0)
            weave(
                filters(jnp.minimum(i + 1, blocks - 1), 1 - t),
                collect(before, 1 - t, window_range(before)[0]),
                messages(i, t),
            )
            collect_more(before, 1 - t)

    weave(collect(blocks - 1, PAIR - 1, window_range(blocks - 1)[0]))
    collect_more(blocks - 1, PAIR - 1)

    @pl.loop(0, atoms // ROWS)
    def _(step):
        at = rows_of(step * ROWS, ROWS, ROWS)
        s_one = s_own[at, :] + sums[at, 0:F]
        v_one = [v_own[c, at, :] + sums[at, (c + 1) * F : (c + 2) * F] for c in range(3)]
        wm = [split(column(par, AT_WM, 2, j)) for j in range(2)]
        u1 = [split(par[AT_U1 + j * F : AT_U1 + (j + 1) * F, :]) for j in range(2)]
        u2 = [split(column(par, AT_U2, 3, j)) for j in range(3)]
        v_pair = [split(v) for v in v_one]
        v_lin = [dot3(v, wm[0]) for v in v_pair]
        w_lin = [dot3(v, wm[1]) for v in v_pair]
        size = jnp.sqrt(v_lin[0] * v_lin[0] + v_lin[1] * v_lin[1] + v_lin[2] * v_lin[2] + 1.0)
        s_pair, size_pair = split(s_one), split(size)
        act = dot3(s_pair, u1[0]) + dot3(size_pair, u1[1]) + par[AT_C1 : AT_C1 + 1, :]
        gate = sigmoid(act)
        hidden = split(act * gate)
        a1, a2, a3 = [dot3(hidden, u2[j]) + par[AT_C2 + j : AT_C2 + j + 1, :] for j in range(3)]
        inner = v_lin[0] * w_lin[0] + v_lin[1] * w_lin[1] + v_lin[2] * w_lin[2]
        s_out = s_one + a3 + a2 * inner
        s_two[at, :] = s_out
        read = par[AT_READ : AT_READ + 1, :]
        out_pair = split(s_out)
        energy = dot3(split(jnp.broadcast_to(read, (8, F))), out_pair, (1, 1))
        error = energy - goal[:, at]
        error_col = jnp.transpose(error)[:, 0:1]
        gpar[AT_READ : AT_READ + 1, :] += dot3(split(error), out_pair)[0:1]
        gs = cot_s[at, :] + error_col * read
        gv = []
        for c in range(3):
            v_two[c, at, :] = v_one[c] + a1 * w_lin[c]
            gv.append(cot_v[c, at, :])
        ga = [gv[0] * w_lin[0] + gv[1] * w_lin[1] + gv[2] * w_lin[2], gs * inner, gs]
        g_inner = gs * a2
        ga_pair = [split(g) for g in ga]
        for j in range(3):
            add_column(gpar, AT_U2, 3, j, dot3(hidden, ga_pair[j], (0, 0)))
            gpar[AT_C2 + j : AT_C2 + j + 1, :] += jnp.sum(ga[j], axis=0, keepdims=True)
        g_hidden = (
            dot3(ga_pair[0], u2[0], (1, 1))
            + dot3(ga_pair[1], u2[1], (1, 1))
            + dot3(ga_pair[2], u2[2], (1, 1))
        )
        g_act = g_hidden * (gate * (1.0 + act * (1.0 - gate)))
        g_act_pair = split(g_act)
        add_column(gpar, AT_U1, 1, 0, dot3(s_pair, g_act_pair, (0, 0)))
        add_column(gpar, AT_U1 + F, 1, 0, dot3(size_pair, g_act_pair, (0, 0)))
        gpar[AT_C1 : AT_C1 + 1, :] += jnp.sum(g_act, axis=0, keepdims=True)
        g_s_one = gs + dot3(g_act_pair, u1[0], (1, 1))
        g_size = dot3(g_act_pair, u1[1], (1, 1)) / size
        gs_own[at, :] = g_s_one
        down = [g_s_one]
        for c in range(3):
            g_w = split(a1 * gv[c] + g_inner * v_lin[c])
            g_v = split(g_inner * w_lin[c] + g_size * v_lin[c])
            add_column(gpar, AT_WM, 2, 0, dot3(v_pair[c], g_v, (0, 0)))
            add_column(gpar, AT_WM, 2, 1, dot3(v_pair[c], g_w, (0, 0)))
            g_v_one = gv[c] + dot3(g_v, wm[0], (1, 1)) + dot3(g_w, wm[1], (1, 1))
            gv_own[c, at, :] = g_v_one
            down.append(g_v_one)
        for k in range(4):
            high, low = split(down[k])
            for part in range(ROWS // WINDOW):
                to = (step * (ROWS // WINDOW) + part) * (2 * WINDOW)
                of = slice(part * WINDOW, (part + 1) * WINDOW)
                gd[rows_of(to, WINDOW, WINDOW), k * F : (k + 1) * F] = high[of]
                gd[rows_of(to + WINDOW, WINDOW, WINDOW), k * F : (k + 1) * F] = low[of]

    twice = (lax.broadcasted_iota(jnp.int32, (1, 2 * WINDOW), 1) % WINDOW).astype(F32)
    for ref in (tab, acc, stage, mbuf, tbuf, turn_buf):
        ref[...] = jnp.zeros_like(ref)

    def collect_places(i, t, w):
        g_rel = turn_buf[t]
        high = g_rel.astype(BF16).astype(F32)
        middle = (g_rel - high).astype(BF16).astype(F32)
        pieces = jnp.concatenate(
            [high, middle, g_rel - high - middle, jnp.zeros_like(g_rel)], axis=0
        )
        got = mm(pieces.astype(BF16), hot(destinations(i), w), (1, 1))
        gpd[:, window(w)] += got[0:8] + got[8:16] + got[16:24]

    def fetch(t, w):
        near = ltbuf[t, :, 75:76] - (w * WINDOW).astype(F32)
        return mm(
            jnp.where(near == twice, 1.0, 0.0).astype(BF16),
            gd[rows_of(w * 2 * WINDOW, 2 * WINDOW, 2 * WINDOW), :],
        )

    def prepare(i, t):
        yield from filters(i, t)
        gbuf[t] = fetch(t, window_range(i)[0])
        yield

    def spread(i, t, earlier):
        for sub in range(BLOCK // SUB):
            at = slice(sub * SUB, (sub + 1) * SUB)
            for j in range(SUB // 2):
                for k, total in enumerate((tab, acc)):
                    spot = sub * SUB + k * (SUB // 2) + j
                    held = (t * BLOCK + spot) * 8
                    total[source(earlier, spot), :] += stage[held : held + 8, :]
                if j % 8 == 7:
                    yield
            to = [pl.ds(t * (BLOCK * 8) + sub * (SUB * 8) + k, SUB, stride=8) for k in range(6)]
            g_s = gbuf[t, at, 0:F]
            g_v = [gbuf[t, at, (c + 1) * F : (c + 2) * F] for c in range(3)]
            x = [rows[comp(i, j, sub), :] for j in range(3)]
            v = [rows[comp(i, 3 + c, sub), :] for c in range(3)]
            f = [fbuf[t, at, j * F : (j + 1) * F] for j in range(3)]
            u = [ltbuf[t, at, 72 + c : 73 + c] for c in range(3)]
            g_m = [
                g_s,
                g_v[0] * u[0] + g_v[1] * u[1] + g_v[2] * u[2],
                g_v[0] * v[0] + g_v[1] * v[1] + g_v[2] * v[2],
            ]
            m2 = x[1] * f[1]
            m3 = x[2] * f[2]
            turn = jnp.zeros((SUB, F), F32)
            for c in range(3):
                total = jnp.sum(g_v[c] * m2, axis=1, keepdims=True)
                turn = jnp.where(wide_lane == 48 + c, total, turn)
                stage[to[3 + c], :] = g_v[c] * m3
            tbuf[t, at, :] = turn
            for j in range(3):
                high, low = split(g_m[j] * x[j])
                mbuf[t, at, j * F : (j + 1) * F] = high
                mbuf[t, at, (3 + j) * F : (4 + j) * F] = low
                stage[to[j], :] = g_m[j] * f[j]
            yield

    def settle(i, t):
        h_high, h_low = mbuf[t, :, : 3 * F], mbuf[t, :, 3 * F : 6 * F]
        back = mm(h_high, wq[...]) + mm(h_low, wq[...]) + tbuf[t]
        yield
        back = jnp.transpose(back)
        yield
        pieces = jnp.concatenate(
            [lane_buf[lane_chunk(i, k), :][0:48] for k in range(per)], axis=1
        ).astype(BF16)
        gwf[...] += mm(pieces, h_high) + mm(pieces, h_low)
        yield
        slope = jnp.concatenate(
            [slope_buf[rows_of((i * per + k) * 24, 24, 24), :] for k in range(per)], axis=1
        )
        g_dist = jnp.sum((back[0:24] + back[24:48]) * slope, axis=0, keepdims=True)
        g_unit = back[48:56]
        unit = jnp.concatenate([lane_buf[lane_chunk(i, k), :][72:80] for k in range(per)], axis=1)
        unit = jnp.where(eight < 3, unit, 0.0)
        inv, free = [
            jnp.concatenate([ref[pl.ds(i * per + k, 1), :] for k in range(per)], axis=1)
            for ref in (inv_buf, free_buf)
        ]
        yield
        along = jnp.sum(g_unit * unit, axis=0, keepdims=True)
        g_rel = g_unit * inv + (g_dist - along * inv) * free * unit
        turn_buf[t] = g_rel
        yield
        stage[pl.ds(t * (BLOCK * 8) + 6, BLOCK, stride=8), :] = jnp.transpose(
            jnp.concatenate([g_rel, jnp.zeros((F - 8, BLOCK), F32)], axis=0)
        )
        yield
        collect_places(i, t, window_range(i)[0])
        yield

    def prepare_more(i, t):
        first, last = window_range(i)

        @pl.loop(first + 1, last + 1)
        def _(w):
            gbuf[t] += fetch(t, w)

    def settle_more(i, t):
        first, last = window_range(i)

        @pl.loop(first + 1, last + 1)
        def _(w):
            collect_places(i, t, w)

    weave(prepare(0, 0))
    prepare_more(0, 0)

    @pl.loop(0, blocks // PAIR)
    def _(step):
        for t in range(PAIR):
            i = step * PAIR + t
            before, after = jnp.maximum(i - 1, 0), jnp.minimum(i + 1, blocks - 1)
            weave(spread(i, t, jnp.maximum(i - 2, 0)), settle(before, 1 - t), prepare(after, 1 - t))
            prepare_more(after, 1 - t)
            settle_more(before, 1 - t)

    weave(settle(blocks - 1, PAIR - 1))
    settle_more(blocks - 1, PAIR - 1)
    for t in range(PAIR):
        for j in range(BLOCK // 2):
            for k, total in enumerate((tab, acc)):
                spot = k * (BLOCK // 2) + j
                held = (t * BLOCK + spot) * 8
                total[source(blocks - PAIR + t, spot), :] += stage[held : held + 8, :]

    for j in range(3):
        total = gwf[0:24, j * F : (j + 1) * F] + gwf[24:48, j * F : (j + 1) * F]
        add_column(gpar, AT_WF, 3, j, total[0:R], R)
        gpar[AT_BF + j : AT_BF + j + 1, :] = total[R : R + 1]

    for s_ref, gs_ref, gv_ref, gp_ref, base, count in (
        (s_own, gs_own, gv_own, gp_own, 0, atoms),
        (s_halo, gs_halo, gv_halo, gp_halo, atoms, halo),
    ):
        own = base == 0
        for k in range(0, count, ROWS):
            at = pl.ds((base + k) * 8 + 6, ROWS, stride=8)
            place = jnp.transpose(tab[at, :] + acc[at, :])[0:8]
            if own:
                place = place - gpd[:, k : k + ROWS]
            gp_ref[:, k : k + ROWS] = place

        @pl.loop(0, count // ROWS)
        def _(step):
            first = step * ROWS
            to = rows_of(first, ROWS, ROWS)

            def gathered(k):
                at = pl.ds((base + first) * 8 + k, ROWS, stride=8)
                return tab[at, :] + acc[at, :]

            for c in range(3):
                if own:
                    gv_ref[c, to, :] += gathered(3 + c)
                else:
                    gv_ref[c, to, :] = gathered(3 + c)
            w1 = split(column(par, AT_W1, 1, 0))
            s_pair = split(s_ref[to, :])
            act = dot3(s_pair, w1) + par[AT_B1 : AT_B1 + 1, :]
            gate = sigmoid(act)
            hidden = split(act * gate)
            g_hidden = jnp.zeros((ROWS, F), F32)
            for j in range(3):
                g_x = gathered(j)
                g_pair = split(g_x)
                add_column(gpar, AT_W2, 3, j, dot3(hidden, g_pair, (0, 0)))
                gpar[AT_B2 + j : AT_B2 + j + 1, :] += jnp.sum(g_x, axis=0, keepdims=True)
                g_hidden = g_hidden + dot3(g_pair, split(column(par, AT_W2, 3, j)), (1, 1))
            g_act = g_hidden * (gate * (1.0 + act * (1.0 - gate)))
            g_act_pair = split(g_act)
            add_column(gpar, AT_W1, 1, 0, dot3(s_pair, g_act_pair, (0, 0)))
            gpar[AT_B1 : AT_B1 + 1, :] += jnp.sum(g_act, axis=0, keepdims=True)
            g_s = dot3(g_act_pair, w1, (1, 1))
            if own:
                gs_ref[to, :] += g_s
            else:
                gs_ref[to, :] = g_s


def layer(atoms, halo, edges):
    shape = jax.ShapeDtypeStruct
    total = atoms + halo
    in_vmem = pl.BlockSpec(memory_space=pltpu.VMEM)
    in_smem = pl.BlockSpec(memory_space=pltpu.SMEM)
    outs = (
        shape((atoms, F), F32),
        shape((3, atoms, F), F32),
        shape((atoms, F), F32),
        shape((3, atoms, F), F32),
        shape((4, halo, F), F32),
        shape((8, atoms), F32),
        shape((8, halo), F32),
        shape((PARAM_PAD, F), F32),
    )
    scratch = [
        pltpu.VMEM((total * 8, F), F32),
        pltpu.VMEM((edges * 8, F), F32),
        pltpu.VMEM((total * 8, F), F32),
        pltpu.VMEM((PAIR * BLOCK * 8, F), F32),
        pltpu.VMEM((48, atoms), BF16),
        pltpu.VMEM((edges // F * LANE_ROWS, F), F32),
        pltpu.VMEM((edges // F * 24, F), F32),
        pltpu.VMEM((edges // F, F), F32),
        pltpu.VMEM((edges // F, F), F32),
        pltpu.VMEM((PAIR, 8, BLOCK), F32),
        pltpu.VMEM((atoms, 4 * F), F32),
        pltpu.VMEM((2 * atoms, 4 * F), BF16),
        pltpu.VMEM((PAIR, BLOCK, 4 * F), F32),
        pltpu.VMEM((PAIR, BLOCK, 3 * F), F32),
        pltpu.VMEM((PAIR, BLOCK, 8 * F), BF16),
        pltpu.VMEM((PAIR, BLOCK, F), F32),
        pltpu.VMEM((PAIR, BLOCK, F), F32),
        pltpu.VMEM((F, 3 * F), BF16),
        pltpu.VMEM((3 * F, F), BF16),
        pltpu.VMEM((48, 3 * F), F32),
        pltpu.VMEM((8, atoms), F32),
    ]
    return pl.pallas_call(
        layer_kernel,
        out_shape=outs,
        in_specs=[in_smem] * 3 + [in_vmem] * 13,
        out_specs=(in_vmem,) * len(outs),
        scratch_shapes=scratch,
        compiler_params=pltpu.CompilerParams(vmem_limit_bytes=62 * 1024 * 1024),
        name="layer",
    )


def hop_offset(j):
    return j + 1 if j < HOPS else HOPS - 1 - j


class Place:
    def __init__(self):
        self.chips = lax.axis_size("atoms")
        self.cores = lax.axis_size("rep")
        self.count = self.chips * self.cores
        self.groups = self.chips // 4
        chip = lax.axis_index("atoms")
        self.core = lax.axis_index("rep")
        self.joint = chip * self.cores + self.core
        self.group = chip // 4
        self.quarter = chip % 4
        self.mate = 1 - self.core

    def other_groups(self):
        return [lax.rem(self.group + k, self.groups) for k in range(1, self.groups)]

    def other_quarters(self):
        return [lax.rem(self.quarter + k, 4) for k in range(1, 4)]

    def in_group(self, group):
        return (group * 4 + self.quarter, self.core)

    def in_quarter(self, quarter):
        return (self.group * 4 + quarter, self.core)

    def beside(self):
        return (self.group * 4 + self.quarter, self.mate)

    def hop(self, by):
        other = self.joint + by
        exists = (other >= 0) & (other < self.count)
        other = jnp.clip(other, 0, self.count - 1)
        return exists, (other // self.cores, other % self.cores)

    def others_of_group(self):
        own = self.quarter * self.cores + self.core
        places = [lax.rem(own + k, 4 * self.cores) for k in range(1, 4 * self.cores)]
        return [(o, (self.group * 4 + o // self.cores, o % self.cores)) for o in places]

    def greet(self):
        barrier = pltpu.get_barrier_semaphore()
        fixed = [self.in_group(g) for g in self.other_groups()]
        fixed += [device for _, device in self.others_of_group()]
        for device in fixed:
            pl.semaphore_signal(barrier, inc=1, device_id=device, device_id_type=MESH)
        hops = [self.hop(hop_offset(j)) for j in range(2 * HOPS)]
        expected = jnp.int32(len(fixed))
        for exists, device in hops:
            expected = expected + jnp.where(exists, 1, 0)

            @pl.when(exists)
            def _():
                pl.semaphore_signal(barrier, inc=1, device_id=device, device_id_type=MESH)

        return expected


def send(src, dst, send_sem, recv_sem, device):
    return pltpu.make_async_remote_copy(
        src_ref=src,
        dst_ref=dst,
        send_sem=send_sem,
        recv_sem=recv_sem,
        device_id=device,
        device_id_type=MESH,
    )


def start_all(copies):
    for copy in copies:
        copy.start()
    return copies


def wait_sent(copies):
    for copy in copies:
        copy.wait_send()


def window_rows(length):
    return -(-((length + F - 1) // F + 1) // 8) * 8


class SmallSum:
    def __init__(self, place, slots_a, slots_b, sends, recvs):
        self.place = place
        self.slots = (slots_a, slots_b)
        self.sends, self.recvs = sends, recvs
        self.sent = []

    def partners(self, phase):
        p = self.place
        if phase == 0:
            return p.quarter * p.cores + p.core, p.others_of_group(), 0
        return p.group, [(g, p.in_group(g)) for g in p.other_groups()], 4 * p.cores

    def start(self, phase, value):
        slots = self.slots[phase]
        mine, others, base = self.partners(phase)
        slots[mine] = value
        for k, (_, device) in enumerate(others):
            spot = slots.at[mine]
            copy = send(spot, spot, self.sends.at[base + k], self.recvs.at[base + mine], device)
            copy.start()
            self.sent.append(copy)

    def finish(self, phase):
        slots = self.slots[phase]
        _, others, base = self.partners(phase)
        for o, device in others:
            spot = slots.at[o]
            send(spot, spot, self.sends.at[base], self.recvs.at[base + o], device).wait_recv()
        total = slots[0]
        for k in range(1, slots.shape[0]):
            total = total + slots[k]
        return total

    def done(self):
        wait_sent(self.sent)


def small_scratch(groups, rows):
    count = groups + 8
    return [
        pltpu.VMEM((8, rows, F), F32),
        pltpu.VMEM((groups, rows, F), F32),
        pltpu.SemaphoreType.DMA((count,)),
        pltpu.SemaphoreType.DMA((count,)),
    ]


def from_flat(ref, rows):
    length = ref.shape[0]
    whole, rest = length // F, length % F
    lines = [ref[pl.ds(r * F, F)].reshape(1, F) for r in range(whole)]
    if rest:
        last = ref[pl.ds(whole * F, rest)].reshape(1, rest)
        lines.append(jnp.concatenate([last, jnp.zeros((1, F - rest), F32)], axis=1))
    lines.append(jnp.zeros((rows - len(lines), F), F32))
    return jnp.concatenate(lines, axis=0)


def to_flat(ref, value):
    length = ref.shape[0]
    whole, rest = length // F, length % F
    for r in range(whole):
        ref[pl.ds(r * F, F)] = value[r]
    if rest:
        ref[pl.ds(whole * F, rest)] = value[whole, :rest]


def gather_kernel(
    send_s,
    par_in,
    s_own,
    v_own,
    p_own,
    energy,
    elements,
    forces,
    edge_src,
    par,
    halo_rows,
    p_halo,
    goal,
    stats,
    src_tiles,
    slots,
    pack,
    places,
    p_out,
    p_in,
    zeros,
    ag_send,
    ag_recv,
    row_send,
    row_recv,
    place_send,
    place_recv,
    zero_sem,
    *small,
    length,
):
    here = Place()
    atoms = s_own.shape[0]
    cap = halo_rows.shape[1] // (2 * HOPS)
    wide = slots.shape[3]
    expected = here.greet()
    sums = SmallSum(here, *small)

    offset = lax.rem(here.joint * length, F)
    lane = lax.broadcasted_iota(jnp.int32, (1, F), 1)
    turned = pltpu.roll(from_flat(par_in, wide), offset, 1)
    above = jnp.concatenate([jnp.zeros((1, F), F32), turned[: wide - 1]], axis=0)
    mine = slots.at[here.group, here.quarter, here.core]
    mine[...] = jnp.where(lane < offset, above, turned)
    src_tiles[...] = edge_src[...] * 8

    count = atoms // F
    energy_row, element_row = lay_flat(energy, count), lay_flat(elements, count)
    hot = jnp.where(
        element_row == lax.broadcasted_iota(jnp.int32, (F, atoms), 0), 1.0, 0.0
    ).astype(BF16)
    high = energy_row.astype(BF16).astype(F32)
    middle = (energy_row - high).astype(BF16).astype(F32)
    eight = lax.broadcasted_iota(jnp.int32, (8, 1), 0)
    left = jnp.where(
        eight == 0,
        high,
        jnp.where(
            eight == 1, middle, jnp.where(eight == 2, energy_row - high - middle, jnp.where(eight == 3, 1.0, 0.0))
        ),
    )
    found = mm(left.astype(BF16), hot, (1, 1))
    squares = jnp.sum(forces[...] * forces[...], axis=0, keepdims=True)
    square = squares[:, 0:F]
    for k in range(1, count):
        square = square + squares[:, k * F : (k + 1) * F]
    tile = jnp.where(
        eight == 0,
        found[0:1] + found[1:2] + found[2:3],
        jnp.where(eight == 1, found[3:4], jnp.where(eight == 2, square, 0.0)),
    )
    places[...] = jnp.transpose(
        jnp.concatenate([p_own[...], jnp.zeros((F - 3, atoms), F32)], axis=0)
    )
    zeros[...] = jnp.zeros_like(zeros)
    hops = range(2 * HOPS)
    for j in hops:

        @pl.loop(0, cap // 16)
        def _(step):
            for k in range(16):
                r = step * 16 + k
                t = send_s[0, j, r]
                r = j * cap + r
                pack[0, pl.ds(r, 1), :] = s_own[pl.ds(t, 1), :]
                for c in range(3):
                    pack[1 + c, pl.ds(r, 1), :] = v_own[c, pl.ds(t, 1), :]
                p_out[pl.ds(r, 1), :] = places[pl.ds(t, 1), :]

    for j in range(0, 2 * HOPS, 2):
        pair = slice(j * cap, (j + 2) * cap)
        p_in[2 * HOPS + j // 2] = jnp.transpose(p_out[pair, :])[0:8]

    pl.semaphore_wait(pltpu.get_barrier_semaphore(), expected)
    first = start_all(
        [
            send(mine, mine, ag_send.at[k], ag_recv.at[here.group], here.in_group(g))
            for k, g in enumerate(here.other_groups())
        ]
    )
    sums.start(0, tile)
    row_copies, place_copies = [], []
    for j in hops:
        exists, device = here.hop(hop_offset(j))
        block = pl.ds(j * cap, cap)
        rows_copy = send(
            pack.at[:, block], halo_rows.at[:, block], row_send.at[j], row_recv.at[j], device
        )
        place_copy = send(
            p_in.at[2 * HOPS + j // 2], p_in.at[j], place_send.at[j], place_recv.at[j], device
        )
        row_copies.append((exists, rows_copy))
        place_copies.append((exists, place_copy))

        @pl.when(exists)
        def _():
            rows_copy.start()
            place_copy.start()

    for j in hops:
        known, device = here.hop(-hop_offset(j))

        @pl.when(jnp.logical_not(known))
        def _():
            p_in[j] = jnp.zeros((8, F), F32)
            fill = pltpu.make_async_copy(
                zeros, halo_rows.at[:, pl.ds(j * cap, cap)], zero_sem.at[j]
            )
            fill.start()
            fill.wait()

    for g in here.other_groups():
        spot = slots.at[g, here.quarter, here.core]
        send(spot, spot, ag_send.at[0], ag_recv.at[g], here.beside()).wait_recv()
    base = here.groups
    line = slots.at[:, here.quarter, here.core]
    second = start_all(
        [
            send(line, line, ag_send.at[base + k], ag_recv.at[base + here.quarter], here.in_quarter(q))
            for k, q in enumerate(here.other_quarters())
        ]
    )
    third = [
        send(
            line, line, ag_send.at[base + 4], ag_recv.at[base + 4 + here.quarter], here.beside()
        )
    ]
    third[0].start()
    sums.start(1, sums.finish(0))
    for k, q in enumerate(here.other_quarters()):
        line = slots.at[:, q, here.core]
        send(line, line, ag_send.at[0], ag_recv.at[base + q], here.beside()).wait_recv()
        copy = send(
            line, line, ag_send.at[base + 5 + k], ag_recv.at[base + 4 + q], here.beside()
        )
        copy.start()
        third.append(copy)
    for q in range(4):
        line = slots.at[:, q, here.mate]
        send(line, line, ag_send.at[0], ag_recv.at[base + 4 + q], here.beside()).wait_recv()

    par[...] = jnp.zeros_like(par)
    for p in range(here.count):
        row = p * length // F
        chip, core = p // here.cores, p % here.cores
        take = min(wide, PARAM_PAD - row)
        par[row : row + take, :] += slots[chip // 4, chip % 4, core, 0:take, :]

    total = sums.finish(1)
    mean = total[0:1] / jnp.maximum(total[1:2], 1.0)
    whole = jnp.sum(total[2:3], axis=1, keepdims=True)
    scale = jnp.sqrt(whole / (3.0 * atoms * here.count) + 1e-06)
    high = mean.astype(BF16).astype(F32)
    middle = (mean - high).astype(BF16).astype(F32)
    left = jnp.where(
        eight == 0,
        high,
        jnp.where(eight == 1, middle, jnp.where(eight == 2, mean - high - middle, 0.0)),
    )
    found = mm(left.astype(BF16), hot)
    goal[...] = (energy_row - (found[0:1] + found[1:2] + found[2:3])) / scale
    stats[...] = jnp.where(eight == 0, mean, jnp.where(eight == 1, scale, 0.0))

    for j in hops:
        known, device = here.hop(-hop_offset(j))

        @pl.when(known)
        def _():
            block = pl.ds(j * cap, cap)
            send(
                pack.at[:, block], halo_rows.at[:, block], row_send.at[j], row_recv.at[j], device
            ).wait_recv()
            send(p_in.at[j], p_in.at[j], place_send.at[j], place_recv.at[j], device).wait_recv()

    low_half = lane < cap
    for j in range(0, 2 * HOPS, 2):
        p_halo[:, j * cap : (j + 2) * cap] = jnp.where(low_half, p_in[j], p_in[j + 1])
    for exists, copy in row_copies + place_copies:

        @pl.when(exists)
        def _():
            copy.wait_send()

    wait_sent(first + second + third)
    sums.done()


def gather_all(atoms, cap, groups, length, edges):
    shape = jax.ShapeDtypeStruct
    halo = 2 * HOPS * cap
    wide = window_rows(length)
    in_vmem = pl.BlockSpec(memory_space=pltpu.VMEM)
    in_smem = pl.BlockSpec(memory_space=pltpu.SMEM)
    return pl.pallas_call(
        functools.partial(gather_kernel, length=length),
        out_shape=(
            shape((PARAM_PAD, F), F32),
            shape((4, halo, F), F32),
            shape((8, halo), F32),
            shape((1, atoms), F32),
            shape((8, F), F32),
            shape((edges // F, F), jnp.int32),
        ),
        in_specs=[in_smem] + [in_vmem] * 8,
        out_specs=(in_vmem, pl.BlockSpec(memory_space=pl.ANY)) + (in_vmem,) * 4,
        scratch_shapes=[
            pltpu.VMEM((groups, 4, 2, wide, F), F32),
            pltpu.VMEM((4, halo, F), F32),
            pltpu.VMEM((atoms, F), F32),
            pltpu.VMEM((halo, F), F32),
            pltpu.VMEM((3 * HOPS, 8, F), F32),
            pltpu.VMEM((4, cap, F), F32),
            pltpu.SemaphoreType.DMA((groups + 8,)),
            pltpu.SemaphoreType.DMA((groups + 8,)),
            pltpu.SemaphoreType.DMA((2 * HOPS,)),
            pltpu.SemaphoreType.DMA((2 * HOPS,)),
            pltpu.SemaphoreType.DMA((2 * HOPS,)),
            pltpu.SemaphoreType.DMA((2 * HOPS,)),
            pltpu.SemaphoreType.DMA((2 * HOPS,)),
        ]
        + small_scratch(groups, 8),
        compiler_params=pltpu.CompilerParams(
            collective_id=0, has_side_effects=True, vmem_limit_bytes=62 * 1024 * 1024
        ),
        name="gather_inputs",
    )


def reduce_kernel(
    gpar,
    g_halo,
    gp_halo,
    par,
    one,
    two,
    back,
    p_back,
    shares,
    norms,
    slots,
    pair_in,
    line_in,
    spot_in,
    turn,
    zeros,
    p_in,
    rs_send,
    rs_recv,
    row_send,
    row_recv,
    place_send,
    place_recv,
    zero_sem,
    *small,
    length,
):
    here = Place()
    cap = back.shape[1] // (2 * HOPS)
    wide = slots.shape[3]
    expected = here.greet()
    sums = SmallSum(here, *small)

    for p in range(here.count):
        row = p * length // F
        chip, core = p // here.cores, p % here.cores
        take = min(wide, PARAM_PAD - row)
        slots[chip // 4, chip % 4, core, 0:take, :] = gpar[row : row + take, :]
    old, m_one, m_two = [from_flat(ref, wide) for ref in (par, one, two)]
    zeros[...] = jnp.zeros_like(zeros)
    order = here.other_quarters() + [here.quarter]
    base = here.groups
    pl.semaphore_wait(pltpu.get_barrier_semaphore(), expected)
    third = start_all(
        [
            send(
                slots.at[:, q, here.mate],
                pair_in.at[:, q],
                rs_send.at[base + 4 + k],
                rs_recv.at[base + 4 + q],
                here.beside(),
            )
            for k, q in enumerate(order)
        ]
    )

    second = []
    for k, q in enumerate(order):
        line = pair_in.at[:, q]
        send(line, line, rs_send.at[0], rs_recv.at[base + 4 + q], here.beside()).wait_recv()
        slots[:, q, here.core] += pair_in[:, q]
        if k < 3:
            copy = send(
                slots.at[:, q, here.core],
                line_in.at[here.quarter],
                rs_send.at[base + k],
                rs_recv.at[base + here.quarter],
                here.in_quarter(q),
            )
            copy.start()
            second.append(copy)

    hops = range(2 * HOPS)
    copies = []
    for j in hops:
        exists, device = here.hop(-hop_offset(j))
        block = pl.ds(j * cap, cap)
        tile = pl.ds((j // 2) * F, F)
        rows_copy = send(
            g_halo.at[:, block], back.at[:, block], row_send.at[j], row_recv.at[j], device
        )
        place_copy = send(
            gp_halo.at[:, tile], p_in.at[j], place_send.at[j], place_recv.at[j], device
        )
        copies += [(exists, rows_copy), (exists, place_copy)]

        @pl.when(exists)
        def _():
            rows_copy.start()
            place_copy.start()

    for j in hops:
        known, device = here.hop(hop_offset(j))

        @pl.when(jnp.logical_not(known))
        def _():
            p_in[j] = jnp.zeros((8, F), F32)
            fill = pltpu.make_async_copy(zeros, back.at[:, pl.ds(j * cap, cap)], zero_sem.at[j])
            fill.start()
            fill.wait()

    for q in here.other_quarters():
        line = line_in.at[q]
        send(line, line, rs_send.at[0], rs_recv.at[base + q], here.beside()).wait_recv()
        slots[:, here.quarter, here.core] += line_in[q]
    first = start_all(
        [
            send(
                slots.at[g, here.quarter, here.core],
                spot_in.at[here.group],
                rs_send.at[k],
                rs_recv.at[here.group],
                here.in_group(g),
            )
            for k, g in enumerate(here.other_groups())
        ]
    )
    total = slots[here.group, here.quarter, here.core]
    for g in here.other_groups():
        spot = spot_in.at[g]
        send(spot, spot, rs_send.at[0], rs_recv.at[g], here.beside()).wait_recv()
        total = total + spot_in[g]

    offset = lax.rem(here.joint * length, F)
    lane = lax.broadcasted_iota(jnp.int32, (1, F), 1)
    turn[0:wide, :] = pltpu.roll(total, lax.rem(F - offset, F), 1)
    turn[wide : wide + 8, :] = jnp.zeros((8, F), F32)
    place = lax.broadcasted_iota(jnp.int32, (wide, F), 0) * F + lane
    inside = place < length
    g = jnp.where(lane + offset < F, turn[0:wide, :], turn[1 : wide + 1, :])
    g = jnp.where(inside, g, 0.0)
    shares[0] = g
    m_one = BETA_ONE * m_one + (1.0 - BETA_ONE) * g
    m_two = BETA_TWO * m_two + (1.0 - BETA_TWO) * g * g
    shares[1] = m_one
    shares[2] = m_two
    direction = (
        m_one
        / (1.0 - BETA_ONE**STEP)
        / (jnp.sqrt(m_two / (1.0 - BETA_TWO**STEP)) + EPSILON)
        + DECAY * old
    )
    spot = place + here.joint * length
    label = jnp.zeros((wide, F), jnp.int32)
    for end in GROUP_ENDS:
        label = label + jnp.where(spot >= end * F, 1, 0)
    label = jnp.where(inside, label, GROUPS)
    lines = []
    for value in (old, direction):
        square = value * value
        lines += [
            jnp.sum(jnp.where(label == k, square, 0.0), axis=0, keepdims=True)
            for k in range(GROUPS)
        ]
        lines.append(jnp.zeros((1, F), F32))
    sums.start(0, jnp.concatenate(lines, axis=0))
    sums.start(1, sums.finish(0))
    whole = jnp.sqrt(jnp.sum(sums.finish(1), axis=1, keepdims=True))
    ratio = whole[0:8] / whole[8:16]
    norms[...] = jnp.broadcast_to(whole, (16, F))
    trust = jnp.zeros((wide, F), F32)
    for k in range(GROUPS):
        trust = jnp.where(label == k, ratio[k : k + 1], trust)
    shares[3] = old - RATE * trust * direction

    for j in hops:
        known, device = here.hop(hop_offset(j))

        @pl.when(known)
        def _():
            block = pl.ds(j * cap, cap)
            tile = p_in.at[j]
            send(
                back.at[:, block], back.at[:, block], row_send.at[j], row_recv.at[j], device
            ).wait_recv()
            send(tile, tile, place_send.at[j], place_recv.at[j], device).wait_recv()

    low_half = lane < cap
    for j in range(0, 2 * HOPS, 2):
        p_back[:, j * cap : (j + 2) * cap] = jnp.where(low_half, p_in[j], p_in[j + 1])
    for exists, copy in copies:

        @pl.when(exists)
        def _():
            copy.wait_send()

    wait_sent(first + second + third)
    sums.done()


def reduce_all(cap, groups, length):
    shape = jax.ShapeDtypeStruct
    halo = 2 * HOPS * cap
    wide = window_rows(length)
    in_vmem = pl.BlockSpec(memory_space=pltpu.VMEM)
    in_any = pl.BlockSpec(memory_space=pl.ANY)
    return pl.pallas_call(
        functools.partial(reduce_kernel, length=length),
        out_shape=(
            shape((4, halo, F), F32),
            shape((8, halo), F32),
            shape((4, wide, F), F32),
            shape((16, F), F32),
        ),
        in_specs=[in_vmem, in_any] + [in_vmem] * 4,
        out_specs=(in_any, in_vmem, in_vmem, in_vmem),
        scratch_shapes=[
            pltpu.VMEM((groups, 4, 2, wide, F), F32),
            pltpu.VMEM((groups, 4, wide, F), F32),
            pltpu.VMEM((4, groups, wide, F), F32),
            pltpu.VMEM((groups, wide, F), F32),
            pltpu.VMEM((wide + 8, F), F32),
            pltpu.VMEM((4, cap, F), F32),
            pltpu.VMEM((2 * HOPS, 8, F), F32),
            pltpu.SemaphoreType.DMA((groups + 8,)),
            pltpu.SemaphoreType.DMA((groups + 8,)),
            pltpu.SemaphoreType.DMA((2 * HOPS,)),
            pltpu.SemaphoreType.DMA((2 * HOPS,)),
            pltpu.SemaphoreType.DMA((2 * HOPS,)),
            pltpu.SemaphoreType.DMA((2 * HOPS,)),
            pltpu.SemaphoreType.DMA((2 * HOPS,)),
        ]
        + small_scratch(groups, 16),
        compiler_params=pltpu.CompilerParams(
            collective_id=1, has_side_effects=True, vmem_limit_bytes=62 * 1024 * 1024
        ),
        name="reduce_outputs",
    )


def finish_kernel(
    back,
    p_back,
    shares,
    norms,
    stats,
    send_rows,
    gs_own,
    gv_own,
    gp_own,
    grad_s,
    grad_v,
    grad_p,
    elem_mean,
    scale,
    grad,
    one_new,
    two_new,
    par_new,
    par_low,
    weight_norms,
    update_norms,
):
    atoms = gs_own.shape[0]
    halo = back.shape[1]
    pick = jnp.concatenate([send_rows[0, j : j + 1, :] for j in range(2 * HOPS)], axis=1)
    hot = jnp.where(pick == lax.broadcasted_iota(jnp.int32, (atoms, halo), 0), 1.0, 0.0)
    hot = hot.astype(BF16)
    for k in range(4):
        high, low = split(back[k])
        extra = mm(hot, high) + mm(hot, low)
        if k == 0:
            grad_s[...] = gs_own[...] + extra
        else:
            grad_v[k - 1] = gv_own[k - 1] + extra
    place = p_back[...]
    high = place.astype(BF16).astype(F32)
    middle = (place - high).astype(BF16).astype(F32)
    pieces = jnp.concatenate([high, middle, place - high - middle, jnp.zeros_like(place)], axis=0)
    got = mm(pieces.astype(BF16), hot, (1, 1))
    grad_p[...] = (gp_own[...] + (got[0:8] + got[8:16] + got[16:24]))[0:3]
    for k, ref in enumerate((grad, one_new, two_new, par_new)):
        to_flat(ref, shares[k])
    to_flat(par_low, shares[3].astype(BF16))
    rows = lax.broadcasted_iota(jnp.int32, (8, F), 0)
    lanes = lax.broadcasted_iota(jnp.int32, (8, F), 1)
    for k, ref in enumerate((weight_norms, update_norms)):
        line = jnp.sum(
            jnp.where(rows == lanes, norms[8 * k : 8 * k + 8, :], 0.0), axis=0, keepdims=True
        )
        ref[...] = line[0, :GROUPS]
    elem_mean[...] = stats[0, :ELEMS]
    scale[...] = stats[1, :1]


def finish(atoms, length):
    shape = jax.ShapeDtypeStruct
    in_vmem = pl.BlockSpec(memory_space=pltpu.VMEM)
    outs = (
        [shape((atoms, F), F32), shape((3, atoms, F), F32), shape((3, atoms), F32)]
        + [shape((ELEMS,), F32), shape((1,), F32)]
        + [shape((length,), F32)] * 4
        + [shape((length,), BF16), shape((GROUPS,), F32), shape((GROUPS,), F32)]
    )
    return pl.pallas_call(
        finish_kernel,
        out_shape=tuple(outs),
        in_specs=[in_vmem] * 9,
        out_specs=(in_vmem,) * len(outs),
        compiler_params=pltpu.CompilerParams(vmem_limit_bytes=62 * 1024 * 1024),
        name="finish",
    )


def body(
    scalars_in,
    vectors_in,
    positions,
    cotan_scalar,
    cotan_vector,
    target_energy,
    forces,
    elements,
    crystal,
    lattice,
    edge_src,
    edge_dst,
    edge_shift,
    edge_count,
    send_rows,
    params,
    first_moment,
    second_moment,
):
    atoms = scalars_in.shape[0]
    edges = edge_src.shape[0]
    cap = send_rows.shape[2]
    halo = 2 * HOPS * cap
    groups = lax.axis_size("atoms") // 4
    length = params.shape[0]
    par, halo_rows, p_halo, goal, stats, src_tiles = gather_all(atoms, cap, groups, length, edges)(
        send_rows,
        params,
        scalars_in,
        vectors_in,
        positions,
        target_energy.reshape(-1, F),
        elements.reshape(-1, F),
        forces,
        edge_src.reshape(-1, F),
    )
    s_two, v_two, gs_own, gv_own, g_halo, gp_own, gp_halo, gpar = layer(atoms, halo, edges)(
        edge_dst,
        edge_count,
        src_tiles.reshape(-1),
        crystal.reshape(-1, F),
        edge_dst.reshape(-1, F),
        edge_shift,
        jnp.transpose(lattice),
        par,
        scalars_in,
        vectors_in,
        positions,
        halo_rows,
        p_halo,
        cotan_scalar,
        cotan_vector,
        goal,
    )
    back, p_back, shares, norms = reduce_all(cap, groups, length)(
        gpar, g_halo, gp_halo, params, first_moment, second_moment
    )
    (
        grad_s,
        grad_v,
        grad_p,
        elem_mean,
        scale,
        grad,
        one_new,
        two_new,
        par_new,
        par_low,
        weight_norms,
        update_norms,
    ) = finish(atoms, length)(
        back, p_back, shares, norms, stats, send_rows, gs_own, gv_own, gp_own
    )
    return (
        s_two,
        v_two,
        grad_s,
        grad_v,
        grad_p,
        elem_mean,
        scale.reshape(()),
        grad,
        one_new,
        two_new,
        par_new,
        par_low,
        weight_norms,
        update_norms,
    )


def solution(mesh):
    joint = ("atoms", "rep")
    in_specs = (
        P(joint, None),
        P(None, joint, None),
        P(None, joint),
        P(joint, None),
        P(None, joint, None),
        P(joint),
        P(None, joint),
        P(joint),
        P(joint),
        P(),
        P(joint),
        P(joint),
        P(None, joint),
        P(joint),
        P(joint, None, None),
        P(joint),
        P(joint),
        P(joint),
    )
    out_specs = (
        P(joint, None),
        P(None, joint, None),
        P(joint, None),
        P(None, joint, None),
        P(None, joint),
        P(),
        P(),
        P(joint),
        P(joint),
        P(joint),
        P(joint),
        P(joint),
        P(),
        P(),
    )
    return jax.shard_map(body, mesh=mesh, in_specs=in_specs, out_specs=out_specs, check_vma=False)
```

```python
import functools

import jax
import jax.numpy as jnp
from jax import lax
from jax.experimental import pallas as pl
from jax.experimental.pallas import tpu as pltpu
from jax.sharding import PartitionSpec as P

F = 128
R = 20
HOPS = 4
ELEMS = 100
STEP = 10
GROUPS = 7

CUTOFF = 5.0
BETA_ONE = 0.9
BETA_TWO = 0.99
RATE = 0.3
DECAY = 0.01
EPSILON = 1e-06

BLOCK = 256
WINDOW = 128
PAIR = 2
LANE_ROWS = 80
SUB = 16
ROWS = 256
F32 = jnp.float32
BF16 = jnp.bfloat16

AT_W1, AT_W2, AT_WF, AT_WM, AT_U1, AT_U2 = 0, 128, 512, 572, 828, 1084
AT_B1, AT_B2, AT_BF, AT_C1, AT_C2, AT_READ, PARAM_ROWS = 1468, 1469, 1472, 1475, 1476, 1479, 1480
PARAM_PAD = PARAM_ROWS + 8
GROUP_ENDS = (128, 512, 572, 828, 1084, 1468)
MESH = pl.DeviceIdType.MESH
BATCHES = ((3, 7), (2, 6), (1, 5), (0, 4))


def mm(left, right, contract=(1, 0)):
    return lax.dot_general(
        left, right, (((contract[0],), (contract[1],)), ((), ())), preferred_element_type=F32
    )


def split(value):
    high = value.astype(BF16)
    return high, (value - high.astype(F32)).astype(BF16)


def dot3(left, right, contract=(1, 0)):
    return (
        mm(left[0], right[0], contract)
        + mm(left[1], right[0], contract)
        + mm(left[0], right[1], contract)
    )


def linear(pair, weights):
    both = jnp.concatenate(pair, axis=1)
    return mm(both, weights[0 : 2 * F, :]) + mm(pair[0], weights[2 * F : 3 * F, :])


def back_through(pair, weights):
    return dot3(pair, (weights[0:F, :], weights[2 * F : 3 * F, :]), (1, 1))


def wide_row(ref, start, parts):
    return jnp.concatenate([ref[start + j : start + j + 1, :] for j in range(parts)], axis=1)


def add_row(ref, start, parts, value):
    total = jnp.sum(value, axis=0, keepdims=True)
    for j in range(parts):
        ref[start + j : start + j + 1, :] += total[:, j * F : (j + 1) * F]


def add_matrix(ref, start, parts, value):
    for j in range(parts):
        add_column(ref, start, parts, j, value[:, j * F : (j + 1) * F], value.shape[0])


def sigmoid(value):
    return 1.0 / (1.0 + jnp.exp(-value))


def column(ref, start, parts, j, count=F):
    if parts == 1:
        return ref[start : start + count, :]
    return ref[pl.ds(start + j, count, stride=parts), :]


def add_column(ref, start, parts, j, value, count=F):
    if parts == 1:
        ref[start : start + count, :] += value
    else:
        ref[pl.ds(start + j, count, stride=parts), :] += value


def rows_of(start, count, unit):
    return pl.ds(pl.multiple_of(start, unit), count)


def lay_flat(ref, count):
    return jnp.concatenate([ref[k : k + 1, :] for k in range(count)], axis=1)


def weave(*parts):
    parts = list(parts)
    while parts:
        for part in list(parts):
            try:
                next(part)
            except StopIteration:
                parts.remove(part)


def layer_kernel(
    dst_s,
    count_s,
    src_s,
    crystal,
    dst_v,
    shift_v,
    lat,
    par,
    s_own,
    v_own,
    p_own,
    halo_rows,
    p_halo,
    cot_s,
    cot_v,
    goal,
    s_two,
    v_two,
    gs_own,
    gv_own,
    g_halo,
    gp_own,
    gp_halo,
    gpar,
    tab,
    rows,
    acc,
    stage,
    dtab,
    lane_buf,
    slope_buf,
    inv_buf,
    free_buf,
    turn_buf,
    sums,
    gd,
    gbuf,
    fbuf,
    mbuf,
    ltbuf,
    tbuf,
    wcat,
    wq,
    gwf,
    gpd,
    w1,
    w2,
    wm,
    u1,
    u2,
):
    atoms = s_own.shape[0]
    halo = halo_rows.shape[1]
    blocks_128 = shift_v.shape[1] // F
    ends_buf = stage.at[0 : blocks_128 * 16]
    shift_buf = stage.at[blocks_128 * 16 : blocks_128 * 24]
    place_buf = stage.at[blocks_128 * 24 : blocks_128 * 32]
    s_halo, v_halo = halo_rows.at[0], halo_rows.at[1:4]
    gs_halo, gv_halo = g_halo.at[0], g_halo.at[1:4]
    edges = shift_v.shape[1]
    blocks = edges // BLOCK

    wcat[...] = jnp.zeros_like(wcat)
    wq[...] = jnp.zeros_like(wq)
    gwf[...] = jnp.zeros_like(gwf)
    gpd[...] = jnp.zeros_like(gpd)
    gpar[...] = jnp.zeros_like(gpar)
    sums[...] = jnp.zeros_like(sums)
    for ref, start, parts in ((w1, AT_W1, 1), (w2, AT_W2, 3), (wm, AT_WM, 2), (u2, AT_U2, 3)):
        for j in range(parts):
            high, low = split(column(par, start, parts, j))
            for k, value in enumerate((high, high, low)):
                ref[k * F : (k + 1) * F, j * F : (j + 1) * F] = value
    u1[0 : 2 * F, :], u1[2 * F : 4 * F, :] = split(par[AT_U1 : AT_U1 + 2 * F, :])
    for j in range(3):
        wide = jnp.concatenate(
            [
                column(par, AT_WF, 3, j, R),
                par[AT_BF + j : AT_BF + j + 1, :],
                jnp.zeros((3, F), F32),
            ],
            axis=0,
        )
        high = wide.astype(BF16).astype(F32)
        low = wide - high
        pieces = jnp.concatenate([high, high, low, jnp.zeros((56, F), F32)], axis=0)
        wcat[:, j * F : (j + 1) * F] = pieces.astype(BF16)
        pieces = jnp.concatenate([high, low, jnp.zeros((80, F), F32)], axis=0)
        wq[j * F : (j + 1) * F, :] = jnp.transpose(pieces).astype(BF16)

    names = lay_flat(crystal, atoms // F)
    spots = lax.broadcasted_iota(jnp.int32, (F, atoms), 0)
    for k in range(atoms // F):
        acc[16 * k : 16 * k + 16, :] = jnp.zeros((16, F), F32)

    @pl.loop(0, lat.shape[1] // F)
    def _(step):
        table = lat[:, rows_of(step * F, F, F)]
        high = table.astype(BF16).astype(F32)
        middle = (table - high).astype(BF16).astype(F32)
        gap = jnp.zeros((7, F), F32)
        pieces = jnp.concatenate([high, gap, middle, gap, table - high - middle, gap], axis=0)
        got = mm(pieces.astype(BF16), jnp.where(names - step * F == spots, 1.0, 0.0).astype(BF16))
        got = got[0:16] + got[16:32] + got[32:48]
        for k in range(atoms // F):
            acc[16 * k : 16 * k + 16, :] += got[:, k * F : (k + 1) * F]

    across = jnp.concatenate([acc[16 * k : 16 * k + 16, :] for k in range(atoms // F)], axis=1)
    part = jnp.concatenate([p_own[...], across[0:9], jnp.zeros((4, atoms), F32)], axis=0)
    high = part.astype(BF16).astype(F32)
    middle = (part - high).astype(BF16).astype(F32)
    low = part - high - middle
    dtab[...] = jnp.concatenate([high, middle, low], axis=0).astype(BF16)

    for s_ref, v_ref, p_ref, base, count in (
        (s_own, v_own, p_own, 0, atoms),
        (s_halo, v_halo, p_halo, atoms, halo),
    ):
        place = jnp.concatenate([p_ref[0:3, :], jnp.zeros((F - 3, count), F32)], axis=0)
        tab[pl.ds(base * 8 + 6, count, stride=8), :] = jnp.transpose(place)
        tab[pl.ds(base * 8 + 7, count, stride=8), :] = jnp.zeros((count, F), F32)
        for c in range(3):
            tab[pl.ds(base * 8 + 3 + c, count, stride=8), :] = v_ref[c]

        @pl.loop(0, count // ROWS)
        def _(step):
            first = step * ROWS
            s_pair = split(s_ref[rows_of(first, ROWS, ROWS), :])
            act = linear(s_pair, w1) + par[AT_B1 : AT_B1 + 1, :]
            x = linear(split(act * sigmoid(act)), w2) + wide_row(par, AT_B2, 3)
            for j in range(3):
                tab[pl.ds((base + first) * 8 + j, ROWS, stride=8), :] = x[:, j * F : (j + 1) * F]

    slots = lax.broadcasted_iota(jnp.int32, (WINDOW, BLOCK), 0)
    eight = lax.broadcasted_iota(jnp.int32, (8, 1), 0)
    wide_lane = lax.broadcasted_iota(jnp.int32, (1, F), 1)
    chunks = edges // F
    per = BLOCK // F

    def destinations(i):
        return jnp.concatenate([dst_v[pl.ds(i * per + k, 1), :] for k in range(per)], axis=1)

    def window_range(i):
        return dst_s[i * BLOCK] // WINDOW, dst_s[i * BLOCK + BLOCK - 1] // WINDOW

    def hot(dst, w):
        return jnp.where(dst - w * WINDOW == slots, 1.0, 0.0).astype(BF16)

    def window(w):
        return rows_of(w * WINDOW, WINDOW, WINDOW)

    def lane_chunk(i, k):
        return rows_of((i * per + k) * LANE_ROWS, LANE_ROWS, LANE_ROWS)

    def source(i, j):
        return pl.ds(pl.multiple_of(src_s[i * BLOCK + j], 8), 8)

    def ends_in(i, w):
        got = mm(dtab[:, window(w)], hot(destinations(i), w))
        return got[0:16] + got[16:32] + got[32:48]

    def gather(i):
        for j in range(BLOCK):
            spot = pl.multiple_of(i * (BLOCK * 8), BLOCK * 8) + j * 8
            rows[pl.ds(pl.multiple_of(spot, 8), 8), :] = tab[source(i, j), :]
            if j % 16 == 15:
                yield

    def ends(i):
        got = ends_in(i, window_range(i)[0])
        yield
        for k in range(per):
            chunk = i * per + k
            shift_buf[pl.ds(pl.multiple_of(chunk * 8, 8), 3), :] = shift_v[
                :, rows_of(chunk * F, F, F)
            ].astype(F32)
            ends_buf[rows_of(chunk * 16, 16, 16), :] = got[:, k * F : (k + 1) * F]
            yield

    def places_of(i):
        for k in range(per):
            chunk = i * per + k
            place = rows[pl.ds(chunk * (F * 8) + 6, F, stride=8), :]
            yield
            place_buf[rows_of(chunk * 8, 8, 8), :] = jnp.transpose(place)[0:8]
            yield

    @pl.loop(0, blocks // PAIR)
    def _(step):
        for t in range(PAIR):
            i = step * PAIR + t
            weave(ends(i), places_of(jnp.maximum(i - 1, 0)), gather(i))
            first, last = window_range(i)

            @pl.loop(first + 1, last + 1)
            def _(w):
                more = ends_in(i, w)
                for k in range(per):
                    ends_buf[rows_of((i * per + k) * 16, 16, 16), :] += more[:, k * F : (k + 1) * F]

    weave(places_of(blocks - 1))

    def dense(ref, row, step):
        return ref[pl.ds(row, chunks, stride=step), :]

    def put_row(row, value):
        lane_buf[pl.ds(row, chunks, stride=LANE_ROWS), :] = value

    shift = [dense(shift_buf, k, 8) for k in range(3)]
    rel = [
        dense(place_buf, c, 8)
        + (
            shift[0] * dense(ends_buf, 3 + c, 16)
            + shift[1] * dense(ends_buf, 6 + c, 16)
            + shift[2] * dense(ends_buf, 9 + c, 16)
        )
        - dense(ends_buf, c, 16)
        for c in range(3)
    ]
    square = rel[0] * rel[0] + rel[1] * rel[1] + rel[2] * rel[2]
    dist = jnp.sqrt(jnp.maximum(square, 0.25))
    inv = 1.0 / dist
    inv_buf[...] = inv
    free_buf[...] = jnp.where(square > 0.25, 1.0, 0.0)
    for c in range(3):
        put_row(72 + c, rel[c] * inv)
    put_row(75, dst_v[...].astype(F32))
    nothing = jnp.zeros((chunks, F), F32)
    for row in (21, 22, 23, 45, 46, 47, 69, 70, 71, 76, 77, 78, 79):
        put_row(row, nothing)
    for row in (21, 22, 23):
        slope_buf[pl.ds(row, chunks, stride=24), :] = nothing
    angle = dist * (jnp.pi / CUTOFF)
    sin_one, cos_one = jnp.sin(angle), jnp.cos(angle)
    place = lax.broadcasted_iota(jnp.int32, (chunks, F), 0) * F + lax.broadcasted_iota(
        jnp.int32, (chunks, F), 1
    )
    inside = (dist < CUTOFF) & (place < count_s[0])
    envelope = jnp.where(inside, 0.5 * (cos_one + 1.0), 0.0)
    fall = jnp.where(inside, (-0.5 * jnp.pi / CUTOFF) * sin_one, 0.0)
    sin_n, cos_n = sin_one, cos_one
    for n in range(R + 1):
        if n < R:
            radial = sin_n * inv
            slope = (((n + 1) * jnp.pi / CUTOFF) * cos_n - radial) * inv
            scaled = envelope * radial
            change = fall * radial + envelope * slope
            sin_n, cos_n = sin_n * cos_one + cos_n * sin_one, cos_n * cos_one - sin_n * sin_one
        else:
            scaled, change = envelope, fall
        high = scaled.astype(BF16).astype(F32)
        put_row(n, high)
        put_row(24 + n, scaled - high)
        put_row(48 + n, high)
        slope_buf[pl.ds(n, chunks, stride=24), :] = change

    def comp(i, k, sub):
        return pl.ds(i * (BLOCK * 8) + sub * (SUB * 8) + k, SUB, stride=8)

    def filters(i, t):
        for k in range(per):
            full = jnp.concatenate(
                [lane_buf[lane_chunk(i, k), :], jnp.zeros((F - LANE_ROWS, F), F32)], axis=0
            )
            ltbuf[t, k * F : (k + 1) * F, :] = jnp.transpose(full)
            yield
        fbuf[t] = mm(ltbuf[t].astype(BF16), wcat[...])
        yield

    def messages(i, t):
        for sub in range(BLOCK // SUB):
            at = slice(sub * SUB, (sub + 1) * SUB)
            m1, m2, m3 = [
                rows[comp(i, j, sub), :] * fbuf[t, at, j * F : (j + 1) * F] for j in range(3)
            ]
            out = [m1]
            for c in range(3):
                out.append(m2 * ltbuf[t, at, 72 + c : 73 + c] + m3 * rows[comp(i, 3 + c, sub), :])
            for k in range(4):
                high, low = split(out[k])
                mbuf[t, at, k * F : (k + 1) * F] = high
                mbuf[t, at, (4 + k) * F : (5 + k) * F] = low
            yield

    def collect(i, t, w):
        pick = hot(destinations(i), w)
        for k in range(2):
            of = slice(k * 2 * F, (k + 1) * 2 * F)
            more = slice((k + 2) * 2 * F, (k + 3) * 2 * F)
            sums[window(w), of] += mm(pick, mbuf[t, :, of]) + mm(pick, mbuf[t, :, more])
            yield

    def collect_more(i, t):
        first, last = window_range(i)

        @pl.loop(first + 1, last + 1)
        def _(w):
            weave(collect(i, t, w))

    mbuf[...] = jnp.zeros_like(mbuf)
    weave(filters(0, 0))

    @pl.loop(0, blocks // PAIR)
    def _(step):
        for t in range(PAIR):
            i = step * PAIR + t
            before = jnp.maximum(i - 1, 0)
            weave(
                filters(jnp.minimum(i + 1, blocks - 1), 1 - t),
                collect(before, 1 - t, window_range(before)[0]),
                messages(i, t),
            )
            collect_more(before, 1 - t)

    weave(collect(blocks - 1, PAIR - 1, window_range(blocks - 1)[0]))
    collect_more(blocks - 1, PAIR - 1)

    @pl.loop(0, atoms // ROWS)
    def _(step):
        at = rows_of(step * ROWS, ROWS, ROWS)
        s_one = s_own[at, :] + sums[at, 0:F]
        v_one = [v_own[c, at, :] + sums[at, (c + 1) * F : (c + 2) * F] for c in range(3)]
        v_pair = [split(v) for v in v_one]
        mixed = [linear(v, wm) for v in v_pair]
        v_lin = [m[:, :F] for m in mixed]
        w_lin = [m[:, F:] for m in mixed]
        size = jnp.sqrt(v_lin[0] * v_lin[0] + v_lin[1] * v_lin[1] + v_lin[2] * v_lin[2] + 1.0)
        s_pair = split(jnp.concatenate([s_one, size], axis=1))
        u1_pair = (u1[0 : 2 * F, :], u1[2 * F : 4 * F, :])
        act = dot3(s_pair, u1_pair) + par[AT_C1 : AT_C1 + 1, :]
        gate = sigmoid(act)
        hidden = split(act * gate)
        gating = linear(hidden, u2) + wide_row(par, AT_C2, 3)
        a1, a2, a3 = [gating[:, j * F : (j + 1) * F] for j in range(3)]
        inner = v_lin[0] * w_lin[0] + v_lin[1] * w_lin[1] + v_lin[2] * w_lin[2]
        s_out = s_one + a3 + a2 * inner
        s_two[at, :] = s_out
        read = par[AT_READ : AT_READ + 1, :]
        out_pair = split(s_out)
        energy = dot3(split(jnp.broadcast_to(read, (8, F))), out_pair, (1, 1))
        error = energy - goal[:, at]
        error_col = jnp.transpose(error)[:, 0:1]
        gpar[AT_READ : AT_READ + 1, :] += dot3(split(error), out_pair)[0:1]
        gs = cot_s[at, :] + error_col * read
        gv = []
        for c in range(3):
            v_two[c, at, :] = v_one[c] + a1 * w_lin[c]
            gv.append(cot_v[c, at, :])
        ga = [gv[0] * w_lin[0] + gv[1] * w_lin[1] + gv[2] * w_lin[2], gs * inner, gs]
        g_inner = gs * a2
        ga = jnp.concatenate(ga, axis=1)
        ga_pair = split(ga)
        add_matrix(gpar, AT_U2, 3, dot3(hidden, ga_pair, (0, 0)))
        add_row(gpar, AT_C2, 3, ga)
        g_act = back_through(ga_pair, u2) * (gate * (1.0 + act * (1.0 - gate)))
        g_act_pair = split(g_act)
        gpar[AT_U1 : AT_U1 + 2 * F, :] += dot3(s_pair, g_act_pair, (0, 0))
        add_row(gpar, AT_C1, 1, g_act)
        g_both = dot3(g_act_pair, u1_pair, (1, 1))
        g_s_one = gs + g_both[:, :F]
        g_size = g_both[:, F:] / size
        gs_own[at, :] = g_s_one
        down = [g_s_one]
        for c in range(3):
            g_mixed = split(
                jnp.concatenate(
                    [
                        g_inner * w_lin[c] + g_size * v_lin[c],
                        a1 * gv[c] + g_inner * v_lin[c],
                    ],
                    axis=1,
                )
            )
            add_matrix(gpar, AT_WM, 2, dot3(v_pair[c], g_mixed, (0, 0)))
            g_v_one = gv[c] + back_through(g_mixed, wm)
            gv_own[c, at, :] = g_v_one
            down.append(g_v_one)
        for k in range(4):
            high, low = split(down[k])
            for part in range(ROWS // WINDOW):
                to = (step * (ROWS // WINDOW) + part) * (2 * WINDOW)
                of = slice(part * WINDOW, (part + 1) * WINDOW)
                gd[rows_of(to, WINDOW, WINDOW), k * F : (k + 1) * F] = high[of]
                gd[rows_of(to + WINDOW, WINDOW, WINDOW), k * F : (k + 1) * F] = low[of]

    twice = (lax.broadcasted_iota(jnp.int32, (1, 2 * WINDOW), 1) % WINDOW).astype(F32)
    for ref in (tab, acc, stage, mbuf, tbuf, turn_buf):
        ref[...] = jnp.zeros_like(ref)

    def collect_places(i, t, w):
        g_rel = turn_buf[t]
        high = g_rel.astype(BF16).astype(F32)
        middle = (g_rel - high).astype(BF16).astype(F32)
        pieces = jnp.concatenate(
            [high, middle, g_rel - high - middle, jnp.zeros_like(g_rel)], axis=0
        )
        got = mm(pieces.astype(BF16), hot(destinations(i), w), (1, 1))
        gpd[:, window(w)] += got[0:8] + got[8:16] + got[16:24]

    def fetch(t, w):
        near = ltbuf[t, :, 75:76] - (w * WINDOW).astype(F32)
        return mm(
            jnp.where(near == twice, 1.0, 0.0).astype(BF16),
            gd[rows_of(w * 2 * WINDOW, 2 * WINDOW, 2 * WINDOW), :],
        )

    def prepare(i, t):
        yield from filters(i, t)
        gbuf[t] = fetch(t, window_range(i)[0])
        yield

    def spread(i, t, earlier):
        for sub in range(BLOCK // SUB):
            at = slice(sub * SUB, (sub + 1) * SUB)
            for j in range(SUB // 2):
                for k, total in enumerate((tab, acc)):
                    spot = sub * SUB + k * (SUB // 2) + j
                    held = (t * BLOCK + spot) * 8
                    total[source(earlier, spot), :] += stage[held : held + 8, :]
                if j % 8 == 7:
                    yield
            to = [pl.ds(t * (BLOCK * 8) + sub * (SUB * 8) + k, SUB, stride=8) for k in range(6)]
            g_s = gbuf[t, at, 0:F]
            g_v = [gbuf[t, at, (c + 1) * F : (c + 2) * F] for c in range(3)]
            x = [rows[comp(i, j, sub), :] for j in range(3)]
            v = [rows[comp(i, 3 + c, sub), :] for c in range(3)]
            f = [fbuf[t, at, j * F : (j + 1) * F] for j in range(3)]
            u = [ltbuf[t, at, 72 + c : 73 + c] for c in range(3)]
            g_m = [
                g_s,
                g_v[0] * u[0] + g_v[1] * u[1] + g_v[2] * u[2],
                g_v[0] * v[0] + g_v[1] * v[1] + g_v[2] * v[2],
            ]
            m2 = x[1] * f[1]
            m3 = x[2] * f[2]
            turn = jnp.zeros((SUB, F), F32)
            for c in range(3):
                total = jnp.sum(g_v[c] * m2, axis=1, keepdims=True)
                turn = jnp.where(wide_lane == 48 + c, total, turn)
                stage[to[3 + c], :] = g_v[c] * m3
            tbuf[t, at, :] = turn
            for j in range(3):
                high, low = split(g_m[j] * x[j])
                mbuf[t, at, j * F : (j + 1) * F] = high
                mbuf[t, at, (3 + j) * F : (4 + j) * F] = low
                stage[to[j], :] = g_m[j] * f[j]
            yield

    def settle(i, t):
        h_high, h_low = mbuf[t, :, : 3 * F], mbuf[t, :, 3 * F : 6 * F]
        back = mm(h_high, wq[...]) + mm(h_low, wq[...]) + tbuf[t]
        yield
        back = jnp.transpose(back)
        yield
        pieces = jnp.concatenate(
            [lane_buf[lane_chunk(i, k), :][0:48] for k in range(per)], axis=1
        ).astype(BF16)
        gwf[...] += mm(pieces, h_high) + mm(pieces, h_low)
        yield
        slope = jnp.concatenate(
            [slope_buf[rows_of((i * per + k) * 24, 24, 24), :] for k in range(per)], axis=1
        )
        g_dist = jnp.sum((back[0:24] + back[24:48]) * slope, axis=0, keepdims=True)
        g_unit = back[48:56]
        unit = jnp.concatenate([lane_buf[lane_chunk(i, k), :][72:80] for k in range(per)], axis=1)
        unit = jnp.where(eight < 3, unit, 0.0)
        inv, free = [
            jnp.concatenate([ref[pl.ds(i * per + k, 1), :] for k in range(per)], axis=1)
            for ref in (inv_buf, free_buf)
        ]
        yield
        along = jnp.sum(g_unit * unit, axis=0, keepdims=True)
        g_rel = g_unit * inv + (g_dist - along * inv) * free * unit
        turn_buf[t] = g_rel
        yield
        stage[pl.ds(t * (BLOCK * 8) + 6, BLOCK, stride=8), :] = jnp.transpose(
            jnp.concatenate([g_rel, jnp.zeros((F - 8, BLOCK), F32)], axis=0)
        )
        yield
        collect_places(i, t, window_range(i)[0])
        yield

    def prepare_more(i, t):
        first, last = window_range(i)

        @pl.loop(first + 1, last + 1)
        def _(w):
            gbuf[t] += fetch(t, w)

    def settle_more(i, t):
        first, last = window_range(i)

        @pl.loop(first + 1, last + 1)
        def _(w):
            collect_places(i, t, w)

    weave(prepare(0, 0))
    prepare_more(0, 0)

    @pl.loop(0, blocks // PAIR)
    def _(step):
        for t in range(PAIR):
            i = step * PAIR + t
            before, after = jnp.maximum(i - 1, 0), jnp.minimum(i + 1, blocks - 1)
            weave(spread(i, t, jnp.maximum(i - 2, 0)), settle(before, 1 - t), prepare(after, 1 - t))
            prepare_more(after, 1 - t)
            settle_more(before, 1 - t)

    weave(settle(blocks - 1, PAIR - 1))
    settle_more(blocks - 1, PAIR - 1)
    for t in range(PAIR):
        for j in range(BLOCK // 2):
            for k, total in enumerate((tab, acc)):
                spot = k * (BLOCK // 2) + j
                held = (t * BLOCK + spot) * 8
                total[source(blocks - PAIR + t, spot), :] += stage[held : held + 8, :]

    for j in range(3):
        total = gwf[0:24, j * F : (j + 1) * F] + gwf[24:48, j * F : (j + 1) * F]
        add_column(gpar, AT_WF, 3, j, total[0:R], R)
        gpar[AT_BF + j : AT_BF + j + 1, :] = total[R : R + 1]

    for s_ref, gs_ref, gv_ref, gp_ref, base, count in (
        (s_own, gs_own, gv_own, gp_own, 0, atoms),
        (s_halo, gs_halo, gv_halo, gp_halo, atoms, halo),
    ):
        own = base == 0
        for k in range(0, count, ROWS):
            at = pl.ds((base + k) * 8 + 6, ROWS, stride=8)
            place = jnp.transpose(tab[at, :] + acc[at, :])[0:8]
            if own:
                place = place - gpd[:, k : k + ROWS]
            gp_ref[:, k : k + ROWS] = place

        @pl.loop(0, count // ROWS)
        def _(step):
            first = step * ROWS
            to = rows_of(first, ROWS, ROWS)

            def gathered(k):
                at = pl.ds((base + first) * 8 + k, ROWS, stride=8)
                return tab[at, :] + acc[at, :]

            for c in range(3):
                if own:
                    gv_ref[c, to, :] += gathered(3 + c)
                else:
                    gv_ref[c, to, :] = gathered(3 + c)
            s_pair = split(s_ref[to, :])
            act = linear(s_pair, w1) + par[AT_B1 : AT_B1 + 1, :]
            gate = sigmoid(act)
            hidden = split(act * gate)
            g_x = jnp.concatenate([gathered(j) for j in range(3)], axis=1)
            g_pair = split(g_x)
            add_matrix(gpar, AT_W2, 3, dot3(hidden, g_pair, (0, 0)))
            add_row(gpar, AT_B2, 3, g_x)
            g_act = back_through(g_pair, w2) * (gate * (1.0 + act * (1.0 - gate)))
            g_act_pair = split(g_act)
            add_matrix(gpar, AT_W1, 1, dot3(s_pair, g_act_pair, (0, 0)))
            add_row(gpar, AT_B1, 1, g_act)
            g_s = back_through(g_act_pair, w1)
            if own:
                gs_ref[to, :] += g_s
            else:
                gs_ref[to, :] = g_s


def layer(atoms, halo, edges):
    shape = jax.ShapeDtypeStruct
    total = atoms + halo
    in_vmem = pl.BlockSpec(memory_space=pltpu.VMEM)
    in_smem = pl.BlockSpec(memory_space=pltpu.SMEM)
    outs = (
        shape((atoms, F), F32),
        shape((3, atoms, F), F32),
        shape((atoms, F), F32),
        shape((3, atoms, F), F32),
        shape((4, halo, F), F32),
        shape((8, atoms), F32),
        shape((8, halo), F32),
        shape((PARAM_PAD, F), F32),
    )
    scratch = [
        pltpu.VMEM((total * 8, F), F32),
        pltpu.VMEM((edges * 8, F), F32),
        pltpu.VMEM((total * 8, F), F32),
        pltpu.VMEM((PAIR * BLOCK * 8, F), F32),
        pltpu.VMEM((48, atoms), BF16),
        pltpu.VMEM((edges // F * LANE_ROWS, F), F32),
        pltpu.VMEM((edges // F * 24, F), F32),
        pltpu.VMEM((edges // F, F), F32),
        pltpu.VMEM((edges // F, F), F32),
        pltpu.VMEM((PAIR, 8, BLOCK), F32),
        pltpu.VMEM((atoms, 4 * F), F32),
        pltpu.VMEM((2 * atoms, 4 * F), BF16),
        pltpu.VMEM((PAIR, BLOCK, 4 * F), F32),
        pltpu.VMEM((PAIR, BLOCK, 3 * F), F32),
        pltpu.VMEM((PAIR, BLOCK, 8 * F), BF16),
        pltpu.VMEM((PAIR, BLOCK, F), F32),
        pltpu.VMEM((PAIR, BLOCK, F), F32),
        pltpu.VMEM((F, 3 * F), BF16),
        pltpu.VMEM((3 * F, F), BF16),
        pltpu.VMEM((48, 3 * F), F32),
        pltpu.VMEM((8, atoms), F32),
        pltpu.VMEM((3 * F, F), BF16),
        pltpu.VMEM((3 * F, 3 * F), BF16),
        pltpu.VMEM((3 * F, 2 * F), BF16),
        pltpu.VMEM((4 * F, F), BF16),
        pltpu.VMEM((3 * F, 3 * F), BF16),
    ]
    return pl.pallas_call(
        layer_kernel,
        out_shape=outs,
        in_specs=[in_smem] * 3 + [in_vmem] * 13,
        out_specs=(in_vmem,) * len(outs),
        scratch_shapes=scratch,
        compiler_params=pltpu.CompilerParams(vmem_limit_bytes=63 * 1024 * 1024),
        name="layer",
    )


def hop_offset(j):
    return j + 1 if j < HOPS else HOPS - 1 - j


class Place:
    def __init__(self):
        self.chips = lax.axis_size("atoms")
        self.cores = lax.axis_size("rep")
        self.count = self.chips * self.cores
        self.groups = self.chips // 4
        chip = lax.axis_index("atoms")
        self.core = lax.axis_index("rep")
        self.joint = chip * self.cores + self.core
        self.group = chip // 4
        self.quarter = chip % 4
        self.mate = 1 - self.core

    def other_groups(self):
        return [lax.rem(self.group + k, self.groups) for k in range(1, self.groups)]

    def other_quarters(self):
        return [lax.rem(self.quarter + k, 4) for k in range(1, 4)]

    def in_group(self, group):
        return (group * 4 + self.quarter, self.core)

    def in_quarter(self, quarter):
        return (self.group * 4 + quarter, self.core)

    def beside(self):
        return (self.group * 4 + self.quarter, self.mate)

    def hop(self, by):
        other = self.joint + by
        exists = (other >= 0) & (other < self.count)
        other = jnp.clip(other, 0, self.count - 1)
        return exists, (other // self.cores, other % self.cores)

    def others_of_group(self):
        own = self.quarter * self.cores + self.core
        places = [lax.rem(own + k, 4 * self.cores) for k in range(1, 4 * self.cores)]
        return [(o, (self.group * 4 + o // self.cores, o % self.cores)) for o in places]

    def greet(self):
        barrier = pltpu.get_barrier_semaphore()
        fixed = [self.in_group(g) for g in self.other_groups()]
        fixed += [device for _, device in self.others_of_group()]
        for device in fixed:
            pl.semaphore_signal(barrier, inc=1, device_id=device, device_id_type=MESH)
        hops = [self.hop(hop_offset(j)) for j in range(2 * HOPS)]
        expected = jnp.int32(len(fixed))
        for exists, device in hops:
            expected = expected + jnp.where(exists, 1, 0)

            @pl.when(exists)
            def _():
                pl.semaphore_signal(barrier, inc=1, device_id=device, device_id_type=MESH)

        return expected


def send(src, dst, send_sem, recv_sem, device):
    return pltpu.make_async_remote_copy(
        src_ref=src,
        dst_ref=dst,
        send_sem=send_sem,
        recv_sem=recv_sem,
        device_id=device,
        device_id_type=MESH,
    )


def start_all(copies):
    for copy in copies:
        copy.start()
    return copies


def wait_sent(copies):
    for copy in copies:
        copy.wait_send()


def window_rows(length):
    return -(-((length + F - 1) // F + 1) // 8) * 8


class SmallSum:
    def __init__(self, place, slots_a, slots_b, sends, recvs):
        self.place = place
        self.slots = (slots_a, slots_b)
        self.sends, self.recvs = sends, recvs
        self.sent = []

    def partners(self, phase):
        p = self.place
        if phase == 0:
            return p.quarter * p.cores + p.core, p.others_of_group(), 0
        return p.group, [(g, p.in_group(g)) for g in p.other_groups()], 4 * p.cores

    def start(self, phase, value):
        slots = self.slots[phase]
        mine, others, base = self.partners(phase)
        slots[mine] = value
        for k, (_, device) in enumerate(others):
            spot = slots.at[mine]
            copy = send(spot, spot, self.sends.at[base + k], self.recvs.at[base + mine], device)
            copy.start()
            self.sent.append(copy)

    def finish(self, phase):
        slots = self.slots[phase]
        _, others, base = self.partners(phase)
        for o, device in others:
            spot = slots.at[o]
            send(spot, spot, self.sends.at[base], self.recvs.at[base + o], device).wait_recv()
        total = slots[0]
        for k in range(1, slots.shape[0]):
            total = total + slots[k]
        return total

    def done(self):
        wait_sent(self.sent)


def small_scratch(groups, rows):
    count = groups + 8
    return [
        pltpu.VMEM((8, rows, F), F32),
        pltpu.VMEM((groups, rows, F), F32),
        pltpu.SemaphoreType.DMA((count,)),
        pltpu.SemaphoreType.DMA((count,)),
    ]


def from_flat(ref, rows):
    length = ref.shape[0]
    whole, rest = length // F, length % F
    lines = [ref[pl.ds(r * F, F)].reshape(1, F) for r in range(whole)]
    if rest:
        last = ref[pl.ds(whole * F, rest)].reshape(1, rest)
        lines.append(jnp.concatenate([last, jnp.zeros((1, F - rest), F32)], axis=1))
    lines.append(jnp.zeros((rows - len(lines), F), F32))
    return jnp.concatenate(lines, axis=0)


def to_flat(ref, value):
    length = ref.shape[0]
    whole, rest = length // F, length % F
    for r in range(whole):
        ref[pl.ds(r * F, F)] = value[r]
    if rest:
        ref[pl.ds(whole * F, rest)] = value[whole, :rest]


def gather_kernel(
    send_s,
    par_in,
    s_own,
    v_own,
    p_own,
    energy,
    elements,
    forces,
    edge_src,
    par,
    halo_rows,
    p_halo,
    goal,
    stats,
    src_tiles,
    slots,
    pack,
    places,
    p_out,
    p_in,
    zeros,
    ag_send,
    ag_recv,
    row_send,
    row_recv,
    place_send,
    place_recv,
    zero_sem,
    *small,
    length,
):
    here = Place()
    atoms = s_own.shape[0]
    cap = halo_rows.shape[1] // (2 * HOPS)
    wide = slots.shape[3]
    expected = here.greet()
    sums = SmallSum(here, *small)

    offset = lax.rem(here.joint * length, F)
    lane = lax.broadcasted_iota(jnp.int32, (1, F), 1)
    turned = pltpu.roll(from_flat(par_in, wide), offset, 1)
    above = jnp.concatenate([jnp.zeros((1, F), F32), turned[: wide - 1]], axis=0)
    mine = slots.at[here.group, here.quarter, here.core]
    mine[...] = jnp.where(lane < offset, above, turned)
    src_tiles[...] = edge_src[...] * 8

    count = atoms // F
    energy_row, element_row = lay_flat(energy, count), lay_flat(elements, count)
    hot = jnp.where(
        element_row == lax.broadcasted_iota(jnp.int32, (F, atoms), 0), 1.0, 0.0
    ).astype(BF16)
    high = energy_row.astype(BF16).astype(F32)
    middle = (energy_row - high).astype(BF16).astype(F32)
    eight = lax.broadcasted_iota(jnp.int32, (8, 1), 0)
    left = jnp.where(
        eight == 0,
        high,
        jnp.where(
            eight == 1, middle, jnp.where(eight == 2, energy_row - high - middle, jnp.where(eight == 3, 1.0, 0.0))
        ),
    )
    found = mm(left.astype(BF16), hot, (1, 1))
    squares = jnp.sum(forces[...] * forces[...], axis=0, keepdims=True)
    square = squares[:, 0:F]
    for k in range(1, count):
        square = square + squares[:, k * F : (k + 1) * F]
    tile = jnp.where(
        eight == 0,
        found[0:1] + found[1:2] + found[2:3],
        jnp.where(eight == 1, found[3:4], jnp.where(eight == 2, square, 0.0)),
    )
    places[...] = jnp.transpose(
        jnp.concatenate([p_own[...], jnp.zeros((F - 3, atoms), F32)], axis=0)
    )
    zeros[...] = jnp.zeros_like(zeros)
    hops = range(2 * HOPS)
    for j in hops:

        @pl.loop(0, cap // 16)
        def _(step):
            for k in range(16):
                r = step * 16 + k
                t = send_s[0, j, r]
                r = j * cap + r
                pack[0, pl.ds(r, 1), :] = s_own[pl.ds(t, 1), :]
                for c in range(3):
                    pack[1 + c, pl.ds(r, 1), :] = v_own[c, pl.ds(t, 1), :]
                p_out[pl.ds(r, 1), :] = places[pl.ds(t, 1), :]

    for j in range(0, 2 * HOPS, 2):
        pair = slice(j * cap, (j + 2) * cap)
        p_in[2 * HOPS + j // 2] = jnp.transpose(p_out[pair, :])[0:8]

    pl.semaphore_wait(pltpu.get_barrier_semaphore(), expected)
    first = start_all(
        [
            send(mine, mine, ag_send.at[k], ag_recv.at[here.group], here.in_group(g))
            for k, g in enumerate(here.other_groups())
        ]
    )
    sums.start(0, tile)
    row_copies, place_copies = [], []
    for j in hops:
        exists, device = here.hop(hop_offset(j))
        block = pl.ds(j * cap, cap)
        rows_copy = send(
            pack.at[:, block], halo_rows.at[:, block], row_send.at[j], row_recv.at[j], device
        )
        place_copy = send(
            p_in.at[2 * HOPS + j // 2], p_in.at[j], place_send.at[j], place_recv.at[j], device
        )
        row_copies.append((exists, rows_copy))
        place_copies.append((exists, place_copy))

        @pl.when(exists)
        def _():
            rows_copy.start()
            place_copy.start()

    for j in hops:
        known, device = here.hop(-hop_offset(j))

        @pl.when(jnp.logical_not(known))
        def _():
            p_in[j] = jnp.zeros((8, F), F32)
            fill = pltpu.make_async_copy(
                zeros, halo_rows.at[:, pl.ds(j * cap, cap)], zero_sem.at[j]
            )
            fill.start()
            fill.wait()

    for g in here.other_groups():
        spot = slots.at[g, here.quarter, here.core]
        send(spot, spot, ag_send.at[0], ag_recv.at[g], here.beside()).wait_recv()
    base = here.groups
    line = slots.at[:, here.quarter, here.core]
    second = start_all(
        [
            send(line, line, ag_send.at[base + k], ag_recv.at[base + here.quarter], here.in_quarter(q))
            for k, q in enumerate(here.other_quarters())
        ]
    )
    third = [
        send(
            line, line, ag_send.at[base + 4], ag_recv.at[base + 4 + here.quarter], here.beside()
        )
    ]
    third[0].start()
    sums.start(1, sums.finish(0))
    for k, q in enumerate(here.other_quarters()):
        line = slots.at[:, q, here.core]
        send(line, line, ag_send.at[0], ag_recv.at[base + q], here.beside()).wait_recv()
        copy = send(
            line, line, ag_send.at[base + 5 + k], ag_recv.at[base + 4 + q], here.beside()
        )
        copy.start()
        third.append(copy)
    for q in range(4):
        line = slots.at[:, q, here.mate]
        send(line, line, ag_send.at[0], ag_recv.at[base + 4 + q], here.beside()).wait_recv()

    par[...] = jnp.zeros_like(par)
    for p in range(here.count):
        row = p * length // F
        chip, core = p // here.cores, p % here.cores
        take = min(wide, PARAM_PAD - row)
        par[row : row + take, :] += slots[chip // 4, chip % 4, core, 0:take, :]

    total = sums.finish(1)
    mean = total[0:1] / jnp.maximum(total[1:2], 1.0)
    whole = jnp.sum(total[2:3], axis=1, keepdims=True)
    scale = jnp.sqrt(whole / (3.0 * atoms * here.count) + 1e-06)
    high = mean.astype(BF16).astype(F32)
    middle = (mean - high).astype(BF16).astype(F32)
    left = jnp.where(
        eight == 0,
        high,
        jnp.where(eight == 1, middle, jnp.where(eight == 2, mean - high - middle, 0.0)),
    )
    found = mm(left.astype(BF16), hot)
    goal[...] = (energy_row - (found[0:1] + found[1:2] + found[2:3])) / scale
    stats[...] = jnp.where(eight == 0, mean, jnp.where(eight == 1, scale, 0.0))

    for j in hops:
        known, device = here.hop(-hop_offset(j))

        @pl.when(known)
        def _():
            block = pl.ds(j * cap, cap)
            send(
                pack.at[:, block], halo_rows.at[:, block], row_send.at[j], row_recv.at[j], device
            ).wait_recv()
            send(p_in.at[j], p_in.at[j], place_send.at[j], place_recv.at[j], device).wait_recv()

    low_half = lane < cap
    for j in range(0, 2 * HOPS, 2):
        p_halo[:, j * cap : (j + 2) * cap] = jnp.where(low_half, p_in[j], p_in[j + 1])
    for exists, copy in row_copies + place_copies:

        @pl.when(exists)
        def _():
            copy.wait_send()

    wait_sent(first + second + third)
    sums.done()


def gather_all(atoms, cap, groups, length, edges):
    shape = jax.ShapeDtypeStruct
    halo = 2 * HOPS * cap
    wide = window_rows(length)
    in_vmem = pl.BlockSpec(memory_space=pltpu.VMEM)
    in_smem = pl.BlockSpec(memory_space=pltpu.SMEM)
    return pl.pallas_call(
        functools.partial(gather_kernel, length=length),
        out_shape=(
            shape((PARAM_PAD, F), F32),
            shape((4, halo, F), F32),
            shape((8, halo), F32),
            shape((1, atoms), F32),
            shape((8, F), F32),
            shape((edges // F, F), jnp.int32),
        ),
        in_specs=[in_smem] + [in_vmem] * 8,
        out_specs=(in_vmem, pl.BlockSpec(memory_space=pl.ANY)) + (in_vmem,) * 4,
        scratch_shapes=[
            pltpu.VMEM((groups, 4, 2, wide, F), F32),
            pltpu.VMEM((4, halo, F), F32),
            pltpu.VMEM((atoms, F), F32),
            pltpu.VMEM((halo, F), F32),
            pltpu.VMEM((3 * HOPS, 8, F), F32),
            pltpu.VMEM((4, cap, F), F32),
            pltpu.SemaphoreType.DMA((groups + 8,)),
            pltpu.SemaphoreType.DMA((groups + 8,)),
            pltpu.SemaphoreType.DMA((2 * HOPS,)),
            pltpu.SemaphoreType.DMA((2 * HOPS,)),
            pltpu.SemaphoreType.DMA((2 * HOPS,)),
            pltpu.SemaphoreType.DMA((2 * HOPS,)),
            pltpu.SemaphoreType.DMA((2 * HOPS,)),
        ]
        + small_scratch(groups, 8),
        compiler_params=pltpu.CompilerParams(
            collective_id=0, has_side_effects=True, vmem_limit_bytes=62 * 1024 * 1024
        ),
        name="gather_inputs",
    )


def reduce_kernel(
    gpar,
    g_halo,
    gp_halo,
    par,
    one,
    two,
    back,
    p_back,
    shares,
    norms,
    slots,
    pair_in,
    line_in,
    spot_in,
    turn,
    zeros,
    p_in,
    rs_send,
    rs_recv,
    row_send,
    row_recv,
    place_send,
    place_recv,
    zero_sem,
    *small,
    length,
):
    here = Place()
    cap = back.shape[1] // (2 * HOPS)
    wide = slots.shape[3]
    expected = here.greet()
    sums = SmallSum(here, *small)

    for p in range(here.count):
        row = p * length // F
        chip, core = p // here.cores, p % here.cores
        take = min(wide, PARAM_PAD - row)
        slots[chip // 4, chip % 4, core, 0:take, :] = gpar[row : row + take, :]
    old, m_one, m_two = [from_flat(ref, wide) for ref in (par, one, two)]
    zeros[...] = jnp.zeros_like(zeros)
    order = here.other_quarters() + [here.quarter]
    base = here.groups
    pl.semaphore_wait(pltpu.get_barrier_semaphore(), expected)
    third = start_all(
        [
            send(
                slots.at[:, q, here.mate],
                pair_in.at[:, q],
                rs_send.at[base + 4 + k],
                rs_recv.at[base + 4 + q],
                here.beside(),
            )
            for k, q in enumerate(order)
        ]
    )

    second = []
    for k, q in enumerate(order):
        line = pair_in.at[:, q]
        send(line, line, rs_send.at[0], rs_recv.at[base + 4 + q], here.beside()).wait_recv()
        slots[:, q, here.core] += pair_in[:, q]
        if k < 3:
            copy = send(
                slots.at[:, q, here.core],
                line_in.at[here.quarter],
                rs_send.at[base + k],
                rs_recv.at[base + here.quarter],
                here.in_quarter(q),
            )
            copy.start()
            second.append(copy)

    hops = range(2 * HOPS)
    copies = []

    def give_back(some):
        for j in some:
            exists, device = here.hop(-hop_offset(j))
            block = pl.ds(j * cap, cap)
            tile = pl.ds((j // 2) * F, F)
            rows_copy = send(
                g_halo.at[:, block], back.at[:, block], row_send.at[j], row_recv.at[j], device
            )
            place_copy = send(
                gp_halo.at[:, tile], p_in.at[j], place_send.at[j], place_recv.at[j], device
            )
            copies.extend([(exists, rows_copy), (exists, place_copy)])

            @pl.when(exists)
            def _():
                rows_copy.start()
                place_copy.start()

    give_back(BATCHES[0])
    for j in hops:
        known, device = here.hop(hop_offset(j))

        @pl.when(jnp.logical_not(known))
        def _():
            p_in[j] = jnp.zeros((8, F), F32)
            fill = pltpu.make_async_copy(zeros, back.at[:, pl.ds(j * cap, cap)], zero_sem.at[j])
            fill.start()
            fill.wait()

    for q in here.other_quarters():
        line = line_in.at[q]
        send(line, line, rs_send.at[0], rs_recv.at[base + q], here.beside()).wait_recv()
        slots[:, here.quarter, here.core] += line_in[q]
    first = start_all(
        [
            send(
                slots.at[g, here.quarter, here.core],
                spot_in.at[here.group],
                rs_send.at[k],
                rs_recv.at[here.group],
                here.in_group(g),
            )
            for k, g in enumerate(here.other_groups())
        ]
    )
    give_back(BATCHES[1])
    total = slots[here.group, here.quarter, here.core]
    for g in here.other_groups():
        spot = spot_in.at[g]
        send(spot, spot, rs_send.at[0], rs_recv.at[g], here.beside()).wait_recv()
        total = total + spot_in[g]

    offset = lax.rem(here.joint * length, F)
    lane = lax.broadcasted_iota(jnp.int32, (1, F), 1)
    turn[0:wide, :] = pltpu.roll(total, lax.rem(F - offset, F), 1)
    turn[wide : wide + 8, :] = jnp.zeros((8, F), F32)
    place = lax.broadcasted_iota(jnp.int32, (wide, F), 0) * F + lane
    inside = place < length
    g = jnp.where(lane + offset < F, turn[0:wide, :], turn[1 : wide + 1, :])
    g = jnp.where(inside, g, 0.0)
    shares[0] = g
    m_one = BETA_ONE * m_one + (1.0 - BETA_ONE) * g
    m_two = BETA_TWO * m_two + (1.0 - BETA_TWO) * g * g
    shares[1] = m_one
    shares[2] = m_two
    direction = (
        m_one
        / (1.0 - BETA_ONE**STEP)
        / (jnp.sqrt(m_two / (1.0 - BETA_TWO**STEP)) + EPSILON)
        + DECAY * old
    )
    spot = place + here.joint * length
    label = jnp.zeros((wide, F), jnp.int32)
    for end in GROUP_ENDS:
        label = label + jnp.where(spot >= end * F, 1, 0)
    label = jnp.where(inside, label, GROUPS)
    lines = []
    for value in (old, direction):
        square = value * value
        lines += [
            jnp.sum(jnp.where(label == k, square, 0.0), axis=0, keepdims=True)
            for k in range(GROUPS)
        ]
        lines.append(jnp.zeros((1, F), F32))
    sums.start(0, jnp.concatenate(lines, axis=0))
    give_back(BATCHES[2])
    sums.start(1, sums.finish(0))
    give_back(BATCHES[3])
    whole = jnp.sqrt(jnp.sum(sums.finish(1), axis=1, keepdims=True))
    ratio = whole[0:8] / whole[8:16]
    norms[...] = jnp.broadcast_to(whole, (16, F))
    trust = jnp.zeros((wide, F), F32)
    for k in range(GROUPS):
        trust = jnp.where(label == k, ratio[k : k + 1], trust)
    shares[3] = old - RATE * trust * direction

    for j in hops:
        known, device = here.hop(hop_offset(j))

        @pl.when(known)
        def _():
            block = pl.ds(j * cap, cap)
            tile = p_in.at[j]
            send(
                back.at[:, block], back.at[:, block], row_send.at[j], row_recv.at[j], device
            ).wait_recv()
            send(tile, tile, place_send.at[j], place_recv.at[j], device).wait_recv()

    low_half = lane < cap
    for j in range(0, 2 * HOPS, 2):
        p_back[:, j * cap : (j + 2) * cap] = jnp.where(low_half, p_in[j], p_in[j + 1])
    for exists, copy in copies:

        @pl.when(exists)
        def _():
            copy.wait_send()

    wait_sent(first + second + third)
    sums.done()


def reduce_all(cap, groups, length):
    shape = jax.ShapeDtypeStruct
    halo = 2 * HOPS * cap
    wide = window_rows(length)
    in_vmem = pl.BlockSpec(memory_space=pltpu.VMEM)
    in_any = pl.BlockSpec(memory_space=pl.ANY)
    return pl.pallas_call(
        functools.partial(reduce_kernel, length=length),
        out_shape=(
            shape((4, halo, F), F32),
            shape((8, halo), F32),
            shape((4, wide, F), F32),
            shape((16, F), F32),
        ),
        in_specs=[in_vmem, in_any] + [in_vmem] * 4,
        out_specs=(in_any, in_vmem, in_vmem, in_vmem),
        scratch_shapes=[
            pltpu.VMEM((groups, 4, 2, wide, F), F32),
            pltpu.VMEM((groups, 4, wide, F), F32),
            pltpu.VMEM((4, groups, wide, F), F32),
            pltpu.VMEM((groups, wide, F), F32),
            pltpu.VMEM((wide + 8, F), F32),
            pltpu.VMEM((4, cap, F), F32),
            pltpu.VMEM((2 * HOPS, 8, F), F32),
            pltpu.SemaphoreType.DMA((groups + 8,)),
            pltpu.SemaphoreType.DMA((groups + 8,)),
            pltpu.SemaphoreType.DMA((2 * HOPS,)),
            pltpu.SemaphoreType.DMA((2 * HOPS,)),
            pltpu.SemaphoreType.DMA((2 * HOPS,)),
            pltpu.SemaphoreType.DMA((2 * HOPS,)),
            pltpu.SemaphoreType.DMA((2 * HOPS,)),
        ]
        + small_scratch(groups, 16),
        compiler_params=pltpu.CompilerParams(
            collective_id=1, has_side_effects=True, vmem_limit_bytes=62 * 1024 * 1024
        ),
        name="reduce_outputs",
    )


def finish_kernel(
    back,
    p_back,
    shares,
    norms,
    stats,
    send_rows,
    gs_own,
    gv_own,
    gp_own,
    grad_s,
    grad_v,
    grad_p,
    elem_mean,
    scale,
    grad,
    one_new,
    two_new,
    par_new,
    par_low,
    weight_norms,
    update_norms,
):
    atoms = gs_own.shape[0]
    halo = back.shape[1]
    pick = jnp.concatenate([send_rows[0, j : j + 1, :] for j in range(2 * HOPS)], axis=1)
    hot = jnp.where(pick == lax.broadcasted_iota(jnp.int32, (atoms, halo), 0), 1.0, 0.0)
    hot = hot.astype(BF16)
    for k in range(4):
        high, low = split(back[k])
        extra = mm(hot, high) + mm(hot, low)
        if k == 0:
            grad_s[...] = gs_own[...] + extra
        else:
            grad_v[k - 1] = gv_own[k - 1] + extra
    place = p_back[...]
    high = place.astype(BF16).astype(F32)
    middle = (place - high).astype(BF16).astype(F32)
    pieces = jnp.concatenate([high, middle, place - high - middle, jnp.zeros_like(place)], axis=0)
    got = mm(pieces.astype(BF16), hot, (1, 1))
    grad_p[...] = (gp_own[...] + (got[0:8] + got[8:16] + got[16:24]))[0:3]
    for k, ref in enumerate((grad, one_new, two_new, par_new)):
        to_flat(ref, shares[k])
    to_flat(par_low, shares[3].astype(BF16))
    rows = lax.broadcasted_iota(jnp.int32, (8, F), 0)
    lanes = lax.broadcasted_iota(jnp.int32, (8, F), 1)
    for k, ref in enumerate((weight_norms, update_norms)):
        line = jnp.sum(
            jnp.where(rows == lanes, norms[8 * k : 8 * k + 8, :], 0.0), axis=0, keepdims=True
        )
        ref[...] = line[0, :GROUPS]
    elem_mean[...] = stats[0, :ELEMS]
    scale[...] = stats[1, :1]


def finish(atoms, length):
    shape = jax.ShapeDtypeStruct
    in_vmem = pl.BlockSpec(memory_space=pltpu.VMEM)
    outs = (
        [shape((atoms, F), F32), shape((3, atoms, F), F32), shape((3, atoms), F32)]
        + [shape((ELEMS,), F32), shape((1,), F32)]
        + [shape((length,), F32)] * 4
        + [shape((length,), BF16), shape((GROUPS,), F32), shape((GROUPS,), F32)]
    )
    return pl.pallas_call(
        finish_kernel,
        out_shape=tuple(outs),
        in_specs=[in_vmem] * 9,
        out_specs=(in_vmem,) * len(outs),
        compiler_params=pltpu.CompilerParams(vmem_limit_bytes=62 * 1024 * 1024),
        name="finish",
    )


def body(
    scalars_in,
    vectors_in,
    positions,
    cotan_scalar,
    cotan_vector,
    target_energy,
    forces,
    elements,
    crystal,
    lattice,
    edge_src,
    edge_dst,
    edge_shift,
    edge_count,
    send_rows,
    params,
    first_moment,
    second_moment,
):
    atoms = scalars_in.shape[0]
    edges = edge_src.shape[0]
    cap = send_rows.shape[2]
    halo = 2 * HOPS * cap
    groups = lax.axis_size("atoms") // 4
    length = params.shape[0]
    par, halo_rows, p_halo, goal, stats, src_tiles = gather_all(atoms, cap, groups, length, edges)(
        send_rows,
        params,
        scalars_in,
        vectors_in,
        positions,
        target_energy.reshape(-1, F),
        elements.reshape(-1, F),
        forces,
        edge_src.reshape(-1, F),
    )
    s_two, v_two, gs_own, gv_own, g_halo, gp_own, gp_halo, gpar = layer(atoms, halo, edges)(
        edge_dst,
        edge_count,
        src_tiles.reshape(-1),
        crystal.reshape(-1, F),
        edge_dst.reshape(-1, F),
        edge_shift,
        jnp.transpose(lattice),
        par,
        scalars_in,
        vectors_in,
        positions,
        halo_rows,
        p_halo,
        cotan_scalar,
        cotan_vector,
        goal,
    )
    back, p_back, shares, norms = reduce_all(cap, groups, length)(
        gpar, g_halo, gp_halo, params, first_moment, second_moment
    )
    (
        grad_s,
        grad_v,
        grad_p,
        elem_mean,
        scale,
        grad,
        one_new,
        two_new,
        par_new,
        par_low,
        weight_norms,
        update_norms,
    ) = finish(atoms, length)(
        back, p_back, shares, norms, stats, send_rows, gs_own, gv_own, gp_own
    )
    return (
        s_two,
        v_two,
        grad_s,
        grad_v,
        grad_p,
        elem_mean,
        scale.reshape(()),
        grad,
        one_new,
        two_new,
        par_new,
        par_low,
        weight_norms,
        update_norms,
    )


def solution(mesh):
    joint = ("atoms", "rep")
    in_specs = (
        P(joint, None),
        P(None, joint, None),
        P(None, joint),
        P(joint, None),
        P(None, joint, None),
        P(joint),
        P(None, joint),
        P(joint),
        P(joint),
        P(),
        P(joint),
        P(joint),
        P(None, joint),
        P(joint),
        P(joint, None, None),
        P(joint),
        P(joint),
        P(joint),
    )
    out_specs = (
        P(joint, None),
        P(None, joint, None),
        P(joint, None),
        P(None, joint, None),
        P(None, joint),
        P(),
        P(),
        P(joint),
        P(joint),
        P(joint),
        P(joint),
        P(joint),
        P(),
        P(),
    )
    return jax.shard_map(body, mesh=mesh, in_specs=in_specs, out_specs=out_specs, check_vma=False)
```

```python
import functools

import jax
import jax.numpy as jnp
from jax import lax
from jax.experimental import pallas as pl
from jax.experimental.pallas import tpu as pltpu
from jax.sharding import PartitionSpec as P

F = 128
R = 20
HOPS = 4
ELEMS = 100
STEP = 10
GROUPS = 7

CUTOFF = 5.0
BETA_ONE = 0.9
BETA_TWO = 0.99
RATE = 0.3
DECAY = 0.01
EPSILON = 1e-06

BLOCK = 256
WINDOW = 128
PAIR = 2
LANE_ROWS = 80
SUB = 16
ROWS = 256
F32 = jnp.float32
BF16 = jnp.bfloat16

AT_W1, AT_W2, AT_WF, AT_WM, AT_U1, AT_U2 = 0, 128, 512, 572, 828, 1084
AT_B1, AT_B2, AT_BF, AT_C1, AT_C2, AT_READ, PARAM_ROWS = 1468, 1469, 1472, 1475, 1476, 1479, 1480
PARAM_PAD = PARAM_ROWS + 8
GROUP_ENDS = (128, 512, 572, 828, 1084, 1468)
MESH = pl.DeviceIdType.MESH
SENT = ((3, 7, 2, 6), (1, 5, 0, 4), ())
BATCHES = ((3, 7), (2, 6), (1, 5), (0, 4))


def mm(left, right, contract=(1, 0)):
    return lax.dot_general(
        left, right, (((contract[0],), (contract[1],)), ((), ())), preferred_element_type=F32
    )


def split(value):
    high = value.astype(BF16)
    return high, (value - high.astype(F32)).astype(BF16)


def dot3(left, right, contract=(1, 0)):
    return (
        mm(left[0], right[0], contract)
        + mm(left[1], right[0], contract)
        + mm(left[0], right[1], contract)
    )


def linear(pair, weights):
    both = jnp.concatenate(pair, axis=1)
    return mm(both, weights[0 : 2 * F, :]) + mm(pair[0], weights[2 * F : 3 * F, :])


def back_through(pair, weights):
    return dot3(pair, (weights[0:F, :], weights[2 * F : 3 * F, :]), (1, 1))


def wide_row(ref, start, parts):
    return jnp.concatenate([ref[start + j : start + j + 1, :] for j in range(parts)], axis=1)


def add_row(ref, start, parts, value):
    total = jnp.sum(value, axis=0, keepdims=True)
    for j in range(parts):
        ref[start + j : start + j + 1, :] += total[:, j * F : (j + 1) * F]


def add_matrix(ref, start, parts, value):
    for j in range(parts):
        add_column(ref, start, parts, j, value[:, j * F : (j + 1) * F], value.shape[0])


def sigmoid(value):
    return 1.0 / (1.0 + jnp.exp(-value))


def column(ref, start, parts, j, count=F):
    if parts == 1:
        return ref[start : start + count, :]
    return ref[pl.ds(start + j, count, stride=parts), :]


def add_column(ref, start, parts, j, value, count=F):
    if parts == 1:
        ref[start : start + count, :] += value
    else:
        ref[pl.ds(start + j, count, stride=parts), :] += value


def rows_of(start, count, unit):
    return pl.ds(pl.multiple_of(start, unit), count)


def lay_flat(ref, count):
    return jnp.concatenate([ref[k : k + 1, :] for k in range(count)], axis=1)


def weave(*parts):
    parts = list(parts)
    while parts:
        for part in list(parts):
            try:
                next(part)
            except StopIteration:
                parts.remove(part)


def layer_kernel(
    dst_s,
    count_s,
    src_s,
    crystal,
    dst_v,
    shift_v,
    lat,
    par,
    s_own,
    v_own,
    p_own,
    halo_rows,
    p_halo,
    cot_s,
    cot_v,
    goal,
    s_two,
    v_two,
    gs_own,
    gv_own,
    g_halo,
    gp_own,
    gp_halo,
    gpar,
    tab,
    rows,
    acc,
    stage,
    dtab,
    lane_buf,
    slope_buf,
    inv_buf,
    free_buf,
    turn_buf,
    sums,
    gd,
    gbuf,
    fbuf,
    mbuf,
    ltbuf,
    tbuf,
    wcat,
    wq,
    gwf,
    gpd,
    w1,
    w2,
    wm,
    u1,
    u2,
):
    atoms = s_own.shape[0]
    halo = halo_rows.shape[1]
    blocks_128 = shift_v.shape[1] // F
    ends_buf = stage.at[0 : blocks_128 * 16]
    shift_buf = stage.at[blocks_128 * 16 : blocks_128 * 24]
    place_buf = stage.at[blocks_128 * 24 : blocks_128 * 32]
    s_halo, v_halo = halo_rows.at[0], halo_rows.at[1:4]
    gs_halo, gv_halo = g_halo.at[0], g_halo.at[1:4]
    edges = shift_v.shape[1]
    blocks = edges // BLOCK

    wcat[...] = jnp.zeros_like(wcat)
    wq[...] = jnp.zeros_like(wq)
    gwf[...] = jnp.zeros_like(gwf)
    gpd[...] = jnp.zeros_like(gpd)
    gpar[...] = jnp.zeros_like(gpar)
    sums[...] = jnp.zeros_like(sums)
    for ref, start, parts in ((w1, AT_W1, 1), (w2, AT_W2, 3), (wm, AT_WM, 2), (u2, AT_U2, 3)):
        for j in range(parts):
            high, low = split(column(par, start, parts, j))
            for k, value in enumerate((high, high, low)):
                ref[k * F : (k + 1) * F, j * F : (j + 1) * F] = value
    u1[0 : 2 * F, :], u1[2 * F : 4 * F, :] = split(par[AT_U1 : AT_U1 + 2 * F, :])
    for j in range(3):
        wide = jnp.concatenate(
            [
                column(par, AT_WF, 3, j, R),
                par[AT_BF + j : AT_BF + j + 1, :],
                jnp.zeros((3, F), F32),
            ],
            axis=0,
        )
        high = wide.astype(BF16).astype(F32)
        low = wide - high
        pieces = jnp.concatenate([high, high, low, jnp.zeros((56, F), F32)], axis=0)
        wcat[:, j * F : (j + 1) * F] = pieces.astype(BF16)
        pieces = jnp.concatenate([high, low, jnp.zeros((80, F), F32)], axis=0)
        wq[j * F : (j + 1) * F, :] = jnp.transpose(pieces).astype(BF16)

    names = lay_flat(crystal, atoms // F)
    spots = lax.broadcasted_iota(jnp.int32, (F, atoms), 0)
    for k in range(atoms // F):
        acc[16 * k : 16 * k + 16, :] = jnp.zeros((16, F), F32)

    @pl.loop(0, lat.shape[1] // F)
    def _(step):
        table = lat[:, rows_of(step * F, F, F)]
        high = table.astype(BF16).astype(F32)
        middle = (table - high).astype(BF16).astype(F32)
        gap = jnp.zeros((7, F), F32)
        pieces = jnp.concatenate([high, gap, middle, gap, table - high - middle, gap], axis=0)
        got = mm(pieces.astype(BF16), jnp.where(names - step * F == spots, 1.0, 0.0).astype(BF16))
        got = got[0:16] + got[16:32] + got[32:48]
        for k in range(atoms // F):
            acc[16 * k : 16 * k + 16, :] += got[:, k * F : (k + 1) * F]

    across = jnp.concatenate([acc[16 * k : 16 * k + 16, :] for k in range(atoms // F)], axis=1)
    part = jnp.concatenate([p_own[...], across[0:9], jnp.zeros((4, atoms), F32)], axis=0)
    high = part.astype(BF16).astype(F32)
    middle = (part - high).astype(BF16).astype(F32)
    low = part - high - middle
    dtab[...] = jnp.concatenate([high, middle, low], axis=0).astype(BF16)

    for s_ref, v_ref, p_ref, base, count in (
        (s_own, v_own, p_own, 0, atoms),
        (s_halo, v_halo, p_halo, atoms, halo),
    ):
        place = jnp.concatenate([p_ref[0:3, :], jnp.zeros((F - 3, count), F32)], axis=0)
        tab[pl.ds(base * 8 + 6, count, stride=8), :] = jnp.transpose(place)
        tab[pl.ds(base * 8 + 7, count, stride=8), :] = jnp.zeros((count, F), F32)
        for c in range(3):
            tab[pl.ds(base * 8 + 3 + c, count, stride=8), :] = v_ref[c]

        @pl.loop(0, count // ROWS)
        def _(step):
            first = step * ROWS
            s_pair = split(s_ref[rows_of(first, ROWS, ROWS), :])
            act = linear(s_pair, w1) + par[AT_B1 : AT_B1 + 1, :]
            x = linear(split(act * sigmoid(act)), w2) + wide_row(par, AT_B2, 3)
            for j in range(3):
                tab[pl.ds((base + first) * 8 + j, ROWS, stride=8), :] = x[:, j * F : (j + 1) * F]

    slots = lax.broadcasted_iota(jnp.int32, (WINDOW, BLOCK), 0)
    eight = lax.broadcasted_iota(jnp.int32, (8, 1), 0)
    wide_lane = lax.broadcasted_iota(jnp.int32, (1, F), 1)
    chunks = edges // F
    per = BLOCK // F

    def destinations(i):
        return jnp.concatenate([dst_v[pl.ds(i * per + k, 1), :] for k in range(per)], axis=1)

    def window_range(i):
        return dst_s[i * BLOCK] // WINDOW, dst_s[i * BLOCK + BLOCK - 1] // WINDOW

    def hot(dst, w):
        return jnp.where(dst - w * WINDOW == slots, 1.0, 0.0).astype(BF16)

    def window(w):
        return rows_of(w * WINDOW, WINDOW, WINDOW)

    def lane_chunk(i, k):
        return rows_of((i * per + k) * LANE_ROWS, LANE_ROWS, LANE_ROWS)

    def source(i, j):
        return pl.ds(pl.multiple_of(src_s[i * BLOCK + j], 8), 8)

    def ends_in(i, w):
        got = mm(dtab[:, window(w)], hot(destinations(i), w))
        return got[0:16] + got[16:32] + got[32:48]

    def gather(i):
        for j in range(BLOCK):
            spot = pl.multiple_of(i * (BLOCK * 8), BLOCK * 8) + j * 8
            rows[pl.ds(pl.multiple_of(spot, 8), 8), :] = tab[source(i, j), :]
            if j % 16 == 15:
                yield

    def ends(i):
        got = ends_in(i, window_range(i)[0])
        yield
        for k in range(per):
            chunk = i * per + k
            shift_buf[pl.ds(pl.multiple_of(chunk * 8, 8), 3), :] = shift_v[
                :, rows_of(chunk * F, F, F)
            ].astype(F32)
            ends_buf[rows_of(chunk * 16, 16, 16), :] = got[:, k * F : (k + 1) * F]
            yield

    def places_of(i):
        for k in range(per):
            chunk = i * per + k
            place = rows[pl.ds(chunk * (F * 8) + 6, F, stride=8), :]
            yield
            place_buf[rows_of(chunk * 8, 8, 8), :] = jnp.transpose(place)[0:8]
            yield

    @pl.loop(0, blocks // PAIR)
    def _(step):
        for t in range(PAIR):
            i = step * PAIR + t
            weave(ends(i), places_of(jnp.maximum(i - 1, 0)), gather(i))
            first, last = window_range(i)

            @pl.loop(first + 1, last + 1)
            def _(w):
                more = ends_in(i, w)
                for k in range(per):
                    ends_buf[rows_of((i * per + k) * 16, 16, 16), :] += more[:, k * F : (k + 1) * F]

    weave(places_of(blocks - 1))

    def dense(ref, row, step):
        return ref[pl.ds(row, chunks, stride=step), :]

    def put_row(row, value):
        lane_buf[pl.ds(row, chunks, stride=LANE_ROWS), :] = value

    shift = [dense(shift_buf, k, 8) for k in range(3)]
    rel = [
        dense(place_buf, c, 8)
        + (
            shift[0] * dense(ends_buf, 3 + c, 16)
            + shift[1] * dense(ends_buf, 6 + c, 16)
            + shift[2] * dense(ends_buf, 9 + c, 16)
        )
        - dense(ends_buf, c, 16)
        for c in range(3)
    ]
    square = rel[0] * rel[0] + rel[1] * rel[1] + rel[2] * rel[2]
    dist = jnp.sqrt(jnp.maximum(square, 0.25))
    inv = 1.0 / dist
    inv_buf[...] = inv
    free_buf[...] = jnp.where(square > 0.25, 1.0, 0.0)
    for c in range(3):
        put_row(72 + c, rel[c] * inv)
    put_row(75, dst_v[...].astype(F32))
    nothing = jnp.zeros((chunks, F), F32)
    for row in (21, 22, 23, 45, 46, 47, 69, 70, 71, 76, 77, 78, 79):
        put_row(row, nothing)
    for row in (21, 22, 23):
        slope_buf[pl.ds(row, chunks, stride=24), :] = nothing
    angle = dist * (jnp.pi / CUTOFF)
    sin_one, cos_one = jnp.sin(angle), jnp.cos(angle)
    place = lax.broadcasted_iota(jnp.int32, (chunks, F), 0) * F + lax.broadcasted_iota(
        jnp.int32, (chunks, F), 1
    )
    inside = (dist < CUTOFF) & (place < count_s[0])
    envelope = jnp.where(inside, 0.5 * (cos_one + 1.0), 0.0)
    fall = jnp.where(inside, (-0.5 * jnp.pi / CUTOFF) * sin_one, 0.0)
    sin_n, cos_n = sin_one, cos_one
    for n in range(R + 1):
        if n < R:
            radial = sin_n * inv
            slope = (((n + 1) * jnp.pi / CUTOFF) * cos_n - radial) * inv
            scaled = envelope * radial
            change = fall * radial + envelope * slope
            sin_n, cos_n = sin_n * cos_one + cos_n * sin_one, cos_n * cos_one - sin_n * sin_one
        else:
            scaled, change = envelope, fall
        high = scaled.astype(BF16).astype(F32)
        put_row(n, high)
        put_row(24 + n, scaled - high)
        put_row(48 + n, high)
        slope_buf[pl.ds(n, chunks, stride=24), :] = change

    def comp(i, k, sub):
        return pl.ds(i * (BLOCK * 8) + sub * (SUB * 8) + k, SUB, stride=8)

    def filters(i, t):
        for k in range(per):
            full = jnp.concatenate(
                [lane_buf[lane_chunk(i, k), :], jnp.zeros((F - LANE_ROWS, F), F32)], axis=0
            )
            ltbuf[t, k * F : (k + 1) * F, :] = jnp.transpose(full)
            yield
        fbuf[t] = mm(ltbuf[t].astype(BF16), wcat[...])
        yield

    def messages(i, t):
        for sub in range(BLOCK // SUB):
            at = slice(sub * SUB, (sub + 1) * SUB)
            m1, m2, m3 = [
                rows[comp(i, j, sub), :] * fbuf[t, at, j * F : (j + 1) * F] for j in range(3)
            ]
            out = [m1]
            for c in range(3):
                out.append(m2 * ltbuf[t, at, 72 + c : 73 + c] + m3 * rows[comp(i, 3 + c, sub), :])
            for k in range(4):
                high, low = split(out[k])
                mbuf[t, at, k * F : (k + 1) * F] = high
                mbuf[t, at, (4 + k) * F : (5 + k) * F] = low
            yield

    def collect(i, t, w):
        pick = hot(destinations(i), w)
        for k in range(2):
            of = slice(k * 2 * F, (k + 1) * 2 * F)
            more = slice((k + 2) * 2 * F, (k + 3) * 2 * F)
            sums[window(w), of] += mm(pick, mbuf[t, :, of]) + mm(pick, mbuf[t, :, more])
            yield

    def collect_more(i, t):
        first, last = window_range(i)

        @pl.loop(first + 1, last + 1)
        def _(w):
            weave(collect(i, t, w))

    mbuf[...] = jnp.zeros_like(mbuf)
    weave(filters(0, 0))

    @pl.loop(0, blocks // PAIR)
    def _(step):
        for t in range(PAIR):
            i = step * PAIR + t
            before = jnp.maximum(i - 1, 0)
            weave(
                filters(jnp.minimum(i + 1, blocks - 1), 1 - t),
                collect(before, 1 - t, window_range(before)[0]),
                messages(i, t),
            )
            collect_more(before, 1 - t)

    weave(collect(blocks - 1, PAIR - 1, window_range(blocks - 1)[0]))
    collect_more(blocks - 1, PAIR - 1)

    @pl.loop(0, atoms // ROWS)
    def _(step):
        at = rows_of(step * ROWS, ROWS, ROWS)
        s_one = s_own[at, :] + sums[at, 0:F]
        v_one = [v_own[c, at, :] + sums[at, (c + 1) * F : (c + 2) * F] for c in range(3)]
        v_pair = [split(v) for v in v_one]
        mixed = [linear(v, wm) for v in v_pair]
        v_lin = [m[:, :F] for m in mixed]
        w_lin = [m[:, F:] for m in mixed]
        size = jnp.sqrt(v_lin[0] * v_lin[0] + v_lin[1] * v_lin[1] + v_lin[2] * v_lin[2] + 1.0)
        s_pair = split(jnp.concatenate([s_one, size], axis=1))
        u1_pair = (u1[0 : 2 * F, :], u1[2 * F : 4 * F, :])
        act = dot3(s_pair, u1_pair) + par[AT_C1 : AT_C1 + 1, :]
        gate = sigmoid(act)
        hidden = split(act * gate)
        gating = linear(hidden, u2) + wide_row(par, AT_C2, 3)
        a1, a2, a3 = [gating[:, j * F : (j + 1) * F] for j in range(3)]
        inner = v_lin[0] * w_lin[0] + v_lin[1] * w_lin[1] + v_lin[2] * w_lin[2]
        s_out = s_one + a3 + a2 * inner
        s_two[at, :] = s_out
        read = par[AT_READ : AT_READ + 1, :]
        out_pair = split(s_out)
        energy = dot3(split(jnp.broadcast_to(read, (8, F))), out_pair, (1, 1))
        error = energy - goal[:, at]
        error_col = jnp.transpose(error)[:, 0:1]
        gpar[AT_READ : AT_READ + 1, :] += dot3(split(error), out_pair)[0:1]
        gs = cot_s[at, :] + error_col * read
        gv = []
        for c in range(3):
            v_two[c, at, :] = v_one[c] + a1 * w_lin[c]
            gv.append(cot_v[c, at, :])
        ga = [gv[0] * w_lin[0] + gv[1] * w_lin[1] + gv[2] * w_lin[2], gs * inner, gs]
        g_inner = gs * a2
        ga = jnp.concatenate(ga, axis=1)
        ga_pair = split(ga)
        add_matrix(gpar, AT_U2, 3, dot3(hidden, ga_pair, (0, 0)))
        add_row(gpar, AT_C2, 3, ga)
        g_act = back_through(ga_pair, u2) * (gate * (1.0 + act * (1.0 - gate)))
        g_act_pair = split(g_act)
        gpar[AT_U1 : AT_U1 + 2 * F, :] += dot3(s_pair, g_act_pair, (0, 0))
        add_row(gpar, AT_C1, 1, g_act)
        g_both = dot3(g_act_pair, u1_pair, (1, 1))
        g_s_one = gs + g_both[:, :F]
        g_size = g_both[:, F:] / size
        gs_own[at, :] = g_s_one
        down = [g_s_one]
        for c in range(3):
            g_mixed = split(
                jnp.concatenate(
                    [
                        g_inner * w_lin[c] + g_size * v_lin[c],
                        a1 * gv[c] + g_inner * v_lin[c],
                    ],
                    axis=1,
                )
            )
            add_matrix(gpar, AT_WM, 2, dot3(v_pair[c], g_mixed, (0, 0)))
            g_v_one = gv[c] + back_through(g_mixed, wm)
            gv_own[c, at, :] = g_v_one
            down.append(g_v_one)
        for k in range(4):
            high, low = split(down[k])
            for part in range(ROWS // WINDOW):
                to = (step * (ROWS // WINDOW) + part) * (2 * WINDOW)
                of = slice(part * WINDOW, (part + 1) * WINDOW)
                gd[rows_of(to, WINDOW, WINDOW), k * F : (k + 1) * F] = high[of]
                gd[rows_of(to + WINDOW, WINDOW, WINDOW), k * F : (k + 1) * F] = low[of]

    twice = (lax.broadcasted_iota(jnp.int32, (1, 2 * WINDOW), 1) % WINDOW).astype(F32)
    for ref in (tab, acc, stage, mbuf, tbuf, turn_buf):
        ref[...] = jnp.zeros_like(ref)

    def collect_places(i, t, w):
        g_rel = turn_buf[t]
        high = g_rel.astype(BF16).astype(F32)
        middle = (g_rel - high).astype(BF16).astype(F32)
        pieces = jnp.concatenate(
            [high, middle, g_rel - high - middle, jnp.zeros_like(g_rel)], axis=0
        )
        got = mm(pieces.astype(BF16), hot(destinations(i), w), (1, 1))
        gpd[:, window(w)] += got[0:8] + got[8:16] + got[16:24]

    def fetch(t, w):
        near = ltbuf[t, :, 75:76] - (w * WINDOW).astype(F32)
        return mm(
            jnp.where(near == twice, 1.0, 0.0).astype(BF16),
            gd[rows_of(w * 2 * WINDOW, 2 * WINDOW, 2 * WINDOW), :],
        )

    def prepare(i, t):
        yield from filters(i, t)
        gbuf[t] = fetch(t, window_range(i)[0])
        yield

    def into_sources(i, t, one, two):
        to = (source(i, one), source(i, two))
        held = [(t * BLOCK + spot) * 8 for spot in (one, two)]
        first = tab[to[0], :] + stage[held[0] : held[0] + 8, :]
        second = acc[to[1], :] + stage[held[1] : held[1] + 8, :]
        tab[to[0], :] = first
        acc[to[1], :] = second

    def spread(i, t, earlier):
        for sub in range(BLOCK // SUB):
            at = slice(sub * SUB, (sub + 1) * SUB)
            for j in range(SUB // 2):
                into_sources(earlier, t, sub * SUB + j, sub * SUB + SUB // 2 + j)
                if j % 4 == 3:
                    yield
            to = [pl.ds(t * (BLOCK * 8) + sub * (SUB * 8) + k, SUB, stride=8) for k in range(6)]
            g_s = gbuf[t, at, 0:F]
            g_v = [gbuf[t, at, (c + 1) * F : (c + 2) * F] for c in range(3)]
            x = [rows[comp(i, j, sub), :] for j in range(3)]
            v = [rows[comp(i, 3 + c, sub), :] for c in range(3)]
            f = [fbuf[t, at, j * F : (j + 1) * F] for j in range(3)]
            u = [ltbuf[t, at, 72 + c : 73 + c] for c in range(3)]
            g_m = [
                g_s,
                g_v[0] * u[0] + g_v[1] * u[1] + g_v[2] * u[2],
                g_v[0] * v[0] + g_v[1] * v[1] + g_v[2] * v[2],
            ]
            m2 = x[1] * f[1]
            m3 = x[2] * f[2]
            turn = jnp.zeros((SUB, F), F32)
            for c in range(3):
                total = jnp.sum(g_v[c] * m2, axis=1, keepdims=True)
                turn = jnp.where(wide_lane == 48 + c, total, turn)
                stage[to[3 + c], :] = g_v[c] * m3
            tbuf[t, at, :] = turn
            for j in range(3):
                high, low = split(g_m[j] * x[j])
                mbuf[t, at, j * F : (j + 1) * F] = high
                mbuf[t, at, (3 + j) * F : (4 + j) * F] = low
                stage[to[j], :] = g_m[j] * f[j]
            yield

    def settle(i, t):
        h_high, h_low = mbuf[t, :, : 3 * F], mbuf[t, :, 3 * F : 6 * F]
        back = mm(h_high, wq[...]) + mm(h_low, wq[...]) + tbuf[t]
        yield
        back = jnp.transpose(back)
        yield
        pieces = jnp.concatenate(
            [lane_buf[lane_chunk(i, k), :][0:48] for k in range(per)], axis=1
        ).astype(BF16)
        gwf[...] += mm(pieces, h_high) + mm(pieces, h_low)
        yield
        slope = jnp.concatenate(
            [slope_buf[rows_of((i * per + k) * 24, 24, 24), :] for k in range(per)], axis=1
        )
        g_dist = jnp.sum((back[0:24] + back[24:48]) * slope, axis=0, keepdims=True)
        g_unit = back[48:56]
        unit = jnp.concatenate([lane_buf[lane_chunk(i, k), :][72:80] for k in range(per)], axis=1)
        unit = jnp.where(eight < 3, unit, 0.0)
        inv, free = [
            jnp.concatenate([ref[pl.ds(i * per + k, 1), :] for k in range(per)], axis=1)
            for ref in (inv_buf, free_buf)
        ]
        yield
        along = jnp.sum(g_unit * unit, axis=0, keepdims=True)
        g_rel = g_unit * inv + (g_dist - along * inv) * free * unit
        turn_buf[t] = g_rel
        yield
        stage[pl.ds(t * (BLOCK * 8) + 6, BLOCK, stride=8), :] = jnp.transpose(
            jnp.concatenate([g_rel, jnp.zeros((F - 8, BLOCK), F32)], axis=0)
        )
        yield
        collect_places(i, t, window_range(i)[0])
        yield

    def prepare_more(i, t):
        first, last = window_range(i)

        @pl.loop(first + 1, last + 1)
        def _(w):
            gbuf[t] += fetch(t, w)

    def settle_more(i, t):
        first, last = window_range(i)

        @pl.loop(first + 1, last + 1)
        def _(w):
            collect_places(i, t, w)

    weave(prepare(0, 0))
    prepare_more(0, 0)

    @pl.loop(0, blocks // PAIR)
    def _(step):
        for t in range(PAIR):
            i = step * PAIR + t
            before, after = jnp.maximum(i - 1, 0), jnp.minimum(i + 1, blocks - 1)
            weave(prepare(after, 1 - t), settle(before, 1 - t), spread(i, t, jnp.maximum(i - 2, 0)))
            prepare_more(after, 1 - t)
            settle_more(before, 1 - t)

    weave(settle(blocks - 1, PAIR - 1))
    settle_more(blocks - 1, PAIR - 1)
    for t in range(PAIR):
        for j in range(BLOCK // 2):
            into_sources(blocks - PAIR + t, t, j, BLOCK // 2 + j)

    for j in range(3):
        total = gwf[0:24, j * F : (j + 1) * F] + gwf[24:48, j * F : (j + 1) * F]
        add_column(gpar, AT_WF, 3, j, total[0:R], R)
        gpar[AT_BF + j : AT_BF + j + 1, :] = total[R : R + 1]

    for s_ref, gs_ref, gv_ref, gp_ref, base, count in (
        (s_own, gs_own, gv_own, gp_own, 0, atoms),
        (s_halo, gs_halo, gv_halo, gp_halo, atoms, halo),
    ):
        own = base == 0
        for k in range(0, count, ROWS):
            at = pl.ds((base + k) * 8 + 6, ROWS, stride=8)
            place = jnp.transpose(tab[at, :] + acc[at, :])[0:8]
            if own:
                place = place - gpd[:, k : k + ROWS]
            gp_ref[:, k : k + ROWS] = place

        @pl.loop(0, count // ROWS)
        def _(step):
            first = step * ROWS
            to = rows_of(first, ROWS, ROWS)

            def gathered(k):
                at = pl.ds((base + first) * 8 + k, ROWS, stride=8)
                return tab[at, :] + acc[at, :]

            for c in range(3):
                if own:
                    gv_ref[c, to, :] += gathered(3 + c)
                else:
                    gv_ref[c, to, :] = gathered(3 + c)
            s_pair = split(s_ref[to, :])
            act = linear(s_pair, w1) + par[AT_B1 : AT_B1 + 1, :]
            gate = sigmoid(act)
            hidden = split(act * gate)
            g_x = jnp.concatenate([gathered(j) for j in range(3)], axis=1)
            g_pair = split(g_x)
            add_matrix(gpar, AT_W2, 3, dot3(hidden, g_pair, (0, 0)))
            add_row(gpar, AT_B2, 3, g_x)
            g_act = back_through(g_pair, w2) * (gate * (1.0 + act * (1.0 - gate)))
            g_act_pair = split(g_act)
            add_matrix(gpar, AT_W1, 1, dot3(s_pair, g_act_pair, (0, 0)))
            add_row(gpar, AT_B1, 1, g_act)
            g_s = back_through(g_act_pair, w1)
            if own:
                gs_ref[to, :] += g_s
            else:
                gs_ref[to, :] = g_s


def layer(atoms, halo, edges):
    shape = jax.ShapeDtypeStruct
    total = atoms + halo
    in_vmem = pl.BlockSpec(memory_space=pltpu.VMEM)
    in_smem = pl.BlockSpec(memory_space=pltpu.SMEM)
    outs = (
        shape((atoms, F), F32),
        shape((3, atoms, F), F32),
        shape((atoms, F), F32),
        shape((3, atoms, F), F32),
        shape((4, halo, F), F32),
        shape((8, atoms), F32),
        shape((8, halo), F32),
        shape((PARAM_PAD, F), F32),
    )
    scratch = [
        pltpu.VMEM((total * 8, F), F32),
        pltpu.VMEM((edges * 8, F), F32),
        pltpu.VMEM((total * 8, F), F32),
        pltpu.VMEM((PAIR * BLOCK * 8, F), F32),
        pltpu.VMEM((48, atoms), BF16),
        pltpu.VMEM((edges // F * LANE_ROWS, F), F32),
        pltpu.VMEM((edges // F * 24, F), F32),
        pltpu.VMEM((edges // F, F), F32),
        pltpu.VMEM((edges // F, F), F32),
        pltpu.VMEM((PAIR, 8, BLOCK), F32),
        pltpu.VMEM((atoms, 4 * F), F32),
        pltpu.VMEM((2 * atoms, 4 * F), BF16),
        pltpu.VMEM((PAIR, BLOCK, 4 * F), F32),
        pltpu.VMEM((PAIR, BLOCK, 3 * F), F32),
        pltpu.VMEM((PAIR, BLOCK, 8 * F), BF16),
        pltpu.VMEM((PAIR, BLOCK, F), F32),
        pltpu.VMEM((PAIR, BLOCK, F), F32),
        pltpu.VMEM((F, 3 * F), BF16),
        pltpu.VMEM((3 * F, F), BF16),
        pltpu.VMEM((48, 3 * F), F32),
        pltpu.VMEM((8, atoms), F32),
        pltpu.VMEM((3 * F, F), BF16),
        pltpu.VMEM((3 * F, 3 * F), BF16),
        pltpu.VMEM((3 * F, 2 * F), BF16),
        pltpu.VMEM((4 * F, F), BF16),
        pltpu.VMEM((3 * F, 3 * F), BF16),
    ]
    return pl.pallas_call(
        layer_kernel,
        out_shape=outs,
        in_specs=[in_smem] * 3 + [in_vmem] * 13,
        out_specs=(in_vmem,) * len(outs),
        scratch_shapes=scratch,
        compiler_params=pltpu.CompilerParams(vmem_limit_bytes=63 * 1024 * 1024),
        name="layer",
    )


def hop_offset(j):
    return j + 1 if j < HOPS else HOPS - 1 - j


class Place:
    def __init__(self):
        self.chips = lax.axis_size("atoms")
        self.cores = lax.axis_size("rep")
        self.count = self.chips * self.cores
        self.groups = self.chips // 4
        chip = lax.axis_index("atoms")
        self.core = lax.axis_index("rep")
        self.joint = chip * self.cores + self.core
        self.group = chip // 4
        self.quarter = chip % 4
        self.mate = 1 - self.core

    def other_groups(self):
        return [lax.rem(self.group + k, self.groups) for k in range(1, self.groups)]

    def other_quarters(self):
        return [lax.rem(self.quarter + k, 4) for k in range(1, 4)]

    def in_group(self, group):
        return (group * 4 + self.quarter, self.core)

    def in_quarter(self, quarter):
        return (self.group * 4 + quarter, self.core)

    def beside(self):
        return (self.group * 4 + self.quarter, self.mate)

    def hop(self, by):
        other = self.joint + by
        exists = (other >= 0) & (other < self.count)
        other = jnp.clip(other, 0, self.count - 1)
        return exists, (other // self.cores, other % self.cores)

    def others_of_group(self):
        own = self.quarter * self.cores + self.core
        places = [lax.rem(own + k, 4 * self.cores) for k in range(1, 4 * self.cores)]
        return [(o, (self.group * 4 + o // self.cores, o % self.cores)) for o in places]

    def greet(self):
        barrier = pltpu.get_barrier_semaphore()
        fixed = [self.in_group(g) for g in self.other_groups()]
        fixed += [device for _, device in self.others_of_group()]
        for device in fixed:
            pl.semaphore_signal(barrier, inc=1, device_id=device, device_id_type=MESH)
        hops = [self.hop(hop_offset(j)) for j in range(2 * HOPS)]
        expected = jnp.int32(len(fixed))
        for exists, device in hops:
            expected = expected + jnp.where(exists, 1, 0)

            @pl.when(exists)
            def _():
                pl.semaphore_signal(barrier, inc=1, device_id=device, device_id_type=MESH)

        return expected


def send(src, dst, send_sem, recv_sem, device):
    return pltpu.make_async_remote_copy(
        src_ref=src,
        dst_ref=dst,
        send_sem=send_sem,
        recv_sem=recv_sem,
        device_id=device,
        device_id_type=MESH,
    )


def start_all(copies):
    for copy in copies:
        copy.start()
    return copies


def wait_sent(copies):
    for copy in copies:
        copy.wait_send()


def window_rows(length):
    return -(-((length + F - 1) // F + 1) // 8) * 8


class SmallSum:
    def __init__(self, place, slots_a, slots_b, sends, recvs):
        self.place = place
        self.slots = (slots_a, slots_b)
        self.sends, self.recvs = sends, recvs
        self.sent = []

    def partners(self, phase):
        p = self.place
        if phase == 0:
            return p.quarter * p.cores + p.core, p.others_of_group(), 0
        return p.group, [(g, p.in_group(g)) for g in p.other_groups()], 4 * p.cores

    def start(self, phase, value):
        slots = self.slots[phase]
        mine, others, base = self.partners(phase)
        slots[mine] = value
        for k, (_, device) in enumerate(others):
            spot = slots.at[mine]
            copy = send(spot, spot, self.sends.at[base + k], self.recvs.at[base + mine], device)
            copy.start()
            self.sent.append(copy)

    def finish(self, phase):
        slots = self.slots[phase]
        _, others, base = self.partners(phase)
        for o, device in others:
            spot = slots.at[o]
            send(spot, spot, self.sends.at[base], self.recvs.at[base + o], device).wait_recv()
        total = slots[0]
        for k in range(1, slots.shape[0]):
            total = total + slots[k]
        return total

    def done(self):
        wait_sent(self.sent)


def small_scratch(groups, rows):
    count = groups + 8
    return [
        pltpu.VMEM((8, rows, F), F32),
        pltpu.VMEM((groups, rows, F), F32),
        pltpu.SemaphoreType.DMA((count,)),
        pltpu.SemaphoreType.DMA((count,)),
    ]


def from_flat(ref, rows):
    length = ref.shape[0]
    whole, rest = length // F, length % F
    lines = [ref[pl.ds(r * F, F)].reshape(1, F) for r in range(whole)]
    if rest:
        last = ref[pl.ds(whole * F, rest)].reshape(1, rest)
        lines.append(jnp.concatenate([last, jnp.zeros((1, F - rest), F32)], axis=1))
    lines.append(jnp.zeros((rows - len(lines), F), F32))
    return jnp.concatenate(lines, axis=0)


def to_flat(ref, value):
    length = ref.shape[0]
    whole, rest = length // F, length % F
    for r in range(whole):
        ref[pl.ds(r * F, F)] = value[r]
    if rest:
        ref[pl.ds(whole * F, rest)] = value[whole, :rest]


def gather_kernel(
    send_s,
    par_in,
    s_own,
    v_own,
    p_own,
    energy,
    elements,
    forces,
    edge_src,
    par,
    halo_rows,
    p_halo,
    goal,
    stats,
    src_tiles,
    slots,
    pack,
    places,
    p_out,
    p_in,
    zeros,
    ag_send,
    ag_recv,
    row_send,
    row_recv,
    place_send,
    place_recv,
    zero_sem,
    *small,
    length,
):
    here = Place()
    atoms = s_own.shape[0]
    cap = halo_rows.shape[1] // (2 * HOPS)
    wide = slots.shape[3]
    expected = here.greet()
    sums = SmallSum(here, *small)

    offset = lax.rem(here.joint * length, F)
    lane = lax.broadcasted_iota(jnp.int32, (1, F), 1)
    turned = pltpu.roll(from_flat(par_in, wide), offset, 1)
    above = jnp.concatenate([jnp.zeros((1, F), F32), turned[: wide - 1]], axis=0)
    mine = slots.at[here.group, here.quarter, here.core]
    mine[...] = jnp.where(lane < offset, above, turned)
    src_tiles[...] = edge_src[...] * 8

    count = atoms // F
    energy_row, element_row = lay_flat(energy, count), lay_flat(elements, count)
    hot = jnp.where(
        element_row == lax.broadcasted_iota(jnp.int32, (F, atoms), 0), 1.0, 0.0
    ).astype(BF16)
    high = energy_row.astype(BF16).astype(F32)
    middle = (energy_row - high).astype(BF16).astype(F32)
    eight = lax.broadcasted_iota(jnp.int32, (8, 1), 0)
    left = jnp.where(
        eight == 0,
        high,
        jnp.where(
            eight == 1, middle, jnp.where(eight == 2, energy_row - high - middle, jnp.where(eight == 3, 1.0, 0.0))
        ),
    )
    found = mm(left.astype(BF16), hot, (1, 1))
    squares = jnp.sum(forces[...] * forces[...], axis=0, keepdims=True)
    square = squares[:, 0:F]
    for k in range(1, count):
        square = square + squares[:, k * F : (k + 1) * F]
    tile = jnp.where(
        eight == 0,
        found[0:1] + found[1:2] + found[2:3],
        jnp.where(eight == 1, found[3:4], jnp.where(eight == 2, square, 0.0)),
    )
    places[...] = jnp.transpose(
        jnp.concatenate([p_own[...], jnp.zeros((F - 3, atoms), F32)], axis=0)
    )
    zeros[...] = jnp.zeros_like(zeros)
    hops = range(2 * HOPS)
    for j in hops:

        @pl.loop(0, cap // 16)
        def _(step):
            for k in range(16):
                r = step * 16 + k
                t = send_s[0, j, r]
                r = j * cap + r
                pack[0, pl.ds(r, 1), :] = s_own[pl.ds(t, 1), :]
                for c in range(3):
                    pack[1 + c, pl.ds(r, 1), :] = v_own[c, pl.ds(t, 1), :]
                p_out[pl.ds(r, 1), :] = places[pl.ds(t, 1), :]

    for j in range(0, 2 * HOPS, 2):
        pair = slice(j * cap, (j + 2) * cap)
        p_in[2 * HOPS + j // 2] = jnp.transpose(p_out[pair, :])[0:8]

    pl.semaphore_wait(pltpu.get_barrier_semaphore(), expected)
    first = start_all(
        [
            send(mine, mine, ag_send.at[k], ag_recv.at[here.group], here.in_group(g))
            for k, g in enumerate(here.other_groups())
        ]
    )
    sums.start(0, tile)
    row_copies, place_copies = [], []

    def give(some):
        for j in some:
            exists, device = here.hop(hop_offset(j))
            block = pl.ds(j * cap, cap)
            rows_copy = send(
                pack.at[:, block], halo_rows.at[:, block], row_send.at[j], row_recv.at[j], device
            )
            place_copy = send(
                p_in.at[2 * HOPS + j // 2], p_in.at[j], place_send.at[j], place_recv.at[j], device
            )
            row_copies.append((exists, rows_copy))
            place_copies.append((exists, place_copy))

            @pl.when(exists)
            def _():
                rows_copy.start()
                place_copy.start()

    give(SENT[0])
    for j in hops:
        known, device = here.hop(-hop_offset(j))

        @pl.when(jnp.logical_not(known))
        def _():
            p_in[j] = jnp.zeros((8, F), F32)
            fill = pltpu.make_async_copy(
                zeros, halo_rows.at[:, pl.ds(j * cap, cap)], zero_sem.at[j]
            )
            fill.start()
            fill.wait()

    for g in here.other_groups():
        spot = slots.at[g, here.quarter, here.core]
        send(spot, spot, ag_send.at[0], ag_recv.at[g], here.beside()).wait_recv()
    base = here.groups
    line = slots.at[:, here.quarter, here.core]
    second = start_all(
        [
            send(line, line, ag_send.at[base + k], ag_recv.at[base + here.quarter], here.in_quarter(q))
            for k, q in enumerate(here.other_quarters())
        ]
    )
    third = [
        send(
            line, line, ag_send.at[base + 4], ag_recv.at[base + 4 + here.quarter], here.beside()
        )
    ]
    third[0].start()
    give(SENT[1])
    sums.start(1, sums.finish(0))
    for k, q in enumerate(here.other_quarters()):
        line = slots.at[:, q, here.core]
        send(line, line, ag_send.at[0], ag_recv.at[base + q], here.beside()).wait_recv()
        copy = send(
            line, line, ag_send.at[base + 5 + k], ag_recv.at[base + 4 + q], here.beside()
        )
        copy.start()
        third.append(copy)
    give(SENT[2])
    for q in range(4):
        line = slots.at[:, q, here.mate]
        send(line, line, ag_send.at[0], ag_recv.at[base + 4 + q], here.beside()).wait_recv()

    par[...] = jnp.zeros_like(par)
    for p in range(here.count):
        row = p * length // F
        chip, core = p // here.cores, p % here.cores
        take = min(wide, PARAM_PAD - row)
        par[row : row + take, :] += slots[chip // 4, chip % 4, core, 0:take, :]

    total = sums.finish(1)
    mean = total[0:1] / jnp.maximum(total[1:2], 1.0)
    whole = jnp.sum(total[2:3], axis=1, keepdims=True)
    scale = jnp.sqrt(whole / (3.0 * atoms * here.count) + 1e-06)
    high = mean.astype(BF16).astype(F32)
    middle = (mean - high).astype(BF16).astype(F32)
    left = jnp.where(
        eight == 0,
        high,
        jnp.where(eight == 1, middle, jnp.where(eight == 2, mean - high - middle, 0.0)),
    )
    found = mm(left.astype(BF16), hot)
    goal[...] = (energy_row - (found[0:1] + found[1:2] + found[2:3])) / scale
    stats[...] = jnp.where(eight == 0, mean, jnp.where(eight == 1, scale, 0.0))

    for j in hops:
        known, device = here.hop(-hop_offset(j))

        @pl.when(known)
        def _():
            block = pl.ds(j * cap, cap)
            send(
                pack.at[:, block], halo_rows.at[:, block], row_send.at[j], row_recv.at[j], device
            ).wait_recv()
            send(p_in.at[j], p_in.at[j], place_send.at[j], place_recv.at[j], device).wait_recv()

    low_half = lane < cap
    for j in range(0, 2 * HOPS, 2):
        p_halo[:, j * cap : (j + 2) * cap] = jnp.where(low_half, p_in[j], p_in[j + 1])
    for exists, copy in row_copies + place_copies:

        @pl.when(exists)
        def _():
            copy.wait_send()

    wait_sent(first + second + third)
    sums.done()


def gather_all(atoms, cap, groups, length, edges):
    shape = jax.ShapeDtypeStruct
    halo = 2 * HOPS * cap
    wide = window_rows(length)
    in_vmem = pl.BlockSpec(memory_space=pltpu.VMEM)
    in_smem = pl.BlockSpec(memory_space=pltpu.SMEM)
    return pl.pallas_call(
        functools.partial(gather_kernel, length=length),
        out_shape=(
            shape((PARAM_PAD, F), F32),
            shape((4, halo, F), F32),
            shape((8, halo), F32),
            shape((1, atoms), F32),
            shape((8, F), F32),
            shape((edges // F, F), jnp.int32),
        ),
        in_specs=[in_smem] + [in_vmem] * 8,
        out_specs=(in_vmem, pl.BlockSpec(memory_space=pl.ANY)) + (in_vmem,) * 4,
        scratch_shapes=[
            pltpu.VMEM((groups, 4, 2, wide, F), F32),
            pltpu.VMEM((4, halo, F), F32),
            pltpu.VMEM((atoms, F), F32),
            pltpu.VMEM((halo, F), F32),
            pltpu.VMEM((3 * HOPS, 8, F), F32),
            pltpu.VMEM((4, cap, F), F32),
            pltpu.SemaphoreType.DMA((groups + 8,)),
            pltpu.SemaphoreType.DMA((groups + 8,)),
            pltpu.SemaphoreType.DMA((2 * HOPS,)),
            pltpu.SemaphoreType.DMA((2 * HOPS,)),
            pltpu.SemaphoreType.DMA((2 * HOPS,)),
            pltpu.SemaphoreType.DMA((2 * HOPS,)),
            pltpu.SemaphoreType.DMA((2 * HOPS,)),
        ]
        + small_scratch(groups, 8),
        compiler_params=pltpu.CompilerParams(
            collective_id=0, has_side_effects=True, vmem_limit_bytes=62 * 1024 * 1024
        ),
        name="gather_inputs",
    )


def reduce_kernel(
    gpar,
    g_halo,
    gp_halo,
    par,
    one,
    two,
    back,
    p_back,
    shares,
    norms,
    slots,
    pair_in,
    line_in,
    spot_in,
    turn,
    zeros,
    p_in,
    rs_send,
    rs_recv,
    row_send,
    row_recv,
    place_send,
    place_recv,
    zero_sem,
    *small,
    length,
):
    here = Place()
    cap = back.shape[1] // (2 * HOPS)
    wide = slots.shape[3]
    expected = here.greet()
    sums = SmallSum(here, *small)

    for p in range(here.count):
        row = p * length // F
        chip, core = p // here.cores, p % here.cores
        take = min(wide, PARAM_PAD - row)
        slots[chip // 4, chip % 4, core, 0:take, :] = gpar[row : row + take, :]
    old, m_one, m_two = [from_flat(ref, wide) for ref in (par, one, two)]
    zeros[...] = jnp.zeros_like(zeros)
    order = here.other_quarters() + [here.quarter]
    base = here.groups
    pl.semaphore_wait(pltpu.get_barrier_semaphore(), expected)
    third = start_all(
        [
            send(
                slots.at[:, q, here.mate],
                pair_in.at[:, q],
                rs_send.at[base + 4 + k],
                rs_recv.at[base + 4 + q],
                here.beside(),
            )
            for k, q in enumerate(order)
        ]
    )

    second = []
    for k, q in enumerate(order):
        line = pair_in.at[:, q]
        send(line, line, rs_send.at[0], rs_recv.at[base + 4 + q], here.beside()).wait_recv()
        slots[:, q, here.core] += pair_in[:, q]
        if k < 3:
            copy = send(
                slots.at[:, q, here.core],
                line_in.at[here.quarter],
                rs_send.at[base + k],
                rs_recv.at[base + here.quarter],
                here.in_quarter(q),
            )
            copy.start()
            second.append(copy)

    hops = range(2 * HOPS)
    copies = []

    def give_back(some):
        for j in some:
            exists, device = here.hop(-hop_offset(j))
            block = pl.ds(j * cap, cap)
            tile = pl.ds((j // 2) * F, F)
            rows_copy = send(
                g_halo.at[:, block], back.at[:, block], row_send.at[j], row_recv.at[j], device
            )
            place_copy = send(
                gp_halo.at[:, tile], p_in.at[j], place_send.at[j], place_recv.at[j], device
            )
            copies.extend([(exists, rows_copy), (exists, place_copy)])

            @pl.when(exists)
            def _():
                rows_copy.start()
                place_copy.start()

    give_back(BATCHES[0])
    for j in hops:
        known, device = here.hop(hop_offset(j))

        @pl.when(jnp.logical_not(known))
        def _():
            p_in[j] = jnp.zeros((8, F), F32)
            fill = pltpu.make_async_copy(zeros, back.at[:, pl.ds(j * cap, cap)], zero_sem.at[j])
            fill.start()
            fill.wait()

    for q in here.other_quarters():
        line = line_in.at[q]
        send(line, line, rs_send.at[0], rs_recv.at[base + q], here.beside()).wait_recv()
        slots[:, here.quarter, here.core] += line_in[q]
    first = start_all(
        [
            send(
                slots.at[g, here.quarter, here.core],
                spot_in.at[here.group],
                rs_send.at[k],
                rs_recv.at[here.group],
                here.in_group(g),
            )
            for k, g in enumerate(here.other_groups())
        ]
    )
    give_back(BATCHES[1])
    total = slots[here.group, here.quarter, here.core]
    for g in here.other_groups():
        spot = spot_in.at[g]
        send(spot, spot, rs_send.at[0], rs_recv.at[g], here.beside()).wait_recv()
        total = total + spot_in[g]

    offset = lax.rem(here.joint * length, F)
    lane = lax.broadcasted_iota(jnp.int32, (1, F), 1)
    turn[0:wide, :] = pltpu.roll(total, lax.rem(F - offset, F), 1)
    turn[wide : wide + 8, :] = jnp.zeros((8, F), F32)
    place = lax.broadcasted_iota(jnp.int32, (wide, F), 0) * F + lane
    inside = place < length
    g = jnp.where(lane + offset < F, turn[0:wide, :], turn[1 : wide + 1, :])
    g = jnp.where(inside, g, 0.0)
    shares[0] = g
    m_one = BETA_ONE * m_one + (1.0 - BETA_ONE) * g
    m_two = BETA_TWO * m_two + (1.0 - BETA_TWO) * g * g
    shares[1] = m_one
    shares[2] = m_two
    direction = (
        m_one
        / (1.0 - BETA_ONE**STEP)
        / (jnp.sqrt(m_two / (1.0 - BETA_TWO**STEP)) + EPSILON)
        + DECAY * old
    )
    spot = place + here.joint * length
    label = jnp.zeros((wide, F), jnp.int32)
    for end in GROUP_ENDS:
        label = label + jnp.where(spot >= end * F, 1, 0)
    label = jnp.where(inside, label, GROUPS)
    lines = []
    for value in (old, direction):
        square = value * value
        lines += [
            jnp.sum(jnp.where(label == k, square, 0.0), axis=0, keepdims=True)
            for k in range(GROUPS)
        ]
        lines.append(jnp.zeros((1, F), F32))
    sums.start(0, jnp.concatenate(lines, axis=0))
    give_back(BATCHES[2])
    sums.start(1, sums.finish(0))
    give_back(BATCHES[3])
    whole = jnp.sqrt(jnp.sum(sums.finish(1), axis=1, keepdims=True))
    ratio = whole[0:8] / whole[8:16]
    norms[...] = jnp.broadcast_to(whole, (16, F))
    trust = jnp.zeros((wide, F), F32)
    for k in range(GROUPS):
        trust = jnp.where(label == k, ratio[k : k + 1], trust)
    shares[3] = old - RATE * trust * direction

    for j in hops:
        known, device = here.hop(hop_offset(j))

        @pl.when(known)
        def _():
            block = pl.ds(j * cap, cap)
            tile = p_in.at[j]
            send(
                back.at[:, block], back.at[:, block], row_send.at[j], row_recv.at[j], device
            ).wait_recv()
            send(tile, tile, place_send.at[j], place_recv.at[j], device).wait_recv()

    low_half = lane < cap
    for j in range(0, 2 * HOPS, 2):
        p_back[:, j * cap : (j + 2) * cap] = jnp.where(low_half, p_in[j], p_in[j + 1])
    for exists, copy in copies:

        @pl.when(exists)
        def _():
            copy.wait_send()

    wait_sent(first + second + third)
    sums.done()


def reduce_all(cap, groups, length):
    shape = jax.ShapeDtypeStruct
    halo = 2 * HOPS * cap
    wide = window_rows(length)
    in_vmem = pl.BlockSpec(memory_space=pltpu.VMEM)
    in_any = pl.BlockSpec(memory_space=pl.ANY)
    return pl.pallas_call(
        functools.partial(reduce_kernel, length=length),
        out_shape=(
            shape((4, halo, F), F32),
            shape((8, halo), F32),
            shape((4, wide, F), F32),
            shape((16, F), F32),
        ),
        in_specs=[in_vmem, in_any] + [in_vmem] * 4,
        out_specs=(in_any, in_vmem, in_vmem, in_vmem),
        scratch_shapes=[
            pltpu.VMEM((groups, 4, 2, wide, F), F32),
            pltpu.VMEM((groups, 4, wide, F), F32),
            pltpu.VMEM((4, groups, wide, F), F32),
            pltpu.VMEM((groups, wide, F), F32),
            pltpu.VMEM((wide + 8, F), F32),
            pltpu.VMEM((4, cap, F), F32),
            pltpu.VMEM((2 * HOPS, 8, F), F32),
            pltpu.SemaphoreType.DMA((groups + 8,)),
            pltpu.SemaphoreType.DMA((groups + 8,)),
            pltpu.SemaphoreType.DMA((2 * HOPS,)),
            pltpu.SemaphoreType.DMA((2 * HOPS,)),
            pltpu.SemaphoreType.DMA((2 * HOPS,)),
            pltpu.SemaphoreType.DMA((2 * HOPS,)),
            pltpu.SemaphoreType.DMA((2 * HOPS,)),
        ]
        + small_scratch(groups, 16),
        compiler_params=pltpu.CompilerParams(
            collective_id=1, has_side_effects=True, vmem_limit_bytes=62 * 1024 * 1024
        ),
        name="reduce_outputs",
    )


def finish_kernel(
    back,
    p_back,
    shares,
    norms,
    stats,
    send_rows,
    gs_own,
    gv_own,
    gp_own,
    grad_s,
    grad_v,
    grad_p,
    elem_mean,
    scale,
    grad,
    one_new,
    two_new,
    par_new,
    par_low,
    weight_norms,
    update_norms,
):
    atoms = gs_own.shape[0]
    halo = back.shape[1]
    pick = jnp.concatenate([send_rows[0, j : j + 1, :] for j in range(2 * HOPS)], axis=1)
    hot = jnp.where(pick == lax.broadcasted_iota(jnp.int32, (atoms, halo), 0), 1.0, 0.0)
    hot = hot.astype(BF16)
    high, low = split(jnp.concatenate([back[k] for k in range(4)], axis=1))
    extra = mm(hot, high) + mm(hot, low)
    grad_s[...] = gs_own[...] + extra[:, :F]
    for c in range(3):
        grad_v[c] = gv_own[c] + extra[:, (c + 1) * F : (c + 2) * F]
    place = p_back[...]
    high = place.astype(BF16).astype(F32)
    middle = (place - high).astype(BF16).astype(F32)
    pieces = jnp.concatenate([high, middle, place - high - middle, jnp.zeros_like(place)], axis=0)
    got = mm(pieces.astype(BF16), hot, (1, 1))
    grad_p[...] = (gp_own[...] + (got[0:8] + got[8:16] + got[16:24]))[0:3]
    for k, ref in enumerate((grad, one_new, two_new, par_new)):
        to_flat(ref, shares[k])
    to_flat(par_low, shares[3].astype(BF16))
    rows = lax.broadcasted_iota(jnp.int32, (8, F), 0)
    lanes = lax.broadcasted_iota(jnp.int32, (8, F), 1)
    for k, ref in enumerate((weight_norms, update_norms)):
        line = jnp.sum(
            jnp.where(rows == lanes, norms[8 * k : 8 * k + 8, :], 0.0), axis=0, keepdims=True
        )
        ref[...] = line[0, :GROUPS]
    elem_mean[...] = stats[0, :ELEMS]
    scale[...] = stats[1, :1]


def finish(atoms, length):
    shape = jax.ShapeDtypeStruct
    in_vmem = pl.BlockSpec(memory_space=pltpu.VMEM)
    outs = (
        [shape((atoms, F), F32), shape((3, atoms, F), F32), shape((3, atoms), F32)]
        + [shape((ELEMS,), F32), shape((1,), F32)]
        + [shape((length,), F32)] * 4
        + [shape((length,), BF16), shape((GROUPS,), F32), shape((GROUPS,), F32)]
    )
    return pl.pallas_call(
        finish_kernel,
        out_shape=tuple(outs),
        in_specs=[in_vmem] * 9,
        out_specs=(in_vmem,) * len(outs),
        compiler_params=pltpu.CompilerParams(vmem_limit_bytes=62 * 1024 * 1024),
        name="finish",
    )


def body(
    scalars_in,
    vectors_in,
    positions,
    cotan_scalar,
    cotan_vector,
    target_energy,
    forces,
    elements,
    crystal,
    lattice,
    edge_src,
    edge_dst,
    edge_shift,
    edge_count,
    send_rows,
    params,
    first_moment,
    second_moment,
):
    atoms = scalars_in.shape[0]
    edges = edge_src.shape[0]
    cap = send_rows.shape[2]
    halo = 2 * HOPS * cap
    groups = lax.axis_size("atoms") // 4
    length = params.shape[0]
    par, halo_rows, p_halo, goal, stats, src_tiles = gather_all(atoms, cap, groups, length, edges)(
        send_rows,
        params,
        scalars_in,
        vectors_in,
        positions,
        target_energy.reshape(-1, F),
        elements.reshape(-1, F),
        forces,
        edge_src.reshape(-1, F),
    )
    s_two, v_two, gs_own, gv_own, g_halo, gp_own, gp_halo, gpar = layer(atoms, halo, edges)(
        edge_dst,
        edge_count,
        src_tiles.reshape(-1),
        crystal.reshape(-1, F),
        edge_dst.reshape(-1, F),
        edge_shift,
        jnp.transpose(lattice),
        par,
        scalars_in,
        vectors_in,
        positions,
        halo_rows,
        p_halo,
        cotan_scalar,
        cotan_vector,
        goal,
    )
    back, p_back, shares, norms = reduce_all(cap, groups, length)(
        gpar, g_halo, gp_halo, params, first_moment, second_moment
    )
    (
        grad_s,
        grad_v,
        grad_p,
        elem_mean,
        scale,
        grad,
        one_new,
        two_new,
        par_new,
        par_low,
        weight_norms,
        update_norms,
    ) = finish(atoms, length)(
        back, p_back, shares, norms, stats, send_rows, gs_own, gv_own, gp_own
    )
    return (
        s_two,
        v_two,
        grad_s,
        grad_v,
        grad_p,
        elem_mean,
        scale.reshape(()),
        grad,
        one_new,
        two_new,
        par_new,
        par_low,
        weight_norms,
        update_norms,
    )


def solution(mesh):
    joint = ("atoms", "rep")
    in_specs = (
        P(joint, None),
        P(None, joint, None),
        P(None, joint),
        P(joint, None),
        P(None, joint, None),
        P(joint),
        P(None, joint),
        P(joint),
        P(joint),
        P(),
        P(joint),
        P(joint),
        P(None, joint),
        P(joint),
        P(joint, None, None),
        P(joint),
        P(joint),
        P(joint),
    )
    out_specs = (
        P(joint, None),
        P(None, joint, None),
        P(joint, None),
        P(None, joint, None),
        P(None, joint),
        P(),
        P(),
        P(joint),
        P(joint),
        P(joint),
        P(joint),
        P(joint),
        P(),
        P(),
    )
    return jax.shard_map(body, mesh=mesh, in_specs=in_specs, out_specs=out_specs, check_vma=False)
```

```python
import functools

import jax
import jax.numpy as jnp
from jax import lax
from jax.experimental import pallas as pl
from jax.experimental.pallas import tpu as pltpu
from jax.sharding import PartitionSpec as P

F = 128
R = 20
HOPS = 4
ELEMS = 100
STEP = 10
GROUPS = 7

CUTOFF = 5.0
BETA_ONE = 0.9
BETA_TWO = 0.99
RATE = 0.3
DECAY = 0.01
EPSILON = 1e-06

BLOCK = 256
WINDOW = 128
PAIR = 2
LANE_ROWS = 80
SUB = 16
ROWS = 256
F32 = jnp.float32
BF16 = jnp.bfloat16

AT_W1, AT_W2, AT_WF, AT_WM, AT_U1, AT_U2 = 0, 128, 512, 572, 828, 1084
AT_B1, AT_B2, AT_BF, AT_C1, AT_C2, AT_READ, PARAM_ROWS = 1468, 1469, 1472, 1475, 1476, 1479, 1480
PARAM_PAD = PARAM_ROWS + 8
GROUP_ENDS = (128, 512, 572, 828, 1084, 1468)
MESH = pl.DeviceIdType.MESH
SENT = ((3, 7, 2, 6), (1, 5, 0, 4), ())
BATCHES = ((3, 7), (2, 6), (1, 5), (0, 4))


def mm(left, right, contract=(1, 0)):
    return lax.dot_general(
        left, right, (((contract[0],), (contract[1],)), ((), ())), preferred_element_type=F32
    )


def split(value):
    high = value.astype(BF16)
    return high, (value - high.astype(F32)).astype(BF16)


def dot3(left, right, contract=(1, 0)):
    return (
        mm(left[0], right[0], contract)
        + mm(left[1], right[0], contract)
        + mm(left[0], right[1], contract)
    )


def linear(pair, weights):
    both = jnp.concatenate(pair, axis=1)
    return mm(both, weights[0 : 2 * F, :]) + mm(pair[0], weights[2 * F : 3 * F, :])


def back_through(pair, weights):
    return dot3(pair, (weights[0:F, :], weights[2 * F : 3 * F, :]), (1, 1))


def wide_row(ref, start, parts):
    return jnp.concatenate([ref[start + j : start + j + 1, :] for j in range(parts)], axis=1)


def add_row(ref, start, parts, value):
    total = jnp.sum(value, axis=0, keepdims=True)
    for j in range(parts):
        ref[start + j : start + j + 1, :] += total[:, j * F : (j + 1) * F]


def add_matrix(ref, start, parts, value):
    for j in range(parts):
        add_column(ref, start, parts, j, value[:, j * F : (j + 1) * F], value.shape[0])


def sigmoid(value):
    return 1.0 / (1.0 + jnp.exp(-value))


def column(ref, start, parts, j, count=F):
    if parts == 1:
        return ref[start : start + count, :]
    return ref[pl.ds(start + j, count, stride=parts), :]


def add_column(ref, start, parts, j, value, count=F):
    if parts == 1:
        ref[start : start + count, :] += value
    else:
        ref[pl.ds(start + j, count, stride=parts), :] += value


def rows_of(start, count, unit):
    return pl.ds(pl.multiple_of(start, unit), count)


def lay_flat(ref, count):
    return jnp.concatenate([ref[k : k + 1, :] for k in range(count)], axis=1)


def weave(*parts):
    parts = list(parts)
    while parts:
        for part in list(parts):
            try:
                next(part)
            except StopIteration:
                parts.remove(part)


def layer_kernel(
    dst_s,
    count_s,
    src_s,
    crystal,
    dst_v,
    shift_v,
    lat,
    par,
    s_own,
    v_own,
    p_own,
    halo_rows,
    p_halo,
    cot_s,
    cot_v,
    goal,
    s_two,
    v_two,
    gs_own,
    gv_own,
    g_halo,
    gp_own,
    gp_halo,
    gpar,
    tab,
    rows,
    acc,
    stage,
    dtab,
    lane_buf,
    slope_buf,
    inv_buf,
    free_buf,
    turn_buf,
    sums,
    gd,
    gbuf,
    fbuf,
    mbuf,
    ltbuf,
    tbuf,
    wcat,
    wq,
    gwf,
    gpd,
    w1,
    w2,
    wm,
    u1,
    u2,
):
    atoms = s_own.shape[0]
    halo = halo_rows.shape[1]
    blocks_128 = shift_v.shape[1] // F
    ends_buf = stage.at[0 : blocks_128 * 16]
    shift_buf = stage.at[blocks_128 * 16 : blocks_128 * 24]
    place_buf = stage.at[blocks_128 * 24 : blocks_128 * 32]
    s_halo, v_halo = halo_rows.at[0], halo_rows.at[1:4]
    gs_halo, gv_halo = g_halo.at[0], g_halo.at[1:4]
    edges = shift_v.shape[1]
    blocks = edges // BLOCK

    wcat[...] = jnp.zeros_like(wcat)
    wq[...] = jnp.zeros_like(wq)
    gwf[...] = jnp.zeros_like(gwf)
    gpd[...] = jnp.zeros_like(gpd)
    gpar[...] = jnp.zeros_like(gpar)
    sums[...] = jnp.zeros_like(sums)
    for ref, start, parts in ((w1, AT_W1, 1), (w2, AT_W2, 3), (wm, AT_WM, 2), (u2, AT_U2, 3)):
        for j in range(parts):
            high, low = split(column(par, start, parts, j))
            for k, value in enumerate((high, high, low)):
                ref[k * F : (k + 1) * F, j * F : (j + 1) * F] = value
    u1[0 : 2 * F, :], u1[2 * F : 4 * F, :] = split(par[AT_U1 : AT_U1 + 2 * F, :])
    for j in range(3):
        wide = jnp.concatenate(
            [
                column(par, AT_WF, 3, j, R),
                par[AT_BF + j : AT_BF + j + 1, :],
                jnp.zeros((3, F), F32),
            ],
            axis=0,
        )
        high = wide.astype(BF16).astype(F32)
        low = wide - high
        pieces = jnp.concatenate([high, high, low, jnp.zeros((56, F), F32)], axis=0)
        wcat[:, j * F : (j + 1) * F] = pieces.astype(BF16)
        pieces = jnp.concatenate([high, low, jnp.zeros((80, F), F32)], axis=0)
        wq[j * F : (j + 1) * F, :] = jnp.transpose(pieces).astype(BF16)

    names = lay_flat(crystal, atoms // F)
    spots = lax.broadcasted_iota(jnp.int32, (F, atoms), 0)
    for k in range(atoms // F):
        acc[16 * k : 16 * k + 16, :] = jnp.zeros((16, F), F32)

    @pl.loop(0, lat.shape[1] // F)
    def _(step):
        table = lat[:, rows_of(step * F, F, F)]
        high = table.astype(BF16).astype(F32)
        middle = (table - high).astype(BF16).astype(F32)
        gap = jnp.zeros((7, F), F32)
        pieces = jnp.concatenate([high, gap, middle, gap, table - high - middle, gap], axis=0)
        got = mm(pieces.astype(BF16), jnp.where(names - step * F == spots, 1.0, 0.0).astype(BF16))
        got = got[0:16] + got[16:32] + got[32:48]
        for k in range(atoms // F):
            acc[16 * k : 16 * k + 16, :] += got[:, k * F : (k + 1) * F]

    across = jnp.concatenate([acc[16 * k : 16 * k + 16, :] for k in range(atoms // F)], axis=1)
    part = jnp.concatenate([p_own[...], across[0:9], jnp.zeros((4, atoms), F32)], axis=0)
    high = part.astype(BF16).astype(F32)
    middle = (part - high).astype(BF16).astype(F32)
    low = part - high - middle
    dtab[...] = jnp.concatenate([high, middle, low], axis=0).astype(BF16)

    for s_ref, v_ref, p_ref, base, count in (
        (s_own, v_own, p_own, 0, atoms),
        (s_halo, v_halo, p_halo, atoms, halo),
    ):
        place = jnp.concatenate([p_ref[0:3, :], jnp.zeros((F - 3, count), F32)], axis=0)
        tab[pl.ds(base * 8 + 6, count, stride=8), :] = jnp.transpose(place)
        tab[pl.ds(base * 8 + 7, count, stride=8), :] = jnp.zeros((count, F), F32)
        for c in range(3):
            tab[pl.ds(base * 8 + 3 + c, count, stride=8), :] = v_ref[c]

        @pl.loop(0, count // ROWS)
        def _(step):
            first = step * ROWS
            s_pair = split(s_ref[rows_of(first, ROWS, ROWS), :])
            act = linear(s_pair, w1) + par[AT_B1 : AT_B1 + 1, :]
            x = linear(split(act * sigmoid(act)), w2) + wide_row(par, AT_B2, 3)
            for j in range(3):
                tab[pl.ds((base + first) * 8 + j, ROWS, stride=8), :] = x[:, j * F : (j + 1) * F]

    slots = lax.broadcasted_iota(jnp.int32, (WINDOW, BLOCK), 0)
    eight = lax.broadcasted_iota(jnp.int32, (8, 1), 0)
    wide_lane = lax.broadcasted_iota(jnp.int32, (1, F), 1)
    chunks = edges // F
    per = BLOCK // F

    def destinations(i):
        return jnp.concatenate([dst_v[pl.ds(i * per + k, 1), :] for k in range(per)], axis=1)

    def window_range(i):
        return dst_s[i * BLOCK] // WINDOW, dst_s[i * BLOCK + BLOCK - 1] // WINDOW

    def hot(dst, w):
        return jnp.where(dst - w * WINDOW == slots, 1.0, 0.0).astype(BF16)

    def window(w):
        return rows_of(w * WINDOW, WINDOW, WINDOW)

    def lane_chunk(i, k):
        return rows_of((i * per + k) * LANE_ROWS, LANE_ROWS, LANE_ROWS)

    def source(i, j):
        return pl.ds(pl.multiple_of(src_s[i * BLOCK + j], 8), 8)

    def ends_in(i, w):
        got = mm(dtab[:, window(w)], hot(destinations(i), w))
        return got[0:16] + got[16:32] + got[32:48]

    def gather(i):
        for j in range(BLOCK):
            spot = pl.multiple_of(i * (BLOCK * 8), BLOCK * 8) + j * 8
            rows[pl.ds(pl.multiple_of(spot, 8), 8), :] = tab[source(i, j), :]
            if j % 16 == 15:
                yield

    def clear(ref, i):
        each = ref.shape[0] // blocks // 8
        for k in range(8):
            ref[rows_of((i * 8 + k) * each, each, each), :] = jnp.zeros((each, F), F32)
            yield

    def ends(i):
        got = ends_in(i, window_range(i)[0])
        yield
        for k in range(per):
            chunk = i * per + k
            shift_buf[pl.ds(pl.multiple_of(chunk * 8, 8), 3), :] = shift_v[
                :, rows_of(chunk * F, F, F)
            ].astype(F32)
            ends_buf[rows_of(chunk * 16, 16, 16), :] = got[:, k * F : (k + 1) * F]
            yield

    def places_of(i):
        for k in range(per):
            chunk = i * per + k
            place = rows[pl.ds(chunk * (F * 8) + 6, F, stride=8), :]
            yield
            place_buf[rows_of(chunk * 8, 8, 8), :] = jnp.transpose(place)[0:8]
            yield

    @pl.loop(0, blocks // PAIR)
    def _(step):
        for t in range(PAIR):
            i = step * PAIR + t
            weave(ends(i), places_of(jnp.maximum(i - 1, 0)), gather(i), clear(acc, i))
            first, last = window_range(i)

            @pl.loop(first + 1, last + 1)
            def _(w):
                more = ends_in(i, w)
                for k in range(per):
                    ends_buf[rows_of((i * per + k) * 16, 16, 16), :] += more[:, k * F : (k + 1) * F]

    weave(places_of(blocks - 1))

    def dense(ref, row, step):
        return ref[pl.ds(row, chunks, stride=step), :]

    def put_row(row, value):
        lane_buf[pl.ds(row, chunks, stride=LANE_ROWS), :] = value

    shift = [dense(shift_buf, k, 8) for k in range(3)]
    rel = [
        dense(place_buf, c, 8)
        + (
            shift[0] * dense(ends_buf, 3 + c, 16)
            + shift[1] * dense(ends_buf, 6 + c, 16)
            + shift[2] * dense(ends_buf, 9 + c, 16)
        )
        - dense(ends_buf, c, 16)
        for c in range(3)
    ]
    square = rel[0] * rel[0] + rel[1] * rel[1] + rel[2] * rel[2]
    dist = jnp.sqrt(jnp.maximum(square, 0.25))
    inv = 1.0 / dist
    inv_buf[...] = inv
    free_buf[...] = jnp.where(square > 0.25, 1.0, 0.0)
    for c in range(3):
        put_row(72 + c, rel[c] * inv)
    put_row(75, dst_v[...].astype(F32))
    nothing = jnp.zeros((chunks, F), F32)
    for row in (21, 22, 23, 45, 46, 47, 69, 70, 71, 76, 77, 78, 79):
        put_row(row, nothing)
    for row in (21, 22, 23):
        slope_buf[pl.ds(row, chunks, stride=24), :] = nothing
    angle = dist * (jnp.pi / CUTOFF)
    sin_one, cos_one = jnp.sin(angle), jnp.cos(angle)
    place = lax.broadcasted_iota(jnp.int32, (chunks, F), 0) * F + lax.broadcasted_iota(
        jnp.int32, (chunks, F), 1
    )
    inside = (dist < CUTOFF) & (place < count_s[0])
    envelope = jnp.where(inside, 0.5 * (cos_one + 1.0), 0.0)
    fall = jnp.where(inside, (-0.5 * jnp.pi / CUTOFF) * sin_one, 0.0)
    sin_n, cos_n = sin_one, cos_one
    for n in range(R + 1):
        if n < R:
            radial = sin_n * inv
            slope = (((n + 1) * jnp.pi / CUTOFF) * cos_n - radial) * inv
            scaled = envelope * radial
            change = fall * radial + envelope * slope
            sin_n, cos_n = sin_n * cos_one + cos_n * sin_one, cos_n * cos_one - sin_n * sin_one
        else:
            scaled, change = envelope, fall
        high = scaled.astype(BF16).astype(F32)
        put_row(n, high)
        put_row(24 + n, scaled - high)
        put_row(48 + n, high)
        slope_buf[pl.ds(n, chunks, stride=24), :] = change

    def comp(i, k, sub):
        return pl.ds(i * (BLOCK * 8) + sub * (SUB * 8) + k, SUB, stride=8)

    def filters(i, t):
        for k in range(per):
            full = jnp.concatenate(
                [lane_buf[lane_chunk(i, k), :], jnp.zeros((F - LANE_ROWS, F), F32)], axis=0
            )
            ltbuf[t, k * F : (k + 1) * F, :] = jnp.transpose(full)
            yield
        fbuf[t] = mm(ltbuf[t].astype(BF16), wcat[...])
        yield

    def messages(i, t):
        for sub in range(BLOCK // SUB):
            at = slice(sub * SUB, (sub + 1) * SUB)
            m1, m2, m3 = [
                rows[comp(i, j, sub), :] * fbuf[t, at, j * F : (j + 1) * F] for j in range(3)
            ]
            out = [m1]
            for c in range(3):
                out.append(m2 * ltbuf[t, at, 72 + c : 73 + c] + m3 * rows[comp(i, 3 + c, sub), :])
            for k in range(4):
                high, low = split(out[k])
                mbuf[t, at, k * F : (k + 1) * F] = high
                mbuf[t, at, (4 + k) * F : (5 + k) * F] = low
            yield

    def collect(i, t, w):
        pick = hot(destinations(i), w)
        for k in range(2):
            of = slice(k * 2 * F, (k + 1) * 2 * F)
            more = slice((k + 2) * 2 * F, (k + 3) * 2 * F)
            sums[window(w), of] += mm(pick, mbuf[t, :, of]) + mm(pick, mbuf[t, :, more])
            yield

    def collect_more(i, t):
        first, last = window_range(i)

        @pl.loop(first + 1, last + 1)
        def _(w):
            weave(collect(i, t, w))

    mbuf[...] = jnp.zeros_like(mbuf)
    weave(filters(0, 0))

    @pl.loop(0, blocks // PAIR)
    def _(step):
        for t in range(PAIR):
            i = step * PAIR + t
            before = jnp.maximum(i - 1, 0)
            weave(
                filters(jnp.minimum(i + 1, blocks - 1), 1 - t),
                collect(before, 1 - t, window_range(before)[0]),
                messages(i, t),
                clear(tab, i),
            )
            collect_more(before, 1 - t)

    weave(collect(blocks - 1, PAIR - 1, window_range(blocks - 1)[0]))
    collect_more(blocks - 1, PAIR - 1)

    @pl.loop(0, atoms // ROWS)
    def _(step):
        at = rows_of(step * ROWS, ROWS, ROWS)
        s_one = s_own[at, :] + sums[at, 0:F]
        v_one = [v_own[c, at, :] + sums[at, (c + 1) * F : (c + 2) * F] for c in range(3)]
        v_pair = [split(v) for v in v_one]
        mixed = [linear(v, wm) for v in v_pair]
        v_lin = [m[:, :F] for m in mixed]
        w_lin = [m[:, F:] for m in mixed]
        size = jnp.sqrt(v_lin[0] * v_lin[0] + v_lin[1] * v_lin[1] + v_lin[2] * v_lin[2] + 1.0)
        s_pair = split(jnp.concatenate([s_one, size], axis=1))
        u1_pair = (u1[0 : 2 * F, :], u1[2 * F : 4 * F, :])
        act = dot3(s_pair, u1_pair) + par[AT_C1 : AT_C1 + 1, :]
        gate = sigmoid(act)
        hidden = split(act * gate)
        gating = linear(hidden, u2) + wide_row(par, AT_C2, 3)
        a1, a2, a3 = [gating[:, j * F : (j + 1) * F] for j in range(3)]
        inner = v_lin[0] * w_lin[0] + v_lin[1] * w_lin[1] + v_lin[2] * w_lin[2]
        s_out = s_one + a3 + a2 * inner
        s_two[at, :] = s_out
        read = par[AT_READ : AT_READ + 1, :]
        out_pair = split(s_out)
        energy = dot3(split(jnp.broadcast_to(read, (8, F))), out_pair, (1, 1))
        error = energy - goal[:, at]
        error_col = jnp.transpose(error)[:, 0:1]
        gpar[AT_READ : AT_READ + 1, :] += dot3(split(error), out_pair)[0:1]
        gs = cot_s[at, :] + error_col * read
        gv = []
        for c in range(3):
            v_two[c, at, :] = v_one[c] + a1 * w_lin[c]
            gv.append(cot_v[c, at, :])
        ga = [gv[0] * w_lin[0] + gv[1] * w_lin[1] + gv[2] * w_lin[2], gs * inner, gs]
        g_inner = gs * a2
        ga = jnp.concatenate(ga, axis=1)
        ga_pair = split(ga)
        add_matrix(gpar, AT_U2, 3, dot3(hidden, ga_pair, (0, 0)))
        add_row(gpar, AT_C2, 3, ga)
        g_act = back_through(ga_pair, u2) * (gate * (1.0 + act * (1.0 - gate)))
        g_act_pair = split(g_act)
        gpar[AT_U1 : AT_U1 + 2 * F, :] += dot3(s_pair, g_act_pair, (0, 0))
        add_row(gpar, AT_C1, 1, g_act)
        g_both = dot3(g_act_pair, u1_pair, (1, 1))
        g_s_one = gs + g_both[:, :F]
        g_size = g_both[:, F:] / size
        gs_own[at, :] = g_s_one
        down = [g_s_one]
        for c in range(3):
            g_mixed = split(
                jnp.concatenate(
                    [
                        g_inner * w_lin[c] + g_size * v_lin[c],
                        a1 * gv[c] + g_inner * v_lin[c],
                    ],
                    axis=1,
                )
            )
            add_matrix(gpar, AT_WM, 2, dot3(v_pair[c], g_mixed, (0, 0)))
            g_v_one = gv[c] + back_through(g_mixed, wm)
            gv_own[c, at, :] = g_v_one
            down.append(g_v_one)
        for k in range(4):
            high, low = split(down[k])
            for part in range(ROWS // WINDOW):
                to = (step * (ROWS // WINDOW) + part) * (2 * WINDOW)
                of = slice(part * WINDOW, (part + 1) * WINDOW)
                gd[rows_of(to, WINDOW, WINDOW), k * F : (k + 1) * F] = high[of]
                gd[rows_of(to + WINDOW, WINDOW, WINDOW), k * F : (k + 1) * F] = low[of]

    twice = (lax.broadcasted_iota(jnp.int32, (1, 2 * WINDOW), 1) % WINDOW).astype(F32)
    for ref in (stage, mbuf, tbuf, turn_buf):
        ref[...] = jnp.zeros_like(ref)

    def collect_places(i, t, w):
        g_rel = turn_buf[t]
        high = g_rel.astype(BF16).astype(F32)
        middle = (g_rel - high).astype(BF16).astype(F32)
        pieces = jnp.concatenate(
            [high, middle, g_rel - high - middle, jnp.zeros_like(g_rel)], axis=0
        )
        got = mm(pieces.astype(BF16), hot(destinations(i), w), (1, 1))
        gpd[:, window(w)] += got[0:8] + got[8:16] + got[16:24]

    def fetch(t, w):
        near = ltbuf[t, :, 75:76] - (w * WINDOW).astype(F32)
        return mm(
            jnp.where(near == twice, 1.0, 0.0).astype(BF16),
            gd[rows_of(w * 2 * WINDOW, 2 * WINDOW, 2 * WINDOW), :],
        )

    def prepare(i, t):
        yield from filters(i, t)
        gbuf[t] = fetch(t, window_range(i)[0])
        yield

    def into_sources(i, t, one, two):
        to = (source(i, one), source(i, two))
        held = [(t * BLOCK + spot) * 8 for spot in (one, two)]
        first = tab[to[0], :] + stage[held[0] : held[0] + 8, :]
        second = acc[to[1], :] + stage[held[1] : held[1] + 8, :]
        tab[to[0], :] = first
        acc[to[1], :] = second

    def spread(i, t, earlier):
        for sub in range(BLOCK // SUB):
            at = slice(sub * SUB, (sub + 1) * SUB)
            for j in range(SUB // 2):
                into_sources(earlier, t, sub * SUB + j, sub * SUB + SUB // 2 + j)
                if j % 4 == 3:
                    yield
            to = [pl.ds(t * (BLOCK * 8) + sub * (SUB * 8) + k, SUB, stride=8) for k in range(6)]
            g_s = gbuf[t, at, 0:F]
            g_v = [gbuf[t, at, (c + 1) * F : (c + 2) * F] for c in range(3)]
            x = [rows[comp(i, j, sub), :] for j in range(3)]
            v = [rows[comp(i, 3 + c, sub), :] for c in range(3)]
            f = [fbuf[t, at, j * F : (j + 1) * F] for j in range(3)]
            u = [ltbuf[t, at, 72 + c : 73 + c] for c in range(3)]
            g_m = [
                g_s,
                g_v[0] * u[0] + g_v[1] * u[1] + g_v[2] * u[2],
                g_v[0] * v[0] + g_v[1] * v[1] + g_v[2] * v[2],
            ]
            m2 = x[1] * f[1]
            m3 = x[2] * f[2]
            turn = jnp.zeros((SUB, F), F32)
            for c in range(3):
                total = jnp.sum(g_v[c] * m2, axis=1, keepdims=True)
                turn = jnp.where(wide_lane == 48 + c, total, turn)
                stage[to[3 + c], :] = g_v[c] * m3
            tbuf[t, at, :] = turn
            for j in range(3):
                high, low = split(g_m[j] * x[j])
                mbuf[t, at, j * F : (j + 1) * F] = high
                mbuf[t, at, (3 + j) * F : (4 + j) * F] = low
                stage[to[j], :] = g_m[j] * f[j]
            yield

    def settle(i, t):
        h_high, h_low = mbuf[t, :, : 3 * F], mbuf[t, :, 3 * F : 6 * F]
        back = mm(h_high, wq[...]) + mm(h_low, wq[...]) + tbuf[t]
        yield
        back = jnp.transpose(back)
        yield
        pieces = jnp.concatenate(
            [lane_buf[lane_chunk(i, k), :][0:48] for k in range(per)], axis=1
        ).astype(BF16)
        gwf[...] += mm(pieces, h_high) + mm(pieces, h_low)
        yield
        slope = jnp.concatenate(
            [slope_buf[rows_of((i * per + k) * 24, 24, 24), :] for k in range(per)], axis=1
        )
        g_dist = jnp.sum((back[0:24] + back[24:48]) * slope, axis=0, keepdims=True)
        g_unit = back[48:56]
        unit = jnp.concatenate([lane_buf[lane_chunk(i, k), :][72:80] for k in range(per)], axis=1)
        unit = jnp.where(eight < 3, unit, 0.0)
        inv, free = [
            jnp.concatenate([ref[pl.ds(i * per + k, 1), :] for k in range(per)], axis=1)
            for ref in (inv_buf, free_buf)
        ]
        yield
        along = jnp.sum(g_unit * unit, axis=0, keepdims=True)
        g_rel = g_unit * inv + (g_dist - along * inv) * free * unit
        turn_buf[t] = g_rel
        yield
        stage[pl.ds(t * (BLOCK * 8) + 6, BLOCK, stride=8), :] = jnp.transpose(
            jnp.concatenate([g_rel, jnp.zeros((F - 8, BLOCK), F32)], axis=0)
        )
        yield
        collect_places(i, t, window_range(i)[0])
        yield

    def prepare_more(i, t):
        first, last = window_range(i)

        @pl.loop(first + 1, last + 1)
        def _(w):
            gbuf[t] += fetch(t, w)

    def settle_more(i, t):
        first, last = window_range(i)

        @pl.loop(first + 1, last + 1)
        def _(w):
            collect_places(i, t, w)

    weave(prepare(0, 0))
    prepare_more(0, 0)

    @pl.loop(0, blocks // PAIR)
    def _(step):
        for t in range(PAIR):
            i = step * PAIR + t
            before, after = jnp.maximum(i - 1, 0), jnp.minimum(i + 1, blocks - 1)
            weave(prepare(after, 1 - t), settle(before, 1 - t), spread(i, t, jnp.maximum(i - 2, 0)))
            prepare_more(after, 1 - t)
            settle_more(before, 1 - t)

    weave(settle(blocks - 1, PAIR - 1))
    settle_more(blocks - 1, PAIR - 1)
    for t in range(PAIR):
        for j in range(BLOCK // 2):
            into_sources(blocks - PAIR + t, t, j, BLOCK // 2 + j)

    for j in range(3):
        total = gwf[0:24, j * F : (j + 1) * F] + gwf[24:48, j * F : (j + 1) * F]
        add_column(gpar, AT_WF, 3, j, total[0:R], R)
        gpar[AT_BF + j : AT_BF + j + 1, :] = total[R : R + 1]

    for s_ref, gs_ref, gv_ref, gp_ref, base, count in (
        (s_own, gs_own, gv_own, gp_own, 0, atoms),
        (s_halo, gs_halo, gv_halo, gp_halo, atoms, halo),
    ):
        own = base == 0
        for k in range(0, count, ROWS):
            at = pl.ds((base + k) * 8 + 6, ROWS, stride=8)
            place = jnp.transpose(tab[at, :] + acc[at, :])[0:8]
            if own:
                place = place - gpd[:, k : k + ROWS]
            gp_ref[:, k : k + ROWS] = place

        @pl.loop(0, count // ROWS)
        def _(step):
            first = step * ROWS
            to = rows_of(first, ROWS, ROWS)

            def gathered(k):
                at = pl.ds((base + first) * 8 + k, ROWS, stride=8)
                return tab[at, :] + acc[at, :]

            for c in range(3):
                if own:
                    gv_ref[c, to, :] += gathered(3 + c)
                else:
                    gv_ref[c, to, :] = gathered(3 + c)
            s_pair = split(s_ref[to, :])
            act = linear(s_pair, w1) + par[AT_B1 : AT_B1 + 1, :]
            gate = sigmoid(act)
            hidden = split(act * gate)
            g_x = jnp.concatenate([gathered(j) for j in range(3)], axis=1)
            g_pair = split(g_x)
            add_matrix(gpar, AT_W2, 3, dot3(hidden, g_pair, (0, 0)))
            add_row(gpar, AT_B2, 3, g_x)
            g_act = back_through(g_pair, w2) * (gate * (1.0 + act * (1.0 - gate)))
            g_act_pair = split(g_act)
            add_matrix(gpar, AT_W1, 1, dot3(s_pair, g_act_pair, (0, 0)))
            add_row(gpar, AT_B1, 1, g_act)
            g_s = back_through(g_act_pair, w1)
            if own:
                gs_ref[to, :] += g_s
            else:
                gs_ref[to, :] = g_s


def layer(atoms, halo, edges):
    shape = jax.ShapeDtypeStruct
    total = atoms + halo
    in_vmem = pl.BlockSpec(memory_space=pltpu.VMEM)
    in_smem = pl.BlockSpec(memory_space=pltpu.SMEM)
    outs = (
        shape((atoms, F), F32),
        shape((3, atoms, F), F32),
        shape((atoms, F), F32),
        shape((3, atoms, F), F32),
        shape((4, halo, F), F32),
        shape((8, atoms), F32),
        shape((8, halo), F32),
        shape((PARAM_PAD, F), F32),
    )
    scratch = [
        pltpu.VMEM((total * 8, F), F32),
        pltpu.VMEM((edges * 8, F), F32),
        pltpu.VMEM((total * 8, F), F32),
        pltpu.VMEM((PAIR * BLOCK * 8, F), F32),
        pltpu.VMEM((48, atoms), BF16),
        pltpu.VMEM((edges // F * LANE_ROWS, F), F32),
        pltpu.VMEM((edges // F * 24, F), F32),
        pltpu.VMEM((edges // F, F), F32),
        pltpu.VMEM((edges // F, F), F32),
        pltpu.VMEM((PAIR, 8, BLOCK), F32),
        pltpu.VMEM((atoms, 4 * F), F32),
        pltpu.VMEM((2 * atoms, 4 * F), BF16),
        pltpu.VMEM((PAIR, BLOCK, 4 * F), F32),
        pltpu.VMEM((PAIR, BLOCK, 3 * F), F32),
        pltpu.VMEM((PAIR, BLOCK, 8 * F), BF16),
        pltpu.VMEM((PAIR, BLOCK, F), F32),
        pltpu.VMEM((PAIR, BLOCK, F), F32),
        pltpu.VMEM((F, 3 * F), BF16),
        pltpu.VMEM((3 * F, F), BF16),
        pltpu.VMEM((48, 3 * F), F32),
        pltpu.VMEM((8, atoms), F32),
        pltpu.VMEM((3 * F, F), BF16),
        pltpu.VMEM((3 * F, 3 * F), BF16),
        pltpu.VMEM((3 * F, 2 * F), BF16),
        pltpu.VMEM((4 * F, F), BF16),
        pltpu.VMEM((3 * F, 3 * F), BF16),
    ]
    return pl.pallas_call(
        layer_kernel,
        out_shape=outs,
        in_specs=[in_smem] * 3 + [in_vmem] * 13,
        out_specs=(in_vmem,) * len(outs),
        scratch_shapes=scratch,
        compiler_params=pltpu.CompilerParams(vmem_limit_bytes=63 * 1024 * 1024),
        name="layer",
    )


def hop_offset(j):
    return j + 1 if j < HOPS else HOPS - 1 - j


class Place:
    def __init__(self):
        self.chips = lax.axis_size("atoms")
        self.cores = lax.axis_size("rep")
        self.count = self.chips * self.cores
        self.groups = self.chips // 4
        chip = lax.axis_index("atoms")
        self.core = lax.axis_index("rep")
        self.joint = chip * self.cores + self.core
        self.group = chip // 4
        self.quarter = chip % 4
        self.mate = 1 - self.core

    def other_groups(self):
        return [lax.rem(self.group + k, self.groups) for k in range(1, self.groups)]

    def other_quarters(self):
        return [lax.rem(self.quarter + k, 4) for k in range(1, 4)]

    def in_group(self, group):
        return (group * 4 + self.quarter, self.core)

    def in_quarter(self, quarter):
        return (self.group * 4 + quarter, self.core)

    def beside(self):
        return (self.group * 4 + self.quarter, self.mate)

    def hop(self, by):
        other = self.joint + by
        exists = (other >= 0) & (other < self.count)
        other = jnp.clip(other, 0, self.count - 1)
        return exists, (other // self.cores, other % self.cores)

    def others_of_group(self):
        own = self.quarter * self.cores + self.core
        places = [lax.rem(own + k, 4 * self.cores) for k in range(1, 4 * self.cores)]
        return [(o, (self.group * 4 + o // self.cores, o % self.cores)) for o in places]

    def greet(self):
        barrier = pltpu.get_barrier_semaphore()
        fixed = [self.in_group(g) for g in self.other_groups()]
        fixed += [device for _, device in self.others_of_group()]
        for device in fixed:
            pl.semaphore_signal(barrier, inc=1, device_id=device, device_id_type=MESH)
        hops = [self.hop(hop_offset(j)) for j in range(2 * HOPS)]
        expected = jnp.int32(len(fixed))
        for exists, device in hops:
            expected = expected + jnp.where(exists, 1, 0)

            @pl.when(exists)
            def _():
                pl.semaphore_signal(barrier, inc=1, device_id=device, device_id_type=MESH)

        return expected


def send(src, dst, send_sem, recv_sem, device):
    return pltpu.make_async_remote_copy(
        src_ref=src,
        dst_ref=dst,
        send_sem=send_sem,
        recv_sem=recv_sem,
        device_id=device,
        device_id_type=MESH,
    )


def start_all(copies):
    for copy in copies:
        copy.start()
    return copies


def wait_sent(copies):
    for copy in copies:
        copy.wait_send()


def window_rows(length):
    return -(-((length + F - 1) // F + 1) // 8) * 8


class SmallSum:
    def __init__(self, place, slots_a, slots_b, sends, recvs):
        self.place = place
        self.slots = (slots_a, slots_b)
        self.sends, self.recvs = sends, recvs
        self.sent = []

    def partners(self, phase):
        p = self.place
        if phase == 0:
            return p.quarter * p.cores + p.core, p.others_of_group(), 0
        return p.group, [(g, p.in_group(g)) for g in p.other_groups()], 4 * p.cores

    def start(self, phase, value):
        slots = self.slots[phase]
        mine, others, base = self.partners(phase)
        slots[mine] = value
        for k, (_, device) in enumerate(others):
            spot = slots.at[mine]
            copy = send(spot, spot, self.sends.at[base + k], self.recvs.at[base + mine], device)
            copy.start()
            self.sent.append(copy)

    def finish(self, phase):
        slots = self.slots[phase]
        _, others, base = self.partners(phase)
        for o, device in others:
            spot = slots.at[o]
            send(spot, spot, self.sends.at[base], self.recvs.at[base + o], device).wait_recv()
        total = slots[0]
        for k in range(1, slots.shape[0]):
            total = total + slots[k]
        return total

    def done(self):
        wait_sent(self.sent)


def small_scratch(groups, rows):
    count = groups + 8
    return [
        pltpu.VMEM((8, rows, F), F32),
        pltpu.VMEM((groups, rows, F), F32),
        pltpu.SemaphoreType.DMA((count,)),
        pltpu.SemaphoreType.DMA((count,)),
    ]


def from_flat(ref, rows):
    length = ref.shape[0]
    whole, rest = length // F, length % F
    lines = [ref[pl.ds(r * F, F)].reshape(1, F) for r in range(whole)]
    if rest:
        last = ref[pl.ds(whole * F, rest)].reshape(1, rest)
        lines.append(jnp.concatenate([last, jnp.zeros((1, F - rest), F32)], axis=1))
    lines.append(jnp.zeros((rows - len(lines), F), F32))
    return jnp.concatenate(lines, axis=0)


def to_flat(ref, value):
    length = ref.shape[0]
    whole, rest = length // F, length % F
    for r in range(whole):
        ref[pl.ds(r * F, F)] = value[r]
    if rest:
        ref[pl.ds(whole * F, rest)] = value[whole, :rest]


def gather_kernel(
    send_s,
    par_in,
    s_h,
    v_h,
    p_own,
    energy,
    elements,
    forces,
    edge_src,
    par,
    halo_rows,
    p_halo,
    goal,
    stats,
    src_tiles,
    s_own,
    v_own,
    own_sem,
    slots,
    pack,
    places,
    p_out,
    p_in,
    zeros,
    ag_send,
    ag_recv,
    row_send,
    row_recv,
    place_send,
    place_recv,
    zero_sem,
    *small,
    length,
):
    here = Place()
    atoms = s_own.shape[0]
    cap = halo_rows.shape[1] // (2 * HOPS)
    wide = slots.shape[3]
    loads = [
        pltpu.make_async_copy(s_h, s_own, own_sem.at[0]),
        pltpu.make_async_copy(v_h, v_own, own_sem.at[1]),
    ]
    for load in loads:
        load.start()
    expected = here.greet()
    sums = SmallSum(here, *small)

    offset = lax.rem(here.joint * length, F)
    lane = lax.broadcasted_iota(jnp.int32, (1, F), 1)
    turned = pltpu.roll(from_flat(par_in, wide), offset, 1)
    above = jnp.concatenate([jnp.zeros((1, F), F32), turned[: wide - 1]], axis=0)
    mine = slots.at[here.group, here.quarter, here.core]
    mine[...] = jnp.where(lane < offset, above, turned)
    src_tiles[...] = edge_src[...] * 8

    count = atoms // F
    energy_row, element_row = lay_flat(energy, count), lay_flat(elements, count)
    hot = jnp.where(
        element_row == lax.broadcasted_iota(jnp.int32, (F, atoms), 0), 1.0, 0.0
    ).astype(BF16)
    high = energy_row.astype(BF16).astype(F32)
    middle = (energy_row - high).astype(BF16).astype(F32)
    eight = lax.broadcasted_iota(jnp.int32, (8, 1), 0)
    left = jnp.where(
        eight == 0,
        high,
        jnp.where(
            eight == 1, middle, jnp.where(eight == 2, energy_row - high - middle, jnp.where(eight == 3, 1.0, 0.0))
        ),
    )
    found = mm(left.astype(BF16), hot, (1, 1))
    squares = jnp.sum(forces[...] * forces[...], axis=0, keepdims=True)
    square = squares[:, 0:F]
    for k in range(1, count):
        square = square + squares[:, k * F : (k + 1) * F]
    tile = jnp.where(
        eight == 0,
        found[0:1] + found[1:2] + found[2:3],
        jnp.where(eight == 1, found[3:4], jnp.where(eight == 2, square, 0.0)),
    )
    places[...] = jnp.transpose(
        jnp.concatenate([p_own[...], jnp.zeros((F - 3, atoms), F32)], axis=0)
    )
    zeros[...] = jnp.zeros_like(zeros)
    for load in loads:
        load.wait()
    hops = range(2 * HOPS)
    for j in hops:

        @pl.loop(0, cap // 16)
        def _(step):
            for k in range(16):
                r = step * 16 + k
                t = send_s[0, j, r]
                r = j * cap + r
                pack[0, pl.ds(r, 1), :] = s_own[pl.ds(t, 1), :]
                for c in range(3):
                    pack[1 + c, pl.ds(r, 1), :] = v_own[c, pl.ds(t, 1), :]
                p_out[pl.ds(r, 1), :] = places[pl.ds(t, 1), :]

    for j in range(0, 2 * HOPS, 2):
        pair = slice(j * cap, (j + 2) * cap)
        p_in[2 * HOPS + j // 2] = jnp.transpose(p_out[pair, :])[0:8]

    pl.semaphore_wait(pltpu.get_barrier_semaphore(), expected)
    first = start_all(
        [
            send(mine, mine, ag_send.at[k], ag_recv.at[here.group], here.in_group(g))
            for k, g in enumerate(here.other_groups())
        ]
    )
    sums.start(0, tile)
    row_copies, place_copies = [], []

    def give(some):
        for j in some:
            exists, device = here.hop(hop_offset(j))
            block = pl.ds(j * cap, cap)
            rows_copy = send(
                pack.at[:, block], halo_rows.at[:, block], row_send.at[j], row_recv.at[j], device
            )
            place_copy = send(
                p_in.at[2 * HOPS + j // 2], p_in.at[j], place_send.at[j], place_recv.at[j], device
            )
            row_copies.append((exists, rows_copy))
            place_copies.append((exists, place_copy))

            @pl.when(exists)
            def _():
                rows_copy.start()
                place_copy.start()

    give(SENT[0])
    for j in hops:
        known, device = here.hop(-hop_offset(j))

        @pl.when(jnp.logical_not(known))
        def _():
            p_in[j] = jnp.zeros((8, F), F32)
            fill = pltpu.make_async_copy(
                zeros, halo_rows.at[:, pl.ds(j * cap, cap)], zero_sem.at[j]
            )
            fill.start()
            fill.wait()

    for g in here.other_groups():
        spot = slots.at[g, here.quarter, here.core]
        send(spot, spot, ag_send.at[0], ag_recv.at[g], here.beside()).wait_recv()
    base = here.groups
    line = slots.at[:, here.quarter, here.core]
    second = start_all(
        [
            send(line, line, ag_send.at[base + k], ag_recv.at[base + here.quarter], here.in_quarter(q))
            for k, q in enumerate(here.other_quarters())
        ]
    )
    third = [
        send(
            line, line, ag_send.at[base + 4], ag_recv.at[base + 4 + here.quarter], here.beside()
        )
    ]
    third[0].start()
    give(SENT[1])
    sums.start(1, sums.finish(0))
    for k, q in enumerate(here.other_quarters()):
        line = slots.at[:, q, here.core]
        send(line, line, ag_send.at[0], ag_recv.at[base + q], here.beside()).wait_recv()
        copy = send(
            line, line, ag_send.at[base + 5 + k], ag_recv.at[base + 4 + q], here.beside()
        )
        copy.start()
        third.append(copy)
    give(SENT[2])
    for q in range(4):
        line = slots.at[:, q, here.mate]
        send(line, line, ag_send.at[0], ag_recv.at[base + 4 + q], here.beside()).wait_recv()

    par[...] = jnp.zeros_like(par)
    for p in range(here.count):
        row = p * length // F
        chip, core = p // here.cores, p % here.cores
        take = min(wide, PARAM_PAD - row)
        par[row : row + take, :] += slots[chip // 4, chip % 4, core, 0:take, :]

    total = sums.finish(1)
    mean = total[0:1] / jnp.maximum(total[1:2], 1.0)
    whole = jnp.sum(total[2:3], axis=1, keepdims=True)
    scale = jnp.sqrt(whole / (3.0 * atoms * here.count) + 1e-06)
    high = mean.astype(BF16).astype(F32)
    middle = (mean - high).astype(BF16).astype(F32)
    left = jnp.where(
        eight == 0,
        high,
        jnp.where(eight == 1, middle, jnp.where(eight == 2, mean - high - middle, 0.0)),
    )
    found = mm(left.astype(BF16), hot)
    goal[...] = (energy_row - (found[0:1] + found[1:2] + found[2:3])) / scale
    stats[...] = jnp.where(eight == 0, mean, jnp.where(eight == 1, scale, 0.0))

    for j in hops:
        known, device = here.hop(-hop_offset(j))

        @pl.when(known)
        def _():
            block = pl.ds(j * cap, cap)
            send(
                pack.at[:, block], halo_rows.at[:, block], row_send.at[j], row_recv.at[j], device
            ).wait_recv()
            send(p_in.at[j], p_in.at[j], place_send.at[j], place_recv.at[j], device).wait_recv()

    low_half = lane < cap
    for j in range(0, 2 * HOPS, 2):
        p_halo[:, j * cap : (j + 2) * cap] = jnp.where(low_half, p_in[j], p_in[j + 1])
    for exists, copy in row_copies + place_copies:

        @pl.when(exists)
        def _():
            copy.wait_send()

    wait_sent(first + second + third)
    sums.done()


def gather_all(atoms, cap, groups, length, edges):
    shape = jax.ShapeDtypeStruct
    halo = 2 * HOPS * cap
    wide = window_rows(length)
    in_vmem = pl.BlockSpec(memory_space=pltpu.VMEM)
    in_smem = pl.BlockSpec(memory_space=pltpu.SMEM)
    return pl.pallas_call(
        functools.partial(gather_kernel, length=length),
        out_shape=(
            shape((PARAM_PAD, F), F32),
            shape((4, halo, F), F32),
            shape((8, halo), F32),
            shape((1, atoms), F32),
            shape((8, F), F32),
            shape((edges // F, F), jnp.int32),
        ),
        in_specs=[in_smem, in_vmem] + [pl.BlockSpec(memory_space=pl.ANY)] * 2 + [in_vmem] * 5,
        out_specs=(in_vmem, pl.BlockSpec(memory_space=pl.ANY)) + (in_vmem,) * 4,
        scratch_shapes=[
            pltpu.VMEM((atoms, F), F32),
            pltpu.VMEM((3, atoms, F), F32),
            pltpu.SemaphoreType.DMA((2,)),
            pltpu.VMEM((groups, 4, 2, wide, F), F32),
            pltpu.VMEM((4, halo, F), F32),
            pltpu.VMEM((atoms, F), F32),
            pltpu.VMEM((halo, F), F32),
            pltpu.VMEM((3 * HOPS, 8, F), F32),
            pltpu.VMEM((4, cap, F), F32),
            pltpu.SemaphoreType.DMA((groups + 8,)),
            pltpu.SemaphoreType.DMA((groups + 8,)),
            pltpu.SemaphoreType.DMA((2 * HOPS,)),
            pltpu.SemaphoreType.DMA((2 * HOPS,)),
            pltpu.SemaphoreType.DMA((2 * HOPS,)),
            pltpu.SemaphoreType.DMA((2 * HOPS,)),
            pltpu.SemaphoreType.DMA((2 * HOPS,)),
        ]
        + small_scratch(groups, 8),
        compiler_params=pltpu.CompilerParams(
            collective_id=0, has_side_effects=True, vmem_limit_bytes=62 * 1024 * 1024
        ),
        name="gather_inputs",
    )


def reduce_kernel(
    gpar_h,
    g_halo,
    gp_halo,
    par,
    one,
    two,
    back,
    p_back,
    shares,
    norms,
    gpar,
    gpar_sem,
    slots,
    pair_in,
    line_in,
    spot_in,
    turn,
    zeros,
    p_in,
    rs_send,
    rs_recv,
    row_send,
    row_recv,
    place_send,
    place_recv,
    zero_sem,
    *small,
    length,
):
    here = Place()
    cap = back.shape[1] // (2 * HOPS)
    wide = slots.shape[3]
    load = pltpu.make_async_copy(gpar_h, gpar, gpar_sem)
    load.start()
    expected = here.greet()
    load.wait()
    sums = SmallSum(here, *small)

    for p in range(here.count):
        row = p * length // F
        chip, core = p // here.cores, p % here.cores
        take = min(wide, PARAM_PAD - row)
        slots[chip // 4, chip % 4, core, 0:take, :] = gpar[row : row + take, :]
    old, m_one, m_two = [from_flat(ref, wide) for ref in (par, one, two)]
    zeros[...] = jnp.zeros_like(zeros)
    order = here.other_quarters() + [here.quarter]
    base = here.groups
    pl.semaphore_wait(pltpu.get_barrier_semaphore(), expected)
    third = start_all(
        [
            send(
                slots.at[:, q, here.mate],
                pair_in.at[:, q],
                rs_send.at[base + 4 + k],
                rs_recv.at[base + 4 + q],
                here.beside(),
            )
            for k, q in enumerate(order)
        ]
    )

    second = []
    for k, q in enumerate(order):
        line = pair_in.at[:, q]
        send(line, line, rs_send.at[0], rs_recv.at[base + 4 + q], here.beside()).wait_recv()
        slots[:, q, here.core] += pair_in[:, q]
        if k < 3:
            copy = send(
                slots.at[:, q, here.core],
                line_in.at[here.quarter],
                rs_send.at[base + k],
                rs_recv.at[base + here.quarter],
                here.in_quarter(q),
            )
            copy.start()
            second.append(copy)

    hops = range(2 * HOPS)
    copies = []

    def give_back(some):
        for j in some:
            exists, device = here.hop(-hop_offset(j))
            block = pl.ds(j * cap, cap)
            tile = pl.ds((j // 2) * F, F)
            rows_copy = send(
                g_halo.at[:, block], back.at[:, block], row_send.at[j], row_recv.at[j], device
            )
            place_copy = send(
                gp_halo.at[:, tile], p_in.at[j], place_send.at[j], place_recv.at[j], device
            )
            copies.extend([(exists, rows_copy), (exists, place_copy)])

            @pl.when(exists)
            def _():
                rows_copy.start()
                place_copy.start()

    give_back(BATCHES[0])
    for j in hops:
        known, device = here.hop(hop_offset(j))

        @pl.when(jnp.logical_not(known))
        def _():
            p_in[j] = jnp.zeros((8, F), F32)
            fill = pltpu.make_async_copy(zeros, back.at[:, pl.ds(j * cap, cap)], zero_sem.at[j])
            fill.start()
            fill.wait()

    for q in here.other_quarters():
        line = line_in.at[q]
        send(line, line, rs_send.at[0], rs_recv.at[base + q], here.beside()).wait_recv()
        slots[:, here.quarter, here.core] += line_in[q]
    first = start_all(
        [
            send(
                slots.at[g, here.quarter, here.core],
                spot_in.at[here.group],
                rs_send.at[k],
                rs_recv.at[here.group],
                here.in_group(g),
            )
            for k, g in enumerate(here.other_groups())
        ]
    )
    give_back(BATCHES[1])
    total = slots[here.group, here.quarter, here.core]
    for g in here.other_groups():
        spot = spot_in.at[g]
        send(spot, spot, rs_send.at[0], rs_recv.at[g], here.beside()).wait_recv()
        total = total + spot_in[g]

    offset = lax.rem(here.joint * length, F)
    lane = lax.broadcasted_iota(jnp.int32, (1, F), 1)
    turn[0:wide, :] = pltpu.roll(total, lax.rem(F - offset, F), 1)
    turn[wide : wide + 8, :] = jnp.zeros((8, F), F32)
    place = lax.broadcasted_iota(jnp.int32, (wide, F), 0) * F + lane
    inside = place < length
    g = jnp.where(lane + offset < F, turn[0:wide, :], turn[1 : wide + 1, :])
    g = jnp.where(inside, g, 0.0)
    shares[0] = g
    m_one = BETA_ONE * m_one + (1.0 - BETA_ONE) * g
    m_two = BETA_TWO * m_two + (1.0 - BETA_TWO) * g * g
    shares[1] = m_one
    shares[2] = m_two
    direction = (
        m_one
        / (1.0 - BETA_ONE**STEP)
        / (jnp.sqrt(m_two / (1.0 - BETA_TWO**STEP)) + EPSILON)
        + DECAY * old
    )
    spot = place + here.joint * length
    label = jnp.zeros((wide, F), jnp.int32)
    for end in GROUP_ENDS:
        label = label + jnp.where(spot >= end * F, 1, 0)
    label = jnp.where(inside, label, GROUPS)
    lines = []
    for value in (old, direction):
        square = value * value
        lines += [
            jnp.sum(jnp.where(label == k, square, 0.0), axis=0, keepdims=True)
            for k in range(GROUPS)
        ]
        lines.append(jnp.zeros((1, F), F32))
    sums.start(0, jnp.concatenate(lines, axis=0))
    give_back(BATCHES[2])
    sums.start(1, sums.finish(0))
    give_back(BATCHES[3])
    whole = jnp.sqrt(jnp.sum(sums.finish(1), axis=1, keepdims=True))
    ratio = whole[0:8] / whole[8:16]
    norms[...] = jnp.broadcast_to(whole, (16, F))
    trust = jnp.zeros((wide, F), F32)
    for k in range(GROUPS):
        trust = jnp.where(label == k, ratio[k : k + 1], trust)
    shares[3] = old - RATE * trust * direction

    for j in hops:
        known, device = here.hop(hop_offset(j))

        @pl.when(known)
        def _():
            block = pl.ds(j * cap, cap)
            tile = p_in.at[j]
            send(
                back.at[:, block], back.at[:, block], row_send.at[j], row_recv.at[j], device
            ).wait_recv()
            send(tile, tile, place_send.at[j], place_recv.at[j], device).wait_recv()

    low_half = lane < cap
    for j in range(0, 2 * HOPS, 2):
        p_back[:, j * cap : (j + 2) * cap] = jnp.where(low_half, p_in[j], p_in[j + 1])
    for exists, copy in copies:

        @pl.when(exists)
        def _():
            copy.wait_send()

    wait_sent(first + second + third)
    sums.done()


def reduce_all(cap, groups, length):
    shape = jax.ShapeDtypeStruct
    halo = 2 * HOPS * cap
    wide = window_rows(length)
    in_vmem = pl.BlockSpec(memory_space=pltpu.VMEM)
    in_any = pl.BlockSpec(memory_space=pl.ANY)
    return pl.pallas_call(
        functools.partial(reduce_kernel, length=length),
        out_shape=(
            shape((4, halo, F), F32),
            shape((8, halo), F32),
            shape((4, wide, F), F32),
            shape((16, F), F32),
        ),
        in_specs=[in_any] * 2 + [in_vmem] * 4,
        out_specs=(in_any, in_vmem, in_vmem, in_vmem),
        scratch_shapes=[
            pltpu.VMEM((PARAM_PAD, F), F32),
            pltpu.SemaphoreType.DMA(()),
            pltpu.VMEM((groups, 4, 2, wide, F), F32),
            pltpu.VMEM((groups, 4, wide, F), F32),
            pltpu.VMEM((4, groups, wide, F), F32),
            pltpu.VMEM((groups, wide, F), F32),
            pltpu.VMEM((wide + 8, F), F32),
            pltpu.VMEM((4, cap, F), F32),
            pltpu.VMEM((2 * HOPS, 8, F), F32),
            pltpu.SemaphoreType.DMA((groups + 8,)),
            pltpu.SemaphoreType.DMA((groups + 8,)),
            pltpu.SemaphoreType.DMA((2 * HOPS,)),
            pltpu.SemaphoreType.DMA((2 * HOPS,)),
            pltpu.SemaphoreType.DMA((2 * HOPS,)),
            pltpu.SemaphoreType.DMA((2 * HOPS,)),
            pltpu.SemaphoreType.DMA((2 * HOPS,)),
        ]
        + small_scratch(groups, 16),
        compiler_params=pltpu.CompilerParams(
            collective_id=1, has_side_effects=True, vmem_limit_bytes=62 * 1024 * 1024
        ),
        name="reduce_outputs",
    )


def finish_kernel(
    back,
    p_back,
    shares,
    norms,
    stats,
    send_rows,
    gs_own,
    gv_own,
    gp_own,
    grad_s,
    grad_v,
    grad_p,
    elem_mean,
    scale,
    grad,
    one_new,
    two_new,
    par_new,
    par_low,
    weight_norms,
    update_norms,
):
    atoms = gs_own.shape[0]
    halo = back.shape[1]
    pick = jnp.concatenate([send_rows[0, j : j + 1, :] for j in range(2 * HOPS)], axis=1)
    hot = jnp.where(pick == lax.broadcasted_iota(jnp.int32, (atoms, halo), 0), 1.0, 0.0)
    hot = hot.astype(BF16)
    high, low = split(jnp.concatenate([back[k] for k in range(4)], axis=1))
    extra = mm(hot, high) + mm(hot, low)
    grad_s[...] = gs_own[...] + extra[:, :F]
    for c in range(3):
        grad_v[c] = gv_own[c] + extra[:, (c + 1) * F : (c + 2) * F]
    place = p_back[...]
    high = place.astype(BF16).astype(F32)
    middle = (place - high).astype(BF16).astype(F32)
    pieces = jnp.concatenate([high, middle, place - high - middle, jnp.zeros_like(place)], axis=0)
    got = mm(pieces.astype(BF16), hot, (1, 1))
    grad_p[...] = (gp_own[...] + (got[0:8] + got[8:16] + got[16:24]))[0:3]
    for k, ref in enumerate((grad, one_new, two_new, par_new)):
        to_flat(ref, shares[k])
    to_flat(par_low, shares[3].astype(BF16))
    rows = lax.broadcasted_iota(jnp.int32, (8, F), 0)
    lanes = lax.broadcasted_iota(jnp.int32, (8, F), 1)
    for k, ref in enumerate((weight_norms, update_norms)):
        line = jnp.sum(
            jnp.where(rows == lanes, norms[8 * k : 8 * k + 8, :], 0.0), axis=0, keepdims=True
        )
        ref[...] = line[0, :GROUPS]
    elem_mean[...] = stats[0, :ELEMS]
    scale[...] = stats[1, :1]


def finish(atoms, length):
    shape = jax.ShapeDtypeStruct
    in_vmem = pl.BlockSpec(memory_space=pltpu.VMEM)
    outs = (
        [shape((atoms, F), F32), shape((3, atoms, F), F32), shape((3, atoms), F32)]
        + [shape((ELEMS,), F32), shape((1,), F32)]
        + [shape((length,), F32)] * 4
        + [shape((length,), BF16), shape((GROUPS,), F32), shape((GROUPS,), F32)]
    )
    return pl.pallas_call(
        finish_kernel,
        out_shape=tuple(outs),
        in_specs=[in_vmem] * 9,
        out_specs=(in_vmem,) * len(outs),
        compiler_params=pltpu.CompilerParams(vmem_limit_bytes=62 * 1024 * 1024),
        name="finish",
    )


def body(
    scalars_in,
    vectors_in,
    positions,
    cotan_scalar,
    cotan_vector,
    target_energy,
    forces,
    elements,
    crystal,
    lattice,
    edge_src,
    edge_dst,
    edge_shift,
    edge_count,
    send_rows,
    params,
    first_moment,
    second_moment,
):
    atoms = scalars_in.shape[0]
    edges = edge_src.shape[0]
    cap = send_rows.shape[2]
    halo = 2 * HOPS * cap
    groups = lax.axis_size("atoms") // 4
    length = params.shape[0]
    par, halo_rows, p_halo, goal, stats, src_tiles = gather_all(atoms, cap, groups, length, edges)(
        send_rows,
        params,
        scalars_in,
        vectors_in,
        positions,
        target_energy.reshape(-1, F),
        elements.reshape(-1, F),
        forces,
        edge_src.reshape(-1, F),
    )
    s_two, v_two, gs_own, gv_own, g_halo, gp_own, gp_halo, gpar = layer(atoms, halo, edges)(
        edge_dst,
        edge_count,
        src_tiles.reshape(-1),
        crystal.reshape(-1, F),
        edge_dst.reshape(-1, F),
        edge_shift,
        jnp.transpose(lattice),
        par,
        scalars_in,
        vectors_in,
        positions,
        halo_rows,
        p_halo,
        cotan_scalar,
        cotan_vector,
        goal,
    )
    back, p_back, shares, norms = reduce_all(cap, groups, length)(
        gpar, g_halo, gp_halo, params, first_moment, second_moment
    )
    (
        grad_s,
        grad_v,
        grad_p,
        elem_mean,
        scale,
        grad,
        one_new,
        two_new,
        par_new,
        par_low,
        weight_norms,
        update_norms,
    ) = finish(atoms, length)(
        back, p_back, shares, norms, stats, send_rows, gs_own, gv_own, gp_own
    )
    return (
        s_two,
        v_two,
        grad_s,
        grad_v,
        grad_p,
        elem_mean,
        scale.reshape(()),
        grad,
        one_new,
        two_new,
        par_new,
        par_low,
        weight_norms,
        update_norms,
    )


def solution(mesh):
    joint = ("atoms", "rep")
    in_specs = (
        P(joint, None),
        P(None, joint, None),
        P(None, joint),
        P(joint, None),
        P(None, joint, None),
        P(joint),
        P(None, joint),
        P(joint),
        P(joint),
        P(),
        P(joint),
        P(joint),
        P(None, joint),
        P(joint),
        P(joint, None, None),
        P(joint),
        P(joint),
        P(joint),
    )
    out_specs = (
        P(joint, None),
        P(None, joint, None),
        P(joint, None),
        P(None, joint, None),
        P(None, joint),
        P(),
        P(),
        P(joint),
        P(joint),
        P(joint),
        P(joint),
        P(joint),
        P(),
        P(),
    )
    return jax.shard_map(body, mesh=mesh, in_specs=in_specs, out_specs=out_specs, check_vma=False)
```
